256 devices in a mesh: region: 4 (over x), level: 32 (over z, y), member: 2 (over core).
Axes of the slice: x: 4, y: 4, z: 8, core: 2. Of those that a mesh axis runs over, the one named last changes fastest.
Arguments:
- state: float32 [3, 64, 80, 8192], P(None, 'level', 'member', 'region'), may hold values from -6 to 6
- ray_cols: int32 [2, 128, 64], replicated, may hold values from 0 to 8191, as said below
- ray_len: int32 [2, 128], replicated, may hold values from 16 to 64, as said below
- ray_weight: float32 [2, 128, 3, 64], replicated, may hold values from -0.4375 to 0.4375
- owner: int32 [2, 128], replicated, may hold values from 0 to 3, as said below
- loc_regions: int32 [2, 128, 2], replicated, may hold values from 0 to 3, as said below
- loc_weight: float32 [2, 128, 2], replicated, may hold values from 0.3 to 0.9
- obs_value: float32 [2, 128, 64], replicated, may hold values from -12 to 12
- obs_var: float32 [2, 128, 64], replicated, may hold values from 4 to 40
Outputs:
- analysis: float32 [3, 64, 80, 8192], P(None, 'level', 'member', 'region')
The draws below stay inside these ranges and needn't reach their ends.
Inputs may be any that keep to these rules, and one draw needn't show every extreme that they name: `ray_cols`: all ray points of one occultation lie in consecutive columns of a single region. In each step, for every region and every owner, exactly 8 occultations of that owner have their rays in that region. `ray_len`: so at most 512 live ray points of one owner's occultations lie in one region in a step; in every step some owner's occultations all have 64 live points, so that owner has exactly 512 in every region. `owner`: each region owns exactly 32 occultations in each step. `loc_regions`: the 2 listed regions of a profile are distinct and never its owner.
All inputs are finite; a program needn't handle non-finite values.
Results may differ from the reference program's by a relative error of at most 0.00018.
Values sent between devices are 32-bit elements; how exact they have to be, the bound alone decides.
No kernel may reach another device: no remote copies, remote signals or barrier semaphores. Data moves between devices by JAX's collectives and lax.ppermute only.
A program may use at most 64 MiB of HBM per device.

```python
import math
import jax
import jax.numpy as jnp
from jax import lax

COL_DEV = 2048
OCC_DEV = 32
MEMBERS = 80
NVAR = 3
RAYS = 64
NLOC = 2
STEPS = 2
LEVELS = 64
NOCC = 128
COLS = 8192
N_REGION = 4


def layout(key):
    base_key = jax.random.fold_in(key, 7)

    def one_step(step_key):
        key_perm, key_rot, key_busy, key_len, key_start, key_off = jax.random.split(step_key, 6)
        shuffle = jax.random.permutation(key_perm, NOCC).astype(jnp.int32)
        owners = shuffle // OCC_DEV
        owner_slot = shuffle % OCC_DEV
        rotation = jax.random.randint(key_rot, (N_REGION,), 0, N_REGION).astype(jnp.int32)
        home_region = (owner_slot + rotation[owners]) % N_REGION
        busy_region = jax.random.randint(key_busy, (), 0, N_REGION).astype(jnp.int32)
        lengths = jax.random.randint(key_len, (NOCC,), RAYS // 4, RAYS + 1).astype(jnp.int32)
        lengths = jnp.where(owners == busy_region, RAYS, lengths).astype(jnp.int32)
        first_col = jax.random.randint(key_start, (NOCC,), 0, COL_DEV - RAYS + 1).astype(jnp.int32)
        columns = home_region[:, None] * COL_DEV + first_col[:, None] + jnp.arange(RAYS, dtype=jnp.int32)[None, :]
        offset = jax.random.randint(key_off, (NOCC,), 1, N_REGION - NLOC + 1).astype(jnp.int32)
        region_list = (owners[:, None] + offset[:, None] + jnp.arange(NLOC, dtype=jnp.int32)[None, :]) % N_REGION
        return (columns.astype(jnp.int32), lengths, owners.astype(jnp.int32), region_list.astype(jnp.int32))
    return jax.vmap(one_step)(jax.random.split(base_key, STEPS))


def draw_ray_cols(key, part):
    return layout(key)[0]


def draw_ray_len(key, part):
    return layout(key)[1]


def draw_owner(key, part):
    return layout(key)[2]


def draw_loc_regions(key, part):
    return layout(key)[3]


def block_scale(rng, shape, cuts, smallest, largest):
    def one(position, shards_of):
        draws = jax.random.uniform(jax.random.fold_in(jax.random.fold_in(rng, 6), position), (shards_of,), jnp.float32, smallest / len(cuts), largest / len(cuts))
        return jnp.repeat(jnp.exp(draws), shape[position] // shards_of).reshape((-1,) + (1,) * (len(shape) - position - 1))

    factor_of = one(*cuts[0])
    for cut in cuts[1:]:
        factor_of = factor_of * one(*cut)
    return factor_of


def centred(key, shape, scale, most, cuts=(), held_as=jnp.bfloat16):
    result = scale * jax.random.normal(key, shape, jnp.float32)
    if cuts:
        result = result * block_scale(key, shape, cuts, -0.22, 0.18)
    return jnp.clip(result, -most, most).astype(held_as)


def setup_inputs(seed: int = 0) -> dict:
    seeds = jax.random.split(jax.random.key(seed), 10)
    return {
        "state": centred(seeds[0], (NVAR, LEVELS, MEMBERS, COLS), 1.0, 6.0, ((1, 32), (2, 2), (3, 4)), jnp.float32),
        "ray_cols": draw_ray_cols(jax.random.fold_in(seeds[9], 71), 0),
        "ray_len": draw_ray_len(jax.random.fold_in(seeds[9], 71), 0),
        "ray_weight": centred(seeds[3], (STEPS, NOCC, NVAR, RAYS), (NVAR * RAYS) ** -0.5, 0.4375, (), jnp.float32),
        "owner": draw_owner(jax.random.fold_in(seeds[9], 71), 0),
        "loc_regions": draw_loc_regions(jax.random.fold_in(seeds[9], 71), 0),
        "loc_weight": jnp.clip(jax.random.uniform(seeds[6], (STEPS, NOCC, NLOC), jnp.float32, 0.3, 0.9), 0.3, 0.9),
        "obs_value": centred(seeds[7], (STEPS, NOCC, LEVELS), 3.0, 12.0, (), jnp.float32),
        "obs_var": jnp.clip(jnp.exp(jax.random.uniform(seeds[8], (STEPS, NOCC, LEVELS), jnp.float32, math.log(4.0), math.log(40.0))), 4.0, 40.0),
    }


def vertical_table(levels):
    level_axis = jnp.arange(levels, dtype=jnp.float32)
    scaled = (level_axis[:, None] - level_axis[None, :]) / (levels / 4.0)
    return jnp.exp(-jnp.abs(scaled))

def reference(state, ray_cols, ray_len, ray_weight, owner, loc_regions, loc_weight, obs_value, obs_var):
    highest = lax.Precision.HIGHEST
    vertical = vertical_table(LEVELS)
    region_ids = jnp.arange(N_REGION, dtype=jnp.int32)
    current = state
    for step_index in range(STEPS):
        live_mask = (jnp.arange(RAYS, dtype=jnp.int32)[None, :] < ray_len[step_index][:, None]).astype(jnp.float32)
        masked_weight = ray_weight[step_index] * live_mask[:, None, :]

        def predict_one(pair_args, current=current):
            column_list, weight_list = pair_args
            gathered = jnp.take(current, column_list, axis=3)
            return jnp.einsum('vlmr,vr->lm', gathered, weight_list, precision=highest)
        predicted = lax.map(predict_one, (ray_cols[step_index], masked_weight))
        ens_mean = lax.optimization_barrier(jnp.mean(predicted, axis=2))
        spread = predicted - ens_mean[:, :, None]
        variance = lax.optimization_barrier(jnp.sum(spread * spread, axis=2)) / (MEMBERS - 1.0)
        total_var = variance + obs_var[step_index]
        kalman_gain = (obs_value[step_index] - ens_mean) / total_var
        shrink = 1.0 / (1.0 + jnp.sqrt(obs_var[step_index] / total_var))
        listed = (loc_regions[step_index][:, :, None] == region_ids[None, None, :]).astype(jnp.float32)
        horiz_loc = (owner[step_index][:, None] == region_ids[None, :]).astype(jnp.float32)
        horiz_loc = horiz_loc + lax.optimization_barrier(jnp.sum(loc_weight[step_index][:, :, None] * listed, axis=1))
        col_blocks = current.reshape(NVAR, LEVELS, MEMBERS, N_REGION, COL_DEV)

        def update_region(region_id, col_blocks=col_blocks, horiz_loc=horiz_loc, spread=spread, kalman_gain=kalman_gain, shrink=shrink, total_var=total_var):
            region_loc = lax.dynamic_index_in_dim(horiz_loc, region_id, 1, keepdims=False)
            mean_coef = region_loc[:, None, None] * vertical[None] * kalman_gain[:, :, None]
            spread_coef = region_loc[:, None, None] * vertical[None] * (shrink / total_var)[:, :, None]
            mean_weights = jnp.einsum('olk,oln->kn', mean_coef, spread, precision=highest)
            weighted = spread_coef[:, :, :, None] * spread[:, :, None, :]
            spread_matrix = jnp.einsum('olkm,oln->kmn', weighted, spread, precision=highest)
            mixing = (mean_weights[:, None, :] - spread_matrix) / (MEMBERS - 1.0)
            block = lax.dynamic_index_in_dim(col_blocks, region_id, 3, keepdims=False)
            return block + jnp.einsum('kmn,vknc->vkmc', mixing, block, precision=highest)
        updated = lax.map(update_region, region_ids)
        current = jnp.moveaxis(updated, 0, 3).reshape(NVAR, LEVELS, MEMBERS, N_REGION * COL_DEV)
    return current
```

```python
import math

import jax
import jax.numpy as jnp
from jax import lax
from jax.experimental import pallas as pl
from jax.experimental.pallas import tpu as pltpu
from jax.sharding import PartitionSpec as P

STEPS = 2
LANES = 128
SUB = 8
HIGHEST = lax.Precision.HIGHEST
F32 = jnp.float32
VMEM = pltpu.VMEM


def iota(shape, dim):
    return lax.broadcasted_iota(jnp.int32, shape, dim)


def dot(a, b):
    return jnp.dot(a, b, precision=HIGHEST, preferred_element_type=F32)


def predict_kernel(nl, nm, nc, regions, slots, rays,
                   state_ref, cols_ref, len_ref, weight_ref, owner_ref, locr_ref, locw_ref, obs_ref, var_ref,
                   msg_ref, later_ref, meta_ref,
                   held, picked, meta_in, tile_v, tile_s, state_sem, tile_sem):
    nv = state_ref.shape[0]
    region = lax.axis_index("region")
    level = lax.axis_index("level")
    copies = [pltpu.make_async_copy(state_ref.at[v], held.at[v], state_sem.at[v]) for v in range(nv)]
    for copy in copies:
        copy.start()
    lane_i = iota((LANES, LANES), 1)
    lane = lane_i.astype(F32)
    sub = iota((LANES, LANES), 0).astype(F32)

    def to_column(row):
        return jnp.sum(jnp.where(sub == lane, row, 0.0), axis=1, keepdims=True)

    region_f = region.astype(F32)
    total = None
    meta_in[...] = jnp.zeros_like(meta_in)
    for step in range(STEPS):
        cols = cols_ref[step].astype(F32)
        first = jnp.min(cols, axis=0, keepdims=True)
        home = jnp.zeros_like(first)
        for q in range(1, regions):
            home = home + (first >= float(q * nc)).astype(F32)
        same = (to_column(home) == home) & (sub < lane)
        rank = jnp.sum(same.astype(F32), axis=0, keepdims=True)
        place = to_column(home * float(slots) + rank)
        order = (place == lane).astype(F32)
        shifted = lane + (region_f - float(step)) * float(slots)
        mine = (place == shifted) & (lane_i >= step * slots) & (lane_i < (step + 1) * slots)
        live = sub[:rays] < len_ref[step:step + 1].astype(F32)
        data = [cols] + [jnp.where(live, weight_ref[step, v], 0.0) for v in range(nv)]
        term = dot(jnp.concatenate(data, axis=0), mine.astype(F32))
        total = term if total is None else total + term
        horiz = (owner_ref[step:step + 1] == region).astype(F32)
        listed = (locr_ref[step] == region).astype(F32)
        horiz = horiz + jnp.sum(locw_ref[step] * listed, axis=0, keepdims=True)
        for l in range(nl):
            meta_in[l:l + 1] = var_ref[step, pl.ds(level * nl + l, 1)]
            meta_in[nl + l:nl + l + 1] = obs_ref[step, pl.ds(level * nl + l, 1)]
        meta_in[2 * nl:2 * nl + 1] = horiz
        meta_ref[step] = dot(meta_in[...], order)
    picked[...] = total
    low = jnp.min(total[:rays], axis=0, keepdims=True) - region_f * float(nc)
    tile_v[...] = jnp.clip(low.astype(jnp.int32) // LANES, 0, nc // LANES - 2)
    scalars = pltpu.make_async_copy(tile_v, tile_s, tile_sem)
    scalars.start()
    scalars.wait()
    for copy in copies:
        copy.wait()
    groups = nl * nm // SUB
    packed = -(-groups // regions)
    lane8 = iota((SUB, LANES), 1)
    lane_r = lane[:rays]
    for step in range(STEPS):
        def eight(block, parts, step=step):
            first_slot = step * slots + block * SUB
            turned = pltpu.roll(picked[...], LANES - first_slot, 1)
            parts = list(parts)
            for u in range(SUB):
                tile = tile_s[0, first_slot + u]
                start = pl.multiple_of(tile * LANES, LANES)
                origin = region * nc + start
                place = turned[:rays, u:u + 1] - origin.astype(F32)
                sums = [None] * nl
                for half in range(2):
                    hit = place == lane_r + float(half * LANES)
                    for v in range(nv):
                        weights = turned[(v + 1) * rays:(v + 2) * rays, u:u + 1]
                        row = jnp.sum(jnp.where(hit, weights, 0.0), axis=0, keepdims=True)
                        for l in range(nl):
                            term = held[v, l, :, pl.ds(start + half * LANES, LANES)] * row
                            sums[l] = term if sums[l] is None else sums[l] + term
                for l in range(nl):
                    result = jnp.sum(sums[l], axis=1, keepdims=True)
                    for r in range(nm // SUB):
                        g = l * (nm // SUB) + r
                        spot = slots * (g % regions) + block * SUB + u
                        parts[g // regions] = jnp.where(lane8 == spot, result[r * SUB:(r + 1) * SUB], parts[g // regions])
            return tuple(parts)
        parts = lax.fori_loop(0, slots // SUB, eight, (jnp.zeros((SUB, LANES), F32),) * packed)
        for j in range(packed):
            if step == 0:
                for d in range(msg_ref.shape[0]):
                    msg_ref[d, j * SUB:(j + 1) * SUB] = parts[j]
            else:
                later_ref[j * SUB:(j + 1) * SUB] = parts[j]


def turn(x, by):
    by = by % LANES
    return pltpu.roll(x, by, 1) if by else x


def pack_mixing(a):
    members = 2 * a.shape[0]
    free = LANES - members
    lane8 = iota((SUB, LANES), 1)
    kept = a.shape[0] - SUB
    last = a[kept:]
    pieces = []
    for j in range(kept // SUB):
        part = a[j * SUB:(j + 1) * SUB]
        low, high = j * free, min((j + 1) * free, members)
        if low < high:
            part = part + turn(jnp.where((lane8 >= low) & (lane8 < high), last, 0.0), members - low)
        pieces.append(part)
    return jnp.concatenate(pieces, axis=0)


def unpack_mixing(p):
    rows = p.shape[0] + SUB
    members = 2 * rows
    free = LANES - members
    lane8 = iota((SUB, LANES), 1)
    last = jnp.zeros((SUB, LANES), F32)
    pieces = []
    for j in range(p.shape[0] // SUB):
        part = p[j * SUB:(j + 1) * SUB]
        low, high = j * free, min((j + 1) * free, members)
        if low < high:
            last = last + jnp.where((lane8 >= low) & (lane8 < high), turn(part, low - members), 0.0)
        pieces.append(jnp.where(lane8 < members, part, 0.0))
    return jnp.concatenate(pieces + [last], axis=0)


def local_kernel(step, nl, nm, regions, slots, levels, level_count, cores,
                 got_ref, meta_ref, msg_ref, local_ref, spread_ref):
    level = lax.axis_index("level")
    member = lax.axis_index("member")
    members = nm * cores
    scale = levels / 4.0
    lane8 = iota((SUB, LANES), 1)
    spread_ref[...] = jnp.zeros_like(spread_ref)
    mats = []
    for l in range(nl):
        rows = []
        for c in range(cores):
            for r in range(nm // SUB):
                g = l * (nm // SUB) + r
                j, k = g // regions, g % regions
                row = None
                for p in range(regions):
                    part = turn(got_ref[p * cores + c, j * SUB:(j + 1) * SUB], slots * (p - k))
                    row = part if row is None else jnp.where(lane8 >= slots * p, part, row)
                rows.append(row)
        predicted = jnp.concatenate(rows, axis=0)
        mean = jnp.sum(predicted, axis=0, keepdims=True) * (1.0 / members)
        spread = predicted - mean
        variance = jnp.sum(spread * spread, axis=0, keepdims=True) * (1.0 / (members - 1.0))
        obs_var = meta_ref[step, l:l + 1]
        obs_value = meta_ref[step, nl + l:nl + l + 1]
        horiz = meta_ref[step, 2 * nl:2 * nl + 1]
        total_var = variance + obs_var
        gain = (obs_value - mean) / total_var
        shrink = 1.0 / (1.0 + jnp.sqrt(obs_var / total_var))
        scaled = horiz * (1.0 / (members - 1.0))
        mean_coef = scaled * gain
        spread_coef = scaled * (shrink / total_var)
        spread_ref[l, 0:members] = spread
        own = spread_ref[l, pl.ds(pl.multiple_of(member * nm, SUB), nm)]
        left = mean_coef - spread_coef * own
        mats.append(lax.dot_general(left, spread_ref[l], (((1,), (1,)), ((), ())), precision=HIGHEST, preferred_element_type=F32))
    up = sum(math.exp(-(nl - 1 - l) / scale) * mats[l] for l in range(nl))
    down = sum(math.exp(-l / scale) * mats[l] for l in range(nl))
    up, down = pack_mixing(up), pack_mixing(down)
    for l in range(nl):
        local_ref[l] = pack_mixing(sum(math.exp(-abs(l - k) / scale) * mats[k] for k in range(nl)))
    for d in range(level_count):
        msg_ref[d] = jnp.where(d > level, up, down)


def combine_levels(nl, levels, level_count, got_ref, local_ref):
    level = lax.axis_index("level")
    scale = levels / 4.0
    fade = math.exp(-nl / scale)
    zero = jnp.zeros(got_ref.shape[1:], F32)
    below = lax.fori_loop(0, level, lambda d, acc: acc * fade + got_ref[d], zero)
    above = lax.fori_loop(0, level_count - 1 - level, lambda d, acc: acc * fade + got_ref[level_count - 1 - d], zero)
    return [
        unpack_mixing(math.exp(-(l + 1) / scale) * below + math.exp(-(nl - l) / scale) * above + local_ref[l])
        for l in range(nl)
    ]


def forecast_kernel(nl, nm, regions, slots, levels, level_count,
                    got_ref, local_ref, own_ref, other_ref, mix_ref, msg_ref, full_ref):
    member = lax.axis_index("member")
    lane8 = iota((SUB, LANES), 1)
    full_ref[...] = jnp.zeros_like(full_ref)
    groups = nl * nm // SUB
    packed = -(-groups // regions)
    parts = [jnp.zeros((SUB, LANES), F32) for _ in range(packed)]
    mats = combine_levels(nl, levels, level_count, got_ref, local_ref)
    for l in range(nl):
        mix_ref[l] = mats[l]
        rows = {}
        for name, ref, at in (("own", own_ref, member), ("other", other_ref, 1 - member)):
            pieces = []
            for r in range(nm // SUB):
                g = l * (nm // SUB) + r
                j, k = g // regions, g % regions
                pieces.append(turn(ref[j * SUB:(j + 1) * SUB], -slots * k))
            rows[name] = jnp.concatenate(pieces, axis=0)
            full_ref[l, pl.ds(pl.multiple_of(at * nm, SUB), nm)] = rows[name]
        result = rows["own"] + dot(mats[l], full_ref[l])
        for r in range(nm // SUB):
            g = l * (nm // SUB) + r
            j, k = g // regions, g % regions
            keep = (lane8 >= slots * k) & (lane8 < slots * (k + 1))
            parts[j] = jnp.where(keep, turn(result[r * SUB:(r + 1) * SUB], slots * k), parts[j])
    for d in range(msg_ref.shape[0]):
        for j in range(packed):
            msg_ref[d, j * SUB:(j + 1) * SUB] = parts[j]


def split(x):
    high = x.astype(jnp.bfloat16).astype(F32)
    return high, x - high


def update_kernel(nl, nm, levels, level_count,
                  got_ref, local_ref, mine_ref, theirs_ref, state_ref, other_ref, out_ref, full_ref, left_ref):
    member = lax.axis_index("member")
    members = 2 * nm

    @pl.when((pl.program_id(0) == 0) & (pl.program_id(1) == 0))
    def _():
        lane = iota((nm, LANES), 1)
        full_ref[...] = jnp.zeros_like(full_ref)
        mats = combine_levels(nl, levels, level_count, got_ref, local_ref)
        for l in range(nl):
            full_ref[l, pl.ds(pl.multiple_of(member * nm, SUB), nm)] = mine_ref[l]
            full_ref[l, pl.ds(pl.multiple_of((1 - member) * nm, SUB), nm)] = theirs_ref[l]
            both = mats[l] + mine_ref[l] + dot(mats[l], full_ref[l])
            swapped = jnp.where(lane < nm, turn(both, -nm), jnp.where(lane < members, turn(both, nm), 0.0))
            both = jnp.where(member == 0, both, swapped)
            high, low = split(both)
            again = turn(high, members)
            left_ref[l, :, 0:LANES] = high + jnp.where(lane >= members, again, 0.0)
            left_ref[l, :, LANES:] = jnp.where(lane < 2 * members - LANES, again, 0.0) + turn(low, 2 * members - LANES)

    own = state_ref[0, 0]
    high, low = split(jnp.concatenate([own, other_ref[0, 0]], axis=0))
    pad = jnp.zeros((2 * LANES - 3 * members, own.shape[1]), F32)
    right = jnp.concatenate([high, low, high, pad], axis=0).astype(jnp.bfloat16)
    left = left_ref[pl.program_id(0)].astype(jnp.bfloat16)
    out_ref[0, 0] = own + jnp.dot(left, right, preferred_element_type=F32)


def body(state, ray_cols, ray_len, ray_weight, owner, loc_regions, loc_weight, obs_value, obs_var):
    regions = lax.axis_size("region")
    level_count = lax.axis_size("level")
    cores = lax.axis_size("member")
    nv, nl, nm, nc = state.shape
    occ, rays = ray_cols.shape[1:]
    slots = occ // regions
    levels = nl * level_count
    assert occ == LANES and regions * slots == LANES and nm % SUB == 0 and cores == 2
    groups = nl * nm // SUB
    block = (-(-groups // regions) * SUB, LANES)
    mixing = (nm - SUB, LANES)
    whole = pl.BlockSpec(memory_space=VMEM)
    swap = [(0, 1), (1, 0)]

    def call(kernel, statics, outs, scratch, *args, specs=None, name=None):
        def wrapped(*refs):
            return kernel(*statics, *refs)
        return pl.pallas_call(
            wrapped,
            out_shape=[jax.ShapeDtypeStruct(s, F32) for s in outs],
            in_specs=specs or [whole] * len(args),
            out_specs=[whole] * len(outs),
            scratch_shapes=scratch,
            compiler_params=pltpu.CompilerParams(vmem_limit_bytes=32 * 2**20),
            name=name,
        )(*args)

    other_state = lax.ppermute(state, "member", swap)
    msg, later, meta = call(
        predict_kernel, (nl, nm, nc, regions, slots, rays),
        [(regions * cores,) + block, block, (STEPS, SUB, LANES)],
        [VMEM(state.shape, F32), VMEM(((nv + 1) * rays, LANES), F32), VMEM((SUB, LANES), F32),
         VMEM((1, LANES), jnp.int32), pltpu.SMEM((1, LANES), jnp.int32),
         pltpu.SemaphoreType.DMA((nv,)), pltpu.SemaphoreType.DMA],
        state, ray_cols.swapaxes(1, 2), ray_len, ray_weight.transpose(0, 2, 3, 1), owner,
        loc_regions.swapaxes(1, 2), loc_weight.swapaxes(1, 2), obs_value.swapaxes(1, 2), obs_var.swapaxes(1, 2),
        specs=[pl.BlockSpec(memory_space=pl.ANY)] + [whole] * 8, name="predict",
    )
    other_later = lax.ppermute(later, "member", swap)

    def assimilate(step, msg):
        got = lax.all_to_all(msg, ("region", "member"), 0, 0, tiled=True)
        out, local = call(
            local_kernel, (step, nl, nm, regions, slots, levels, level_count, cores),
            [(level_count,) + mixing, (nl,) + mixing], [VMEM((nl, LANES, LANES), F32)],
            got, meta, name="local",
        )
        return lax.all_to_all(out, "level", 0, 0, tiled=True), local

    got, local = assimilate(0, msg)
    mine, msg = call(
        forecast_kernel, (nl, nm, regions, slots, levels, level_count),
        [(nl, nm, LANES), (regions * cores,) + block], [VMEM((nl, LANES, LANES), F32)],
        got, local, later, other_later, name="forecast",
    )
    theirs = lax.ppermute(mine, "member", swap)
    got, local = assimilate(1, msg)
    tile = pl.BlockSpec((1, 1, nm, nc), lambda l, v: (v, l, 0, 0))

    def update(*refs):
        return update_kernel(nl, nm, levels, level_count, *refs)

    return pl.pallas_call(
        update,
        grid=(nl, nv),
        out_shape=jax.ShapeDtypeStruct(state.shape, F32),
        in_specs=[whole] * 4 + [tile] * 2,
        out_specs=tile,
        scratch_shapes=[VMEM((nl, LANES, LANES), F32), VMEM((nl, nm, 2 * LANES), F32)],
        compiler_params=pltpu.CompilerParams(vmem_limit_bytes=32 * 2**20),
        name="update",
    )(got, local, mine, theirs, state, other_state)


def solution(mesh):
    in_specs = (P(None, "level", "member", "region"), P(), P(), P(), P(), P(), P(), P(), P())
    out_specs = P(None, "level", "member", "region")
    return jax.shard_map(body, mesh=mesh, in_specs=in_specs, out_specs=out_specs, check_vma=False)
```

```python
import math

import jax
import jax.numpy as jnp
from jax import lax
from jax.experimental import pallas as pl
from jax.experimental.pallas import tpu as pltpu
from jax.sharding import PartitionSpec as P

STEPS = 2
LANES = 128
SUB = 8
HIGHEST = lax.Precision.HIGHEST
F32 = jnp.float32
BF16 = jnp.bfloat16
VMEM = pltpu.VMEM
BY_LANES = (((1,), (1,)), ((), ()))


def iota(shape, dim):
    return lax.broadcasted_iota(jnp.int32, shape, dim)


def dot(a, b):
    return jnp.dot(a, b, precision=HIGHEST, preferred_element_type=F32)


def turn(x, by):
    by = by % LANES
    return pltpu.roll(x, by, 1) if by else x


def pick(chosen, values):
    chosen = chosen.astype(BF16)
    total = None
    for _ in range(3):
        part = values.astype(BF16)
        term = lax.dot_general(chosen, part, BY_LANES, preferred_element_type=F32)
        total = term if total is None else total + term
        values = values - part.astype(F32)
    return total


def predict_kernel(nl, nm, nc, regions, slots, rays,
                   state_hbm, cols_hbm, len_hbm, weight_hbm, owner_hbm, locr_hbm, locw_hbm, obs_hbm, var_hbm,
                   msg_ref, later_ref, meta_ref,
                   held, cols_ref, len_ref, weight_ref, owner_ref, locr_ref, locw_ref, obs_ref, var_ref,
                   rows_ref, masked, sorted_ref, meta_in, place_v, place_s, state_sem, arg_sem, place_sem):
    nv = state_hbm.shape[0]
    region = lax.axis_index("region")
    level = lax.axis_index("level")
    pairs = [(cols_hbm, cols_ref), (len_hbm, len_ref), (weight_hbm, weight_ref), (owner_hbm, owner_ref),
             (locr_hbm, locr_ref), (locw_hbm, locw_ref), (obs_hbm, obs_ref), (var_hbm, var_ref)]
    fetches = [pltpu.make_async_copy(a, b, arg_sem.at[i]) for i, (a, b) in enumerate(pairs)]
    for copy in fetches:
        copy.start()
    copies = [pltpu.make_async_copy(state_hbm.at[v], held.at[v], state_sem.at[v]) for v in range(nv)]
    for copy in copies:
        copy.start()
    for copy in fetches:
        copy.wait()
    lane = iota((LANES, LANES), 1)
    sub = iota((LANES, LANES), 0)
    sub8 = iota((SUB, LANES), 0)
    earlier = (sub < lane).astype(BF16)
    region_f = region.astype(F32)
    firsts, places, worst = [], [], None
    for step in range(STEPS):
        cols = cols_ref[step].astype(F32)
        first = jnp.min(cols, axis=0, keepdims=True)
        off = jnp.max(jnp.abs(cols - first - sub[:rays].astype(F32)))
        worst = off if worst is None else jnp.maximum(worst, off)
        home = jnp.zeros_like(first)
        for q in range(1, regions):
            home = home + (first >= float(q * nc)).astype(F32)
        at_home = (sub8.astype(F32) == home).astype(F32)
        count = jnp.dot(at_home.astype(BF16), earlier, preferred_element_type=F32)
        rank = jnp.sum(at_home * count, axis=0, keepdims=True)
        places.append(home * float(slots) + rank)
        firsts.append(first)
        live = sub[:rays] < len_ref[step:step + 1]
        for v in range(nv):
            masked[v, :, step * LANES:(step + 1) * LANES] = jnp.where(live, weight_ref[step, v], 0.0)
    slot = sub[:STEPS * slots].astype(F32)
    mine = []
    for step in range(STEPS):
        ours = (slot >= float(step * slots)) & (slot < float((step + 1) * slots))
        mine.append(((places[step] == slot + (region_f - float(step)) * float(slots)) & ours).astype(F32))
    mine = jnp.concatenate(mine, axis=1)
    first = jnp.broadcast_to(jnp.concatenate(firsts, axis=1), (SUB, STEPS * LANES))
    own_first = jnp.zeros((SUB, STEPS * slots), F32)
    for _ in range(2):
        part = first.astype(BF16)
        own_first = own_first + lax.dot_general(part, mine.astype(BF16), BY_LANES, preferred_element_type=F32)
        first = first - part.astype(F32)
    low = own_first.astype(jnp.int32) - region * nc
    tile = jnp.clip(low // LANES, 0, nc // LANES - 2)
    place_v[...] = jnp.zeros_like(place_v)
    place_v[:, 0:STEPS * slots] = jnp.where(sub8[:, :STEPS * slots] == 0, tile, jnp.clip(low - tile * LANES, 0, 2 * LANES - 1))
    scalars = pltpu.make_async_copy(place_v, place_s, place_sem)
    scalars.start()

    @pl.when(worst > 0.5)
    def _():
        column = jnp.concatenate([cols_ref[s].astype(F32) - firsts[s] for s in range(STEPS)], axis=1)

        def one(d, carry):
            hit = column == d.astype(F32)
            for v in range(nv):
                sorted_ref[v, pl.ds(d, 1)] = jnp.sum(jnp.where(hit, masked[v], 0.0), axis=0, keepdims=True)
            return carry
        lax.fori_loop(0, rays, one, 0)
        masked[...] = sorted_ref[...]

    for v in range(nv):
        rows_ref[v] = jnp.zeros((STEPS * slots, LANES), F32)
        rows_ref[v, :, 0:rays] = pick(mine, masked[v])
    meta_in[...] = jnp.zeros_like(meta_in)
    for step in range(STEPS):
        horiz = (owner_ref[step:step + 1] == region).astype(F32)
        listed = (locr_ref[step] == region).astype(F32)
        horiz = horiz + jnp.sum(locw_ref[step] * listed, axis=0, keepdims=True)
        for l in range(nl):
            meta_in[l:l + 1] = var_ref[step, pl.ds(level * nl + l, 1)]
            meta_in[nl + l:nl + l + 1] = obs_ref[step, pl.ds(level * nl + l, 1)]
        meta_in[2 * nl:2 * nl + 1] = horiz
        order = (places[step] == sub.astype(F32)).astype(F32)
        meta_ref[step] = lax.dot_general(meta_in[...], order, BY_LANES, precision=HIGHEST, preferred_element_type=F32)
    scalars.wait()
    for copy in copies:
        copy.wait()
    groups = nl * nm // SUB
    packed = -(-groups // regions)
    lane8 = iota((SUB, LANES), 1)
    for step in range(STEPS):
        def eight(block, parts, step=step):
            parts = list(parts)
            for u in range(SUB):
                slot = block * SUB + u
                tile = place_s[0, step * slots + slot]
                shift = place_s[1, step * slots + slot]
                start = pl.multiple_of(tile * LANES, LANES)
                sums = [None] * nl
                for v in range(nv):
                    row = jnp.broadcast_to(rows_ref[v, pl.ds(step * slots + slot, 1)], (SUB, LANES))
                    row = pltpu.roll(row, shift & (LANES - 1), 1)
                    for half in range(2):
                        kept = jnp.where((lane8 >= shift) if half == 0 else (lane8 < shift), row, 0.0)
                        for l in range(nl):
                            data = held[v, l, :, pl.ds(start + half * LANES, LANES)]
                            terms = [data[r * SUB:(r + 1) * SUB] * kept for r in range(nm // SUB)]
                            sums[l] = terms if sums[l] is None else [a + b for a, b in zip(sums[l], terms)]
                for l in range(nl):
                    for r in range(nm // SUB):
                        g = l * (nm // SUB) + r
                        result = jnp.sum(sums[l][r], axis=1, keepdims=True)
                        parts[g // regions] = jnp.where(lane8 == slots * (g % regions) + slot, result, parts[g // regions])
            return tuple(parts)
        parts = lax.fori_loop(0, slots // SUB, eight, (jnp.zeros((SUB, LANES), F32),) * packed)
        for j in range(packed):
            if step == 0:
                for d in range(msg_ref.shape[0]):
                    msg_ref[d, j * SUB:(j + 1) * SUB] = parts[j]
            else:
                later_ref[j * SUB:(j + 1) * SUB] = parts[j]


def skew(x, by, sign):
    x = turn(x, by)
    sub8 = iota((SUB, LANES), 0)
    for bit in range(3):
        x = jnp.where((sub8 >> bit) % 2 == 1, turn(x, sign << bit), x)
    return x


def pack_mixing(s, w):
    nm = s.shape[0]
    width, across = nm + 2, LANES // (nm + 2)
    lane8 = iota((SUB, LANES), 1)
    pieces = []
    for g in range(nm // SUB):
        at = width * (g % across)
        part = skew(s[g * SUB:(g + 1) * SUB], at - g * SUB, -1)
        part = jnp.where((lane8 >= at) & (lane8 <= at + nm), part, 0.0)
        part = jnp.where(lane8 == at + nm + 1, w[g * SUB:(g + 1) * SUB], part)
        if g % across:
            pieces[-1] = pieces[-1] + part
        else:
            pieces.append(part)
    return jnp.concatenate(pieces, axis=0)


def unpack_mixing(p, nm):
    width, across = nm + 2, LANES // (nm + 2)
    lane8 = iota((SUB, LANES), 1)
    band, w = [], []
    for g in range(nm // SUB):
        at, j = width * (g % across), g // across
        part = p[j * SUB:(j + 1) * SUB]
        band.append(skew(jnp.where((lane8 >= at) & (lane8 <= at + nm), part, 0.0), g * SUB - at, 1))
        w.append(part[:, at + nm + 1:at + nm + 2])
    return jnp.concatenate(band, axis=0), jnp.concatenate(w, axis=0)


def mixing_rows(first, second, nm):
    (band, w), (band_2, w_2) = first, second
    lane = iota((nm, LANES), 1)
    sub = iota((nm, LANES), 0)
    top = jnp.where((lane > sub) & (lane < nm), band, 0.0)
    low = jnp.where(lane < sub, turn(band_2, -nm), 0.0)
    top = jnp.where(lane == nm, w, top)
    low = jnp.where(lane == nm, w_2, low)
    rest = jnp.zeros((LANES - 2 * nm, LANES), F32)
    turned = jnp.concatenate([top, low, rest], axis=0).T
    return turned[nm:nm + 1] - (band + turned[:nm])


def local_kernel(step, nl, nm, regions, slots, levels, level_count, cores,
                 got_ref, meta_ref, msg_ref, local_ref, spread_ref):
    level = lax.axis_index("level")
    member = lax.axis_index("member")
    members = nm * cores
    scale = levels / 4.0
    lane8 = iota((SUB, LANES), 1)
    mats = []
    for l in range(nl):
        rows = []
        for c in (member, 1 - member):
            for r in range(nm // SUB):
                g = l * (nm // SUB) + r
                j, k = g // regions, g % regions
                row = None
                for p in range(regions):
                    part = turn(got_ref[p * cores + c, j * SUB:(j + 1) * SUB], slots * (p - k))
                    row = part if row is None else jnp.where(lane8 >= slots * p, part, row)
                rows.append(row)
        predicted = jnp.concatenate(rows, axis=0)
        mean = jnp.sum(predicted, axis=0, keepdims=True) * (1.0 / members)
        spread = predicted - mean
        variance = jnp.sum(spread * spread, axis=0, keepdims=True) * (1.0 / (members - 1.0))
        obs_var = meta_ref[step, l:l + 1]
        obs_value = meta_ref[step, nl + l:nl + l + 1]
        horiz = meta_ref[step, 2 * nl:2 * nl + 1]
        total_var = variance + obs_var
        gain = (obs_value - mean) / total_var
        shrink = 1.0 / (1.0 + jnp.sqrt(obs_var / total_var))
        scaled = horiz * (1.0 / (members - 1.0))
        spread_ref[l, 0:members] = spread
        spread_ref[l, members:] = jnp.zeros((LANES - members, LANES), F32)
        own = spread[:nm]
        left = scaled * (shrink / total_var) * own
        s = lax.dot_general(left, spread_ref[l], BY_LANES, precision=HIGHEST, preferred_element_type=F32)
        mats.append(pack_mixing(s, jnp.sum(scaled * gain * own, axis=1, keepdims=True)))
    up = sum(math.exp(-(nl - 1 - l) / scale) * mats[l] for l in range(nl))
    down = sum(math.exp(-l / scale) * mats[l] for l in range(nl))
    for l in range(nl):
        local_ref[l] = sum(math.exp(-abs(l - k) / scale) * mats[k] for k in range(nl))
    for d in range(level_count):
        msg_ref[d] = jnp.where(d > level, up, down)


def combine_kernel(nl, levels, level_count, got_ref, local_ref, *refs):
    out_ref = refs[-1]
    level = lax.axis_index("level")
    scale = levels / 4.0
    fade = math.exp(-nl / scale)
    rows = got_ref.shape[1]
    zero = jnp.zeros(got_ref.shape[1:], F32)
    below = lax.fori_loop(0, level, lambda d, acc: acc * fade + got_ref[d], zero)
    above = lax.fori_loop(0, level_count - 1 - level, lambda d, acc: acc * fade + got_ref[level_count - 1 - d], zero)
    for l in range(nl):
        out_ref[l * rows:(l + 1) * rows] = (
            math.exp(-(l + 1) / scale) * below + math.exp(-(nl - l) / scale) * above + local_ref[l]
        )
    if len(refs) > 1:
        out_ref[nl * rows:] = refs[0][...]


def forecast_kernel(nl, nm, regions, slots, own_ref, other_ref, mix_ref, msg_ref, full_ref):
    lane8 = iota((SUB, LANES), 1)
    lane = iota((nm, LANES), 1)
    groups = nl * nm // SUB
    packed = -(-groups // regions)
    first = own_ref.shape[0] - packed * SUB
    rows = first // nl
    parts = [jnp.zeros((SUB, LANES), F32) for _ in range(packed)]
    for l in range(nl):
        pieces = []
        for ref in (own_ref, other_ref):
            for r in range(nm // SUB):
                g = l * (nm // SUB) + r
                j, k = g // regions, g % regions
                pieces.append(turn(ref[first + j * SUB:first + (j + 1) * SUB], -slots * k))
        own = jnp.concatenate(pieces[:nm // SUB], axis=0)
        pieces.append(jnp.zeros((LANES - 2 * nm, LANES), F32))
        full_ref[l] = jnp.concatenate(pieces, axis=0)
        bands = [unpack_mixing(ref[l * rows:(l + 1) * rows], nm) for ref in (own_ref, other_ref)]
        upper = mixing_rows(bands[0], bands[1], nm)
        mix_ref[l, 0:nm] = upper
        result = own + dot(upper, full_ref[l])
        for r in range(nm // SUB):
            g = l * (nm // SUB) + r
            j, k = g // regions, g % regions
            keep = (lane8 >= slots * k) & (lane8 < slots * (k + 1))
            parts[j] = jnp.where(keep, turn(result[r * SUB:(r + 1) * SUB], slots * k), parts[j])
        lower = mixing_rows(bands[1], bands[0], nm)
        swapped = jnp.where(lane < nm, turn(lower, -nm), jnp.where(lane < 2 * nm, turn(lower, nm), 0.0))
        mix_ref[l, nm:2 * nm] = swapped
        mix_ref[l, 2 * nm:] = jnp.zeros((LANES - 2 * nm, LANES), F32)
    for d in range(msg_ref.shape[0]):
        for j in range(packed):
            msg_ref[d, j * SUB:(j + 1) * SUB] = parts[j]


def split(x):
    high = x.astype(BF16).astype(F32)
    return high, x - high


def update_kernel(nl, nm, own_ref, other_ref, mix_ref, state_hbm, theirs_hbm, out_hbm,
                  mine_v, theirs_v, out_v, left_ref, in_sem, out_sem):
    nv = state_hbm.shape[0]
    members = 2 * nm
    blocks = [(v, l) for l in range(nl) for v in range(nv)]
    fetches = []
    for i, (v, l) in enumerate(blocks):
        pair = (pltpu.make_async_copy(state_hbm.at[v, l], mine_v.at[v, l], in_sem.at[2 * i]),
                pltpu.make_async_copy(theirs_hbm.at[v, l], theirs_v.at[v, l], in_sem.at[2 * i + 1]))
        for copy in pair:
            copy.start()
        fetches.append(pair)
    rows = own_ref.shape[0] // nl
    lane = iota((nm, LANES), 1)
    for l in range(nl):
        bands = [unpack_mixing(ref[l * rows:(l + 1) * rows], nm) for ref in (own_ref, other_ref)]
        second = mixing_rows(bands[0], bands[1], nm)
        both = second + mix_ref[l, 0:nm] + dot(second, mix_ref[l])
        high, low = split(both)
        again = turn(high, members)
        left_ref[l, :, 0:LANES] = high + jnp.where(lane >= members, again, 0.0)
        left_ref[l, :, LANES:] = jnp.where(lane < 2 * members - LANES, again, 0.0) + turn(low, 2 * members - LANES)
    pad = jnp.zeros((2 * LANES - 3 * members, state_hbm.shape[3]), F32)
    stores = []
    for i, (v, l) in enumerate(blocks):
        for copy in fetches[i]:
            copy.wait()
        own = mine_v[v, l]
        high, low = split(jnp.concatenate([own, theirs_v[v, l]], axis=0))
        right = jnp.concatenate([high, low, high, pad], axis=0).astype(BF16)
        out_v[v, l] = own + jnp.dot(left_ref[l].astype(BF16), right, preferred_element_type=F32)
        copy = pltpu.make_async_copy(out_v.at[v, l], out_hbm.at[v, l], out_sem.at[i])
        copy.start()
        stores.append(copy)
    for copy in stores:
        copy.wait()


def body(state, ray_cols, ray_len, ray_weight, owner, loc_regions, loc_weight, obs_value, obs_var):
    regions = lax.axis_size("region")
    level_count = lax.axis_size("level")
    cores = lax.axis_size("member")
    nv, nl, nm, nc = state.shape
    occ, rays = ray_cols.shape[1:]
    slots = occ // regions
    levels = nl * level_count
    assert occ == LANES and regions * slots == LANES and nm % SUB == 0 and cores == 2
    groups = nl * nm // SUB
    block = (-(-groups // regions) * SUB, LANES)
    mixing = (-(-(nm // SUB) // (LANES // (nm + 2))) * SUB, LANES)
    whole = pl.BlockSpec(memory_space=VMEM)
    outside = pl.BlockSpec(memory_space=pltpu.HBM)
    swap = [(0, 1), (1, 0)]
    dma = pltpu.SemaphoreType.DMA

    def call(kernel, statics, outs, scratch, *args, specs=None, out_specs=None, name=None):
        def wrapped(*refs):
            return kernel(*statics, *refs)
        return pl.pallas_call(
            wrapped,
            out_shape=[jax.ShapeDtypeStruct(s, F32) for s in outs],
            in_specs=specs or [whole] * len(args),
            out_specs=out_specs or [whole] * len(outs),
            scratch_shapes=scratch,
            compiler_params=pltpu.CompilerParams(vmem_limit_bytes=32 * 2**20),
            name=name,
        )(*args)

    other_state = lax.ppermute(state, "member", swap)
    given = [ray_cols.swapaxes(1, 2), ray_len, ray_weight.transpose(0, 2, 3, 1), owner, loc_regions.swapaxes(1, 2),
             loc_weight.swapaxes(1, 2), obs_value.swapaxes(1, 2), obs_var.swapaxes(1, 2)]
    msg, later, meta = call(
        predict_kernel, (nl, nm, nc, regions, slots, rays),
        [(regions * cores,) + block, block, (STEPS, SUB, LANES)],
        [VMEM(state.shape, F32)] + [VMEM(a.shape, a.dtype) for a in given]
        + [VMEM((nv, STEPS * slots, LANES), F32), VMEM((nv, rays, STEPS * LANES), F32),
           VMEM((nv, rays, STEPS * LANES), F32), VMEM((SUB, LANES), F32),
           VMEM((SUB, LANES), jnp.int32), pltpu.SMEM((SUB, LANES), jnp.int32), dma((nv,)), dma((len(given),)), dma],
        state, *given, specs=[outside] * (1 + len(given)), name="predict",
    )

    def assimilate(step, msg, *more):
        got = lax.all_to_all(msg, ("region", "member"), 0, 0, tiled=True)
        out, local = call(
            local_kernel, (step, nl, nm, regions, slots, levels, level_count, cores),
            [(level_count,) + mixing, (nl,) + mixing], [VMEM((nl, LANES, LANES), F32)],
            got, meta, name="local",
        )
        got = lax.all_to_all(out, "level", 0, 0, tiled=True)
        rows = nl * mixing[0] + sum(a.shape[0] for a in more)
        own, = call(combine_kernel, (nl, levels, level_count), [(rows, LANES)], [], got, local, *more, name="combine")
        return own, lax.ppermute(own, "member", swap)

    own, other = assimilate(0, msg, later)
    mix, msg = call(
        forecast_kernel, (nl, nm, regions, slots),
        [(nl, LANES, LANES), (regions * cores,) + block], [VMEM((nl, LANES, LANES), F32)],
        own, other, name="forecast",
    )
    own, other = assimilate(1, msg)
    out, = call(
        update_kernel, (nl, nm), [state.shape],
        [VMEM(state.shape, F32)] * 3 + [VMEM((nl, nm, 2 * LANES), F32), dma((2 * nv * nl,)), dma((nv * nl,))],
        own, other, mix, state, other_state, specs=[whole] * 3 + [outside] * 2, out_specs=[outside], name="update",
    )
    return out


def solution(mesh):
    in_specs = (P(None, "level", "member", "region"), P(), P(), P(), P(), P(), P(), P(), P())
    out_specs = P(None, "level", "member", "region")
    return jax.shard_map(body, mesh=mesh, in_specs=in_specs, out_specs=out_specs, check_vma=False)
```

```python
import math

import jax
import jax.numpy as jnp
from jax import lax
from jax.experimental import pallas as pl
from jax.experimental.pallas import tpu as pltpu
from jax.sharding import PartitionSpec as P

STEPS = 2
LANES = 128
SUB = 8
HIGHEST = lax.Precision.HIGHEST
F32 = jnp.float32
BF16 = jnp.bfloat16
VMEM = pltpu.VMEM
BY_LANES = (((1,), (1,)), ((), ()))


def iota(shape, dim):
    return lax.broadcasted_iota(jnp.int32, shape, dim)


def dot(a, b):
    return jnp.dot(a, b, precision=HIGHEST, preferred_element_type=F32)


def turn(x, by):
    by = by % LANES
    return pltpu.roll(x, by, 1) if by else x


def pick(chosen, values):
    chosen = chosen.astype(BF16)
    total = None
    for _ in range(3):
        part = values.astype(BF16)
        term = lax.dot_general(chosen, part, BY_LANES, preferred_element_type=F32)
        total = term if total is None else total + term
        values = values - part.astype(F32)
    return total


def predict_kernel(nl, nm, nc, regions, slots, rays,
                   state_hbm, cols_hbm, len_hbm, weight_hbm, owner_hbm, locr_hbm, locw_hbm, obs_hbm, var_hbm,
                   msg_ref, later_ref, meta_ref,
                   held, cols_ref, len_ref, weight_ref, owner_ref, locr_ref, locw_ref, obs_ref, var_ref,
                   rows_ref, masked, sorted_ref, meta_in, place_v, place_s, state_sem, arg_sem, place_sem):
    nv = state_hbm.shape[0]
    region = lax.axis_index("region")
    level = lax.axis_index("level")
    pairs = [(cols_hbm, cols_ref), (len_hbm, len_ref), (weight_hbm, weight_ref), (owner_hbm, owner_ref),
             (locr_hbm, locr_ref), (locw_hbm, locw_ref), (obs_hbm, obs_ref), (var_hbm, var_ref)]
    fetches = [pltpu.make_async_copy(a, b, arg_sem.at[i]) for i, (a, b) in enumerate(pairs)]
    for copy in fetches:
        copy.start()
    copies = [pltpu.make_async_copy(state_hbm.at[v], held.at[v], state_sem.at[v]) for v in range(nv)]
    for copy in copies:
        copy.start()
    for copy in fetches:
        copy.wait()
    lane = iota((LANES, LANES), 1)
    sub = iota((LANES, LANES), 0)
    sub8 = iota((SUB, LANES), 0)
    earlier = (sub < lane).astype(BF16)
    region_f = region.astype(F32)
    firsts, places, worst = [], [], None
    for step in range(STEPS):
        cols = cols_ref[step].astype(F32)
        first = jnp.min(cols, axis=0, keepdims=True)
        off = jnp.max(jnp.abs(cols - first - sub[:rays].astype(F32)))
        worst = off if worst is None else jnp.maximum(worst, off)
        home = jnp.zeros_like(first)
        for q in range(1, regions):
            home = home + (first >= float(q * nc)).astype(F32)
        at_home = (sub8.astype(F32) == home).astype(F32)
        count = jnp.dot(at_home.astype(BF16), earlier, preferred_element_type=F32)
        rank = jnp.sum(at_home * count, axis=0, keepdims=True)
        places.append(home * float(slots) + rank)
        firsts.append(first)
        live = sub[:rays] < len_ref[step:step + 1]
        for v in range(nv):
            masked[v, :, step * LANES:(step + 1) * LANES] = jnp.where(live, weight_ref[step, v], 0.0)
    slot = sub[:STEPS * slots].astype(F32)
    mine = []
    for step in range(STEPS):
        ours = (slot >= float(step * slots)) & (slot < float((step + 1) * slots))
        mine.append(((places[step] == slot + (region_f - float(step)) * float(slots)) & ours).astype(F32))
    mine = jnp.concatenate(mine, axis=1)
    first = jnp.broadcast_to(jnp.concatenate(firsts, axis=1), (SUB, STEPS * LANES))
    own_first = jnp.zeros((SUB, STEPS * slots), F32)
    for _ in range(2):
        part = first.astype(BF16)
        own_first = own_first + lax.dot_general(part, mine.astype(BF16), BY_LANES, preferred_element_type=F32)
        first = first - part.astype(F32)
    low = own_first.astype(jnp.int32) - region * nc
    tile = jnp.clip(low // LANES, 0, nc // LANES - 2)
    place_v[...] = jnp.zeros_like(place_v)
    place_v[:, 0:STEPS * slots] = jnp.where(sub8[:, :STEPS * slots] == 0, tile, jnp.clip(low - tile * LANES, 0, 2 * LANES - 1))
    scalars = pltpu.make_async_copy(place_v, place_s, place_sem)
    scalars.start()

    @pl.when(worst > 0.5)
    def _():
        column = jnp.concatenate([cols_ref[s].astype(F32) - firsts[s] for s in range(STEPS)], axis=1)

        def one(d, carry):
            hit = column == d.astype(F32)
            for v in range(nv):
                sorted_ref[v, pl.ds(d, 1)] = jnp.sum(jnp.where(hit, masked[v], 0.0), axis=0, keepdims=True)
            return carry
        lax.fori_loop(0, rays, one, 0)
        masked[...] = sorted_ref[...]

    for v in range(nv):
        rows_ref[v] = jnp.zeros((STEPS * slots, LANES), F32)
        rows_ref[v, :, 0:rays] = pick(mine, masked[v])
    meta_in[...] = jnp.zeros_like(meta_in)
    for step in range(STEPS):
        horiz = (owner_ref[step:step + 1] == region).astype(F32)
        listed = (locr_ref[step] == region).astype(F32)
        horiz = horiz + jnp.sum(locw_ref[step] * listed, axis=0, keepdims=True)
        for l in range(nl):
            meta_in[l:l + 1] = var_ref[step, pl.ds(level * nl + l, 1)]
            meta_in[nl + l:nl + l + 1] = obs_ref[step, pl.ds(level * nl + l, 1)]
        meta_in[2 * nl:2 * nl + 1] = horiz
        order = (places[step] == sub.astype(F32)).astype(F32)
        meta_ref[step] = lax.dot_general(meta_in[...], order, BY_LANES, precision=HIGHEST, preferred_element_type=F32)
    scalars.wait()
    for copy in copies:
        copy.wait()
    groups = nl * nm // SUB
    packed = -(-groups // regions)
    lane8 = iota((SUB, LANES), 1)
    for step in range(STEPS):
        def eight(block, parts, step=step):
            parts = list(parts)
            for u in range(SUB):
                slot = block * SUB + u
                tile = place_s[0, step * slots + slot]
                shift = place_s[1, step * slots + slot]
                start = pl.multiple_of(tile * LANES, LANES)
                sums = [None] * nl
                for v in range(nv):
                    row = jnp.broadcast_to(rows_ref[v, pl.ds(step * slots + slot, 1)], (SUB, LANES))
                    row = pltpu.roll(row, shift & (LANES - 1), 1)
                    for half in range(2):
                        kept = jnp.where((lane8 >= shift) if half == 0 else (lane8 < shift), row, 0.0)
                        for l in range(nl):
                            data = held[v, l, :, pl.ds(start + half * LANES, LANES)]
                            terms = [data[r * SUB:(r + 1) * SUB] * kept for r in range(nm // SUB)]
                            sums[l] = terms if sums[l] is None else [a + b for a, b in zip(sums[l], terms)]
                for l in range(nl):
                    for r in range(nm // SUB):
                        g = l * (nm // SUB) + r
                        result = jnp.sum(sums[l][r], axis=1, keepdims=True)
                        parts[g // regions] = jnp.where(lane8 == slots * (g % regions) + slot, result, parts[g // regions])
            return tuple(parts)
        parts = lax.fori_loop(0, slots // SUB, eight, (jnp.zeros((SUB, LANES), F32),) * packed)
        for j in range(packed):
            if step == 0:
                for d in range(msg_ref.shape[0]):
                    msg_ref[d, j * SUB:(j + 1) * SUB] = parts[j]
            else:
                later_ref[j * SUB:(j + 1) * SUB] = parts[j]


def skew(x, by, sign):
    x = turn(x, by)
    sub8 = iota((SUB, LANES), 0)
    for bit in range(3):
        x = jnp.where((sub8 >> bit) % 2 == 1, turn(x, sign << bit), x)
    return x


def pack_mixing(s, w):
    nm = s.shape[0]
    width, across = nm + 2, LANES // (nm + 2)
    lane8 = iota((SUB, LANES), 1)
    pieces = []
    for g in range(nm // SUB):
        at = width * (g % across)
        part = skew(s[g * SUB:(g + 1) * SUB], at - g * SUB, -1)
        part = jnp.where((lane8 >= at) & (lane8 <= at + nm), part, 0.0)
        part = jnp.where(lane8 == at + nm + 1, w[g * SUB:(g + 1) * SUB], part)
        if g % across:
            pieces[-1] = pieces[-1] + part
        else:
            pieces.append(part)
    return jnp.concatenate(pieces, axis=0)


def unpack_mixing(p, nm):
    width, across = nm + 2, LANES // (nm + 2)
    lane8 = iota((SUB, LANES), 1)
    band, w = [], []
    for g in range(nm // SUB):
        at, j = width * (g % across), g // across
        part = p[j * SUB:(j + 1) * SUB]
        band.append(skew(jnp.where((lane8 >= at) & (lane8 <= at + nm), part, 0.0), g * SUB - at, 1))
        w.append(part[:, at + nm + 1:at + nm + 2])
    return jnp.concatenate(band, axis=0), jnp.concatenate(w, axis=0)


def mixing_rows(first, second, nm):
    (band, w), (band_2, w_2) = first, second
    lane = iota((nm, LANES), 1)
    sub = iota((nm, LANES), 0)
    top = jnp.where((lane > sub) & (lane < nm), band, 0.0)
    low = jnp.where(lane < sub, turn(band_2, -nm), 0.0)
    top = jnp.where(lane == nm, w, top)
    low = jnp.where(lane == nm, w_2, low)
    rest = jnp.zeros((LANES - 2 * nm, LANES), F32)
    turned = jnp.concatenate([top, low, rest], axis=0).T
    return turned[nm:nm + 1] - (band + turned[:nm])


def local_kernel(step, nl, nm, regions, slots, levels, level_count, cores,
                 got_ref, meta_ref, msg_ref, local_ref, spread_ref):
    level = lax.axis_index("level")
    member = lax.axis_index("member")
    members = nm * cores
    scale = levels / 4.0
    lane8 = iota((SUB, LANES), 1)
    mats = []
    for l in range(nl):
        rows = []
        for c in (member, 1 - member):
            for r in range(nm // SUB):
                g = l * (nm // SUB) + r
                j, k = g // regions, g % regions
                row = None
                for p in range(regions):
                    part = turn(got_ref[p * cores + c, j * SUB:(j + 1) * SUB], slots * (p - k))
                    row = part if row is None else jnp.where(lane8 >= slots * p, part, row)
                rows.append(row)
        predicted = jnp.concatenate(rows, axis=0)
        mean = jnp.sum(predicted, axis=0, keepdims=True) * (1.0 / members)
        spread = predicted - mean
        variance = jnp.sum(spread * spread, axis=0, keepdims=True) * (1.0 / (members - 1.0))
        obs_var = meta_ref[step, l:l + 1]
        obs_value = meta_ref[step, nl + l:nl + l + 1]
        horiz = meta_ref[step, 2 * nl:2 * nl + 1]
        total_var = variance + obs_var
        gain = (obs_value - mean) / total_var
        shrink = 1.0 / (1.0 + jnp.sqrt(obs_var / total_var))
        scaled = horiz * (1.0 / (members - 1.0))
        spread_ref[l, 0:members] = spread
        spread_ref[l, members:] = jnp.zeros((LANES - members, LANES), F32)
        own = spread[:nm]
        left = scaled * (shrink / total_var) * own
        s = lax.dot_general(left, spread_ref[l], BY_LANES, precision=HIGHEST, preferred_element_type=F32)
        mats.append(pack_mixing(s, jnp.sum(scaled * gain * own, axis=1, keepdims=True)))
    up = sum(math.exp(-(nl - 1 - l) / scale) * mats[l] for l in range(nl))
    down = sum(math.exp(-l / scale) * mats[l] for l in range(nl))
    for l in range(nl):
        local_ref[l] = sum(math.exp(-abs(l - k) / scale) * mats[k] for k in range(nl))
    for d in range(level_count):
        msg_ref[d] = jnp.where(d > level, up, down)


def combine_kernel(nl, levels, level_count, got_ref, local_ref, *refs):
    out_ref = refs[-1]
    level = lax.axis_index("level")
    scale = levels / 4.0
    fade = math.exp(-nl / scale)
    rows = got_ref.shape[1]
    zero = jnp.zeros(got_ref.shape[1:], F32)
    below = lax.fori_loop(0, level, lambda d, acc: acc * fade + got_ref[d], zero)
    above = lax.fori_loop(0, level_count - 1 - level, lambda d, acc: acc * fade + got_ref[level_count - 1 - d], zero)
    for l in range(nl):
        out_ref[l * rows:(l + 1) * rows] = (
            math.exp(-(l + 1) / scale) * below + math.exp(-(nl - l) / scale) * above + local_ref[l]
        )
    if len(refs) > 1:
        out_ref[nl * rows:] = refs[0][...]


def forecast_kernel(nl, nm, regions, slots, own_ref, other_ref, mix_ref, msg_ref, full_ref):
    lane8 = iota((SUB, LANES), 1)
    lane = iota((nm, LANES), 1)
    groups = nl * nm // SUB
    packed = -(-groups // regions)
    first = own_ref.shape[0] - packed * SUB
    rows = first // nl
    parts = [jnp.zeros((SUB, LANES), F32) for _ in range(packed)]
    for l in range(nl):
        pieces = []
        for ref in (own_ref, other_ref):
            for r in range(nm // SUB):
                g = l * (nm // SUB) + r
                j, k = g // regions, g % regions
                pieces.append(turn(ref[first + j * SUB:first + (j + 1) * SUB], -slots * k))
        own = jnp.concatenate(pieces[:nm // SUB], axis=0)
        pieces.append(jnp.zeros((LANES - 2 * nm, LANES), F32))
        full_ref[l] = jnp.concatenate(pieces, axis=0)
        bands = [unpack_mixing(ref[l * rows:(l + 1) * rows], nm) for ref in (own_ref, other_ref)]
        upper = mixing_rows(bands[0], bands[1], nm)
        mix_ref[l, 0:nm] = upper
        result = own + dot(upper, full_ref[l])
        for r in range(nm // SUB):
            g = l * (nm // SUB) + r
            j, k = g // regions, g % regions
            keep = (lane8 >= slots * k) & (lane8 < slots * (k + 1))
            parts[j] = jnp.where(keep, turn(result[r * SUB:(r + 1) * SUB], slots * k), parts[j])
        lower = mixing_rows(bands[1], bands[0], nm)
        swapped = jnp.where(lane < nm, turn(lower, -nm), jnp.where(lane < 2 * nm, turn(lower, nm), 0.0))
        mix_ref[l, nm:2 * nm] = swapped
        mix_ref[l, 2 * nm:] = jnp.zeros((LANES - 2 * nm, LANES), F32)
    for d in range(msg_ref.shape[0]):
        for j in range(packed):
            msg_ref[d, j * SUB:(j + 1) * SUB] = parts[j]


def split(x):
    high = x.astype(BF16).astype(F32)
    return high, x - high


def update_kernel(nl, nm, own_ref, other_ref, mix_ref, state_ref, theirs_ref, out_hbm,
                  out_v, left_ref, out_sem):
    nv = state_ref.shape[0]
    members = 2 * nm
    blocks = [(v, l) for l in range(nl) for v in range(nv)]
    rows = own_ref.shape[0] // nl
    lane = iota((nm, LANES), 1)
    for l in range(nl):
        bands = [unpack_mixing(ref[l * rows:(l + 1) * rows], nm) for ref in (own_ref, other_ref)]
        second = mixing_rows(bands[0], bands[1], nm)
        both = second + mix_ref[l, 0:nm] + dot(second, mix_ref[l])
        high, low = split(both)
        again = turn(high, members)
        left_ref[l, :, 0:LANES] = high + jnp.where(lane >= members, again, 0.0)
        left_ref[l, :, LANES:] = jnp.where(lane < 2 * members - LANES, again, 0.0) + turn(low, 2 * members - LANES)
    pad = jnp.zeros((2 * LANES - 3 * members, state_ref.shape[3]), F32)
    stores = []
    for i, (v, l) in enumerate(blocks):
        own = state_ref[v, l]
        high, low = split(jnp.concatenate([own, theirs_ref[v, l]], axis=0))
        right = jnp.concatenate([high, low, high, pad], axis=0).astype(BF16)
        out_v[v, l] = own + jnp.dot(left_ref[l].astype(BF16), right, preferred_element_type=F32)
        copy = pltpu.make_async_copy(out_v.at[v, l], out_hbm.at[v, l], out_sem.at[i])
        copy.start()
        stores.append(copy)
    for copy in stores:
        copy.wait()


def body(state, ray_cols, ray_len, ray_weight, owner, loc_regions, loc_weight, obs_value, obs_var):
    regions = lax.axis_size("region")
    level_count = lax.axis_size("level")
    cores = lax.axis_size("member")
    nv, nl, nm, nc = state.shape
    occ, rays = ray_cols.shape[1:]
    slots = occ // regions
    levels = nl * level_count
    assert occ == LANES and regions * slots == LANES and nm % SUB == 0 and cores == 2
    groups = nl * nm // SUB
    block = (-(-groups // regions) * SUB, LANES)
    mixing = (-(-(nm // SUB) // (LANES // (nm + 2))) * SUB, LANES)
    whole = pl.BlockSpec(memory_space=VMEM)
    outside = pl.BlockSpec(memory_space=pltpu.HBM)
    swap = [(0, 1), (1, 0)]
    dma = pltpu.SemaphoreType.DMA

    def call(kernel, statics, outs, scratch, *args, specs=None, out_specs=None, name=None, limit=32):
        def wrapped(*refs):
            return kernel(*statics, *refs)
        return pl.pallas_call(
            wrapped,
            out_shape=[jax.ShapeDtypeStruct(s, F32) for s in outs],
            in_specs=specs or [whole] * len(args),
            out_specs=out_specs or [whole] * len(outs),
            scratch_shapes=scratch,
            compiler_params=pltpu.CompilerParams(vmem_limit_bytes=limit * 2**20),
            name=name,
        )(*args)

    other_state = lax.ppermute(state, "member", swap)
    given = [ray_cols.swapaxes(1, 2), ray_len, ray_weight.transpose(0, 2, 3, 1), owner, loc_regions.swapaxes(1, 2),
             loc_weight.swapaxes(1, 2), obs_value.swapaxes(1, 2), obs_var.swapaxes(1, 2)]
    msg, later, meta = call(
        predict_kernel, (nl, nm, nc, regions, slots, rays),
        [(regions * cores,) + block, block, (STEPS, SUB, LANES)],
        [VMEM(state.shape, F32)] + [VMEM(a.shape, a.dtype) for a in given]
        + [VMEM((nv, STEPS * slots, LANES), F32), VMEM((nv, rays, STEPS * LANES), F32),
           VMEM((nv, rays, STEPS * LANES), F32), VMEM((SUB, LANES), F32),
           VMEM((SUB, LANES), jnp.int32), pltpu.SMEM((SUB, LANES), jnp.int32), dma((nv,)), dma((len(given),)), dma],
        state, *given, specs=[outside] * (1 + len(given)), name="predict", limit=60,
    )

    def assimilate(step, msg, *more):
        got = lax.all_to_all(msg, ("region", "member"), 0, 0, tiled=True)
        out, local = call(
            local_kernel, (step, nl, nm, regions, slots, levels, level_count, cores),
            [(level_count,) + mixing, (nl,) + mixing], [VMEM((nl, LANES, LANES), F32)],
            got, meta, name="local",
        )
        got = lax.all_to_all(out, "level", 0, 0, tiled=True)
        rows = nl * mixing[0] + sum(a.shape[0] for a in more)
        own, = call(combine_kernel, (nl, levels, level_count), [(rows, LANES)], [], got, local, *more, name="combine")
        return own, lax.ppermute(own, "member", swap)

    own, other = assimilate(0, msg, later)
    mix, msg = call(
        forecast_kernel, (nl, nm, regions, slots),
        [(nl, LANES, LANES), (regions * cores,) + block], [VMEM((nl, LANES, LANES), F32)],
        own, other, name="forecast",
    )
    own, other = assimilate(1, msg)
    out, = call(
        update_kernel, (nl, nm), [state.shape],
        [VMEM(state.shape, F32), VMEM((nl, nm, 2 * LANES), F32), dma((nv * nl,))],
        own, other, mix, state, other_state, out_specs=[outside], name="update",
    )
    return out


def solution(mesh):
    in_specs = (P(None, "level", "member", "region"), P(), P(), P(), P(), P(), P(), P(), P())
    out_specs = P(None, "level", "member", "region")
    return jax.shard_map(body, mesh=mesh, in_specs=in_specs, out_specs=out_specs, check_vma=False)
```

```python
import math

import jax
import jax.numpy as jnp
from jax import lax
from jax.experimental import pallas as pl
from jax.experimental.pallas import tpu as pltpu
from jax.sharding import PartitionSpec as P

STEPS = 2
LANES = 128
SUB = 8
HIGHEST = lax.Precision.HIGHEST
F32 = jnp.float32
BF16 = jnp.bfloat16
VMEM = pltpu.VMEM
BY_LANES = (((1,), (1,)), ((), ()))


def iota(shape, dim):
    return lax.broadcasted_iota(jnp.int32, shape, dim)


def dot(a, b):
    return jnp.dot(a, b, precision=HIGHEST, preferred_element_type=F32)


def turn(x, by):
    by = by % LANES
    return pltpu.roll(x, by, 1) if by else x


def pick(chosen, values):
    chosen = chosen.astype(BF16)
    total = None
    for _ in range(3):
        part = values.astype(BF16)
        term = lax.dot_general(chosen, part, BY_LANES, preferred_element_type=F32)
        total = term if total is None else total + term
        values = values - part.astype(F32)
    return total


def predict_kernel(nl, nm, nc, regions, slots, rays,
                   state_hbm, cols_hbm, len_hbm, weight_hbm, owner_hbm, locr_hbm, locw_hbm, obs_hbm, var_hbm,
                   msg_ref, later_ref, meta_ref,
                   held, cols_ref, len_ref, weight_ref, owner_ref, locr_ref, locw_ref, obs_ref, var_ref,
                   masked, sorted_ref, spread_out, meta_in, state_sem, arg_sem):
    nv = state_hbm.shape[0]
    region = lax.axis_index("region")
    level = lax.axis_index("level")
    pairs = [(cols_hbm, cols_ref), (len_hbm, len_ref), (weight_hbm, weight_ref), (owner_hbm, owner_ref),
             (locr_hbm, locr_ref), (locw_hbm, locw_ref), (obs_hbm, obs_ref), (var_hbm, var_ref)]
    fetches = [pltpu.make_async_copy(a, b, arg_sem.at[i]) for i, (a, b) in enumerate(pairs)]
    for copy in fetches:
        copy.start()
    copies = [pltpu.make_async_copy(state_hbm.at[v], held.at[v], state_sem.at[v]) for v in range(nv)]
    for copy in copies:
        copy.start()
    lane = iota((LANES, LANES), 1)
    sub = iota((LANES, LANES), 0)
    sub8 = iota((SUB, LANES), 0)
    earlier = (sub < lane).astype(BF16)
    region_f = region.astype(F32)
    masked[nv * rays:] = jnp.zeros((masked.shape[0] - nv * rays, STEPS * LANES), F32)
    meta_in[...] = jnp.zeros_like(meta_in)
    for copy in fetches:
        copy.wait()
    firsts, places, worst = [], [], None
    for step in range(STEPS):
        cols = cols_ref[step].astype(F32)
        first = jnp.min(cols, axis=0, keepdims=True)
        off = jnp.max(jnp.abs(cols - first - sub[:rays].astype(F32)))
        worst = off if worst is None else jnp.maximum(worst, off)
        home = jnp.zeros_like(first)
        for q in range(1, regions):
            home = home + (first >= float(q * nc)).astype(F32)
        at_home = (sub8.astype(F32) == home).astype(F32)
        count = jnp.dot(at_home.astype(BF16), earlier, preferred_element_type=F32)
        rank = jnp.sum(at_home * count, axis=0, keepdims=True)
        places.append(home * float(slots) + rank)
        firsts.append(first)
        live = sub[:rays] < len_ref[step:step + 1]
        for v in range(nv):
            masked[v * rays:(v + 1) * rays, step * LANES:(step + 1) * LANES] = jnp.where(live, weight_ref[step, v], 0.0)
    slot = sub[:STEPS * slots].astype(F32)
    mine = []
    for step in range(STEPS):
        ours = (slot >= float(step * slots)) & (slot < float((step + 1) * slots))
        mine.append(((places[step] == slot + (region_f - float(step)) * float(slots)) & ours).astype(F32))
    mine = jnp.concatenate(mine, axis=1)

    @pl.when(worst > 0.5)
    def _():
        column = jnp.concatenate([cols_ref[s].astype(F32) - firsts[s] for s in range(STEPS)], axis=1)

        def one(d, carry):
            hit = column == d.astype(F32)
            for v in range(nv):
                weights = masked[v * rays:(v + 1) * rays]
                sorted_ref[pl.ds(v * rays + d, 1)] = jnp.sum(jnp.where(hit, weights, 0.0), axis=0, keepdims=True)
            return carry
        lax.fori_loop(0, rays, one, 0)
        masked[0:nv * rays] = sorted_ref[...]

    first = jnp.broadcast_to(jnp.concatenate(firsts, axis=1), (LANES, STEPS * LANES))
    low = pick(mine, first).astype(jnp.int32) - region * nc
    tile, shift = low >> 7, low & (LANES - 1)
    picked = pick(mine, masked[...])
    lane_s = lane[:STEPS * slots]
    for v in range(nv):
        at = v * rays
        row = picked[:, at // LANES * LANES:(at // LANES + 1) * LANES]
        at = at % LANES
        row = turn(jnp.where((lane_s >= at) & (lane_s < at + rays), row, 0.0), -at)
        for bit in range(7):
            row = jnp.where((shift >> bit) % 2 == 1, turn(row, 1 << bit), row)
        near, far = jnp.where(lane_s >= shift, row, 0.0), jnp.where(lane_s < shift, row, 0.0)
        for t in range(nc // LANES):
            there = jnp.where(tile == t, near, jnp.where(tile == t - 1, far, 0.0))
            high = there.astype(BF16)
            spread_out[v, 0:STEPS * slots, t * LANES:(t + 1) * LANES] = high
            spread_out[v, STEPS * slots:, t * LANES:(t + 1) * LANES] = (there - high.astype(F32)).astype(BF16)
    for step in range(STEPS):
        horiz = (owner_ref[step:step + 1] == region).astype(F32)
        listed = (locr_ref[step] == region).astype(F32)
        horiz = horiz + jnp.sum(locw_ref[step] * listed, axis=0, keepdims=True)
        for l in range(nl):
            meta_in[l:l + 1] = var_ref[step, pl.ds(level * nl + l, 1)]
            meta_in[nl + l:nl + l + 1] = obs_ref[step, pl.ds(level * nl + l, 1)]
        meta_in[2 * nl:2 * nl + 1] = horiz
        order = (places[step] == sub.astype(F32)).astype(F32)
        meta_ref[step] = lax.dot_general(meta_in[...], order, BY_LANES, precision=HIGHEST, preferred_element_type=F32)
    total = None
    for v in range(nv):
        copies[v].wait()
        prior = jnp.concatenate([held[v, l] for l in range(nl)], axis=0)
        high = prior.astype(BF16)
        left = jnp.concatenate([high, (prior - high.astype(F32)).astype(BF16)], axis=0)
        term = lax.dot_general(left, spread_out[v], BY_LANES, preferred_element_type=F32)
        total = term if total is None else total + term
    result = total[:nl * nm] + total[nl * nm:]
    result = result + turn(result, -STEPS * slots)
    groups = nl * nm // SUB
    packed = -(-groups // regions)
    lane8 = lane[:SUB]
    for step in range(STEPS):
        parts = [jnp.zeros((SUB, LANES), F32) for _ in range(packed)]
        for g in range(groups):
            j, k = g // regions, g % regions
            here = (lane8 >= slots * k) & (lane8 < slots * (k + 1))
            parts[j] = jnp.where(here, turn(result[g * SUB:(g + 1) * SUB], slots * (k - step)), parts[j])
        for j in range(packed):
            if step == 0:
                for d in range(msg_ref.shape[0]):
                    msg_ref[d, j * SUB:(j + 1) * SUB] = parts[j]
            else:
                later_ref[j * SUB:(j + 1) * SUB] = parts[j]


def skew(x, by, sign):
    x = turn(x, by)
    sub8 = iota((SUB, LANES), 0)
    for bit in range(3):
        x = jnp.where((sub8 >> bit) % 2 == 1, turn(x, sign << bit), x)
    return x


def pack_mixing(s, w):
    nm = s.shape[0]
    width, across = nm + 2, LANES // (nm + 2)
    lane8 = iota((SUB, LANES), 1)
    pieces = []
    for g in range(nm // SUB):
        at = width * (g % across)
        part = skew(s[g * SUB:(g + 1) * SUB], at - g * SUB, -1)
        part = jnp.where((lane8 >= at) & (lane8 <= at + nm), part, 0.0)
        part = jnp.where(lane8 == at + nm + 1, w[g * SUB:(g + 1) * SUB], part)
        if g % across:
            pieces[-1] = pieces[-1] + part
        else:
            pieces.append(part)
    return jnp.concatenate(pieces, axis=0)


def unpack_mixing(p, nm):
    width, across = nm + 2, LANES // (nm + 2)
    lane8 = iota((SUB, LANES), 1)
    band, w = [], []
    for g in range(nm // SUB):
        at, j = width * (g % across), g // across
        part = p[j * SUB:(j + 1) * SUB]
        band.append(skew(jnp.where((lane8 >= at) & (lane8 <= at + nm), part, 0.0), g * SUB - at, 1))
        w.append(part[:, at + nm + 1:at + nm + 2])
    return jnp.concatenate(band, axis=0), jnp.concatenate(w, axis=0)


def mixing_rows(first, second, nm):
    (band, w), (band_2, w_2) = first, second
    lane = iota((nm, LANES), 1)
    sub = iota((nm, LANES), 0)
    top = jnp.where((lane > sub) & (lane < nm), band, 0.0)
    low = jnp.where(lane < sub, turn(band_2, -nm), 0.0)
    top = jnp.where(lane == nm, w, top)
    low = jnp.where(lane == nm, w_2, low)
    rest = jnp.zeros((LANES - 2 * nm, LANES), F32)
    turned = jnp.concatenate([top, low, rest], axis=0).T
    return turned[nm:nm + 1] - (band + turned[:nm])


def local_kernel(step, nl, nm, regions, slots, levels, level_count, cores,
                 got_ref, meta_ref, *refs):
    level = lax.axis_index("level")
    member = lax.axis_index("member")
    members = nm * cores
    scale = levels / 4.0
    lane8 = iota((SUB, LANES), 1)
    fetches = []
    if step == 0:
        later_hbm, msg_ref, local_ref, meta_out, later_ref, spread_ref, sem = refs
        fetches = [pltpu.make_async_copy(meta_ref, meta_out, sem.at[0]), pltpu.make_async_copy(later_hbm, later_ref, sem.at[1])]
        meta_ref = meta_out
    else:
        msg_ref, local_ref, spread_ref = refs
    for copy in fetches:
        copy.start()
    all_spread = []
    for l in range(nl):
        rows = []
        for c in (member, 1 - member):
            for r in range(nm // SUB):
                g = l * (nm // SUB) + r
                j, k = g // regions, g % regions
                row = None
                for p in range(regions):
                    part = turn(got_ref[p * cores + c, j * SUB:(j + 1) * SUB], slots * (p - k))
                    row = part if row is None else jnp.where(lane8 >= slots * p, part, row)
                rows.append(row)
        predicted = jnp.concatenate(rows, axis=0)
        mean = jnp.sum(predicted, axis=0, keepdims=True) * (1.0 / members)
        spread = predicted - mean
        variance = jnp.sum(spread * spread, axis=0, keepdims=True) * (1.0 / (members - 1.0))
        all_spread.append((mean, spread, variance))
    for copy in fetches:
        copy.wait()
    mats = []
    for l, (mean, spread, variance) in enumerate(all_spread):
        obs_var = meta_ref[step, l:l + 1]
        obs_value = meta_ref[step, nl + l:nl + l + 1]
        horiz = meta_ref[step, 2 * nl:2 * nl + 1]
        total_var = variance + obs_var
        gain = (obs_value - mean) / total_var
        shrink = 1.0 / (1.0 + jnp.sqrt(obs_var / total_var))
        scaled = horiz * (1.0 / (members - 1.0))
        spread_ref[l, 0:members] = spread
        spread_ref[l, members:] = jnp.zeros((LANES - members, LANES), F32)
        own = spread[:nm]
        left = scaled * (shrink / total_var) * own
        s = lax.dot_general(left, spread_ref[l], BY_LANES, precision=HIGHEST, preferred_element_type=F32)
        mats.append(pack_mixing(s, jnp.sum(scaled * gain * own, axis=1, keepdims=True)))
    up = sum(math.exp(-(nl - 1 - l) / scale) * mats[l] for l in range(nl))
    down = sum(math.exp(-l / scale) * mats[l] for l in range(nl))
    for l in range(nl):
        local_ref[l] = sum(math.exp(-abs(l - k) / scale) * mats[k] for k in range(nl))
    for d in range(level_count):
        msg_ref[d] = jnp.where(d > level, up, down)


def combine_kernel(nl, levels, level_count, got_ref, local_ref, *refs):
    out_ref = refs[-1]
    level = lax.axis_index("level")
    scale = levels / 4.0
    fade = math.exp(-nl / scale)
    rows = got_ref.shape[1]
    zero = jnp.zeros(got_ref.shape[1:], F32)
    below = lax.fori_loop(0, level, lambda d, acc: acc * fade + got_ref[d], zero)
    above = lax.fori_loop(0, level_count - 1 - level, lambda d, acc: acc * fade + got_ref[level_count - 1 - d], zero)
    for l in range(nl):
        out_ref[l * rows:(l + 1) * rows] = (
            math.exp(-(l + 1) / scale) * below + math.exp(-(nl - l) / scale) * above + local_ref[l]
        )
    if len(refs) > 1:
        out_ref[nl * rows:] = refs[0][...]


def forecast_kernel(nl, nm, regions, slots, own_ref, other_ref, mix_ref, msg_ref, full_ref):
    lane8 = iota((SUB, LANES), 1)
    lane = iota((nm, LANES), 1)
    groups = nl * nm // SUB
    packed = -(-groups // regions)
    first = own_ref.shape[0] - packed * SUB
    rows = first // nl
    parts = [jnp.zeros((SUB, LANES), F32) for _ in range(packed)]
    for l in range(nl):
        pieces = []
        for ref in (own_ref, other_ref):
            for r in range(nm // SUB):
                g = l * (nm // SUB) + r
                j, k = g // regions, g % regions
                pieces.append(turn(ref[first + j * SUB:first + (j + 1) * SUB], -slots * k))
        own = jnp.concatenate(pieces[:nm // SUB], axis=0)
        pieces.append(jnp.zeros((LANES - 2 * nm, LANES), F32))
        full_ref[l] = jnp.concatenate(pieces, axis=0)
        bands = [unpack_mixing(ref[l * rows:(l + 1) * rows], nm) for ref in (own_ref, other_ref)]
        upper = mixing_rows(bands[0], bands[1], nm)
        mix_ref[l, 0:nm] = upper
        result = own + dot(upper, full_ref[l])
        for r in range(nm // SUB):
            g = l * (nm // SUB) + r
            j, k = g // regions, g % regions
            keep = (lane8 >= slots * k) & (lane8 < slots * (k + 1))
            parts[j] = jnp.where(keep, turn(result[r * SUB:(r + 1) * SUB], slots * k), parts[j])
        lower = mixing_rows(bands[1], bands[0], nm)
        swapped = jnp.where(lane < nm, turn(lower, -nm), jnp.where(lane < 2 * nm, turn(lower, nm), 0.0))
        mix_ref[l, nm:2 * nm] = swapped
        mix_ref[l, 2 * nm:] = jnp.zeros((LANES - 2 * nm, LANES), F32)
    for d in range(msg_ref.shape[0]):
        for j in range(packed):
            msg_ref[d, j * SUB:(j + 1) * SUB] = parts[j]


def split(x):
    high = x.astype(BF16).astype(F32)
    return high, x - high


def update_kernel(nl, nm, own_ref, other_ref, mix_ref, state_ref, theirs_ref, out_hbm,
                  out_v, left_ref, out_sem):
    nv = state_ref.shape[0]
    members = 2 * nm
    blocks = [(v, l) for l in range(nl) for v in range(nv)]
    rows = own_ref.shape[0] // nl
    lane = iota((nm, LANES), 1)
    for l in range(nl):
        bands = [unpack_mixing(ref[l * rows:(l + 1) * rows], nm) for ref in (own_ref, other_ref)]
        second = mixing_rows(bands[0], bands[1], nm)
        both = second + mix_ref[l, 0:nm] + dot(second, mix_ref[l])
        high, low = split(both)
        again = turn(high, members)
        left_ref[l, :, 0:LANES] = high + jnp.where(lane >= members, again, 0.0)
        left_ref[l, :, LANES:] = jnp.where(lane < 2 * members - LANES, again, 0.0) + turn(low, 2 * members - LANES)
    pad = jnp.zeros((2 * LANES - 3 * members, state_ref.shape[3]), F32)
    stores = []
    for i, (v, l) in enumerate(blocks):
        own = state_ref[v, l]
        high, low = split(jnp.concatenate([own, theirs_ref[v, l]], axis=0))
        right = jnp.concatenate([high, low, high, pad], axis=0).astype(BF16)
        out_v[v, l] = own + jnp.dot(left_ref[l].astype(BF16), right, preferred_element_type=F32)
        copy = pltpu.make_async_copy(out_v.at[v, l], out_hbm.at[v, l], out_sem.at[i])
        copy.start()
        stores.append(copy)
    for copy in stores:
        copy.wait()


def body(state, ray_cols, ray_len, ray_weight, owner, loc_regions, loc_weight, obs_value, obs_var):
    regions = lax.axis_size("region")
    level_count = lax.axis_size("level")
    cores = lax.axis_size("member")
    nv, nl, nm, nc = state.shape
    occ, rays = ray_cols.shape[1:]
    slots = occ // regions
    levels = nl * level_count
    assert occ == LANES and regions * slots == LANES and nm % SUB == 0 and cores == 2
    assert LANES % rays == 0 and 2 * STEPS * slots == LANES
    groups = nl * nm // SUB
    block = (-(-groups // regions) * SUB, LANES)
    mixing = (-(-(nm // SUB) // (LANES // (nm + 2))) * SUB, LANES)
    whole = pl.BlockSpec(memory_space=VMEM)
    outside = pl.BlockSpec(memory_space=pltpu.HBM)
    swap = [(0, 1), (1, 0)]
    dma = pltpu.SemaphoreType.DMA

    def call(kernel, statics, outs, scratch, *args, specs=None, out_specs=None, name=None, limit=32):
        def wrapped(*refs):
            return kernel(*statics, *refs)
        return pl.pallas_call(
            wrapped,
            out_shape=[jax.ShapeDtypeStruct(s, F32) for s in outs],
            in_specs=specs or [whole] * len(args),
            out_specs=out_specs or [whole] * len(outs),
            scratch_shapes=scratch,
            compiler_params=pltpu.CompilerParams(vmem_limit_bytes=limit * 2**20),
            name=name,
        )(*args)

    other_state = lax.ppermute(state, "member", swap)
    given = [ray_cols.swapaxes(1, 2), ray_len, ray_weight.transpose(0, 2, 3, 1), owner, loc_regions.swapaxes(1, 2),
             loc_weight.swapaxes(1, 2), obs_value.swapaxes(1, 2), obs_var.swapaxes(1, 2)]
    msg, later, meta = call(
        predict_kernel, (nl, nm, nc, regions, slots, rays),
        [(regions * cores,) + block, block, (STEPS, SUB, LANES)],
        [VMEM(state.shape, F32)] + [VMEM(a.shape, a.dtype) for a in given]
        + [VMEM((-(-nv * rays // LANES) * LANES, STEPS * LANES), F32), VMEM((nv * rays, STEPS * LANES), F32),
           VMEM((nv, 2 * STEPS * slots, nc), BF16), VMEM((SUB, LANES), F32), dma((nv,)), dma((len(given),))],
        state, *given, specs=[outside] * (1 + len(given)), name="predict", limit=60,
    )

    def assimilate(step, msg, meta, later=None):
        got = lax.all_to_all(msg, ("region", "member"), 0, 0, tiled=True)
        statics = (step, nl, nm, regions, slots, levels, level_count, cores)
        outs, scratch = [(level_count,) + mixing, (nl,) + mixing], [VMEM((nl, LANES, LANES), F32)]
        if later is None:
            out, local = call(local_kernel, statics, outs, scratch, got, meta, name="local")
            more = []
        else:
            out, local, meta, later = call(
                local_kernel, statics, outs + [meta.shape, later.shape], scratch + [dma((2,))],
                got, meta, later, specs=[whole] + [outside] * 2, name="local",
            )
            more = [later]
        got = lax.all_to_all(out, "level", 0, 0, tiled=True)
        rows = nl * mixing[0] + sum(a.shape[0] for a in more)
        own, = call(combine_kernel, (nl, levels, level_count), [(rows, LANES)], [], got, local, *more, name="combine")
        return own, lax.ppermute(own, "member", swap), meta

    own, other, meta = assimilate(0, msg, meta, later)
    mix, msg = call(
        forecast_kernel, (nl, nm, regions, slots),
        [(nl, LANES, LANES), (regions * cores,) + block], [VMEM((nl, LANES, LANES), F32)],
        own, other, name="forecast",
    )
    own, other, _ = assimilate(1, msg, meta)
    out, = call(
        update_kernel, (nl, nm), [state.shape],
        [VMEM(state.shape, F32), VMEM((nl, nm, 2 * LANES), F32), dma((nv * nl,))],
        own, other, mix, state, other_state, out_specs=[outside], name="update",
    )
    return out


def solution(mesh):
    in_specs = (P(None, "level", "member", "region"), P(), P(), P(), P(), P(), P(), P(), P())
    out_specs = P(None, "level", "member", "region")
    return jax.shard_map(body, mesh=mesh, in_specs=in_specs, out_specs=out_specs, check_vma=False)
```

```python
import math

import jax
import jax.numpy as jnp
from jax import lax
from jax.experimental import pallas as pl
from jax.experimental.pallas import tpu as pltpu
from jax.sharding import PartitionSpec as P

STEPS = 2
LANES = 128
SUB = 8
HIGHEST = lax.Precision.HIGHEST
F32 = jnp.float32
BF16 = jnp.bfloat16
VMEM = pltpu.VMEM
BY_LANES = (((1,), (1,)), ((), ()))


def iota(shape, dim):
    return lax.broadcasted_iota(jnp.int32, shape, dim)


def dot(a, b):
    return jnp.dot(a, b, precision=HIGHEST, preferred_element_type=F32)


def turn(x, by):
    by = by % LANES
    return pltpu.roll(x, by, 1) if by else x


def pick(chosen, values):
    chosen = chosen.astype(BF16)
    total = None
    for _ in range(3):
        part = values.astype(BF16)
        term = lax.dot_general(chosen, part, BY_LANES, preferred_element_type=F32)
        total = term if total is None else total + term
        values = values - part.astype(F32)
    return total


def predict_kernel(nl, nm, nc, regions, slots, rays,
                   state_hbm, cols_hbm, len_hbm, weight_hbm, owner_hbm, locr_hbm, locw_hbm, obs_hbm, var_hbm,
                   msg_ref, later_ref, meta_ref,
                   held, cols_ref, len_ref, weight_ref, owner_ref, locr_ref, locw_ref, obs_ref, var_ref,
                   masked, sorted_ref, spread_out, meta_in, state_sem, arg_sem):
    nv = state_hbm.shape[0]
    region = lax.axis_index("region")
    level = lax.axis_index("level")
    pairs = [(cols_hbm, cols_ref), (len_hbm, len_ref), (weight_hbm, weight_ref), (owner_hbm, owner_ref),
             (locr_hbm, locr_ref), (locw_hbm, locw_ref), (obs_hbm, obs_ref), (var_hbm, var_ref)]
    fetches = [pltpu.make_async_copy(a, b, arg_sem.at[i]) for i, (a, b) in enumerate(pairs)]
    for copy in fetches:
        copy.start()
    copies = [pltpu.make_async_copy(state_hbm.at[v], held.at[v], state_sem.at[v]) for v in range(nv)]
    for copy in copies:
        copy.start()
    lane = iota((LANES, LANES), 1)
    sub = iota((LANES, LANES), 0)
    sub8 = iota((SUB, LANES), 0)
    earlier = (sub < lane).astype(BF16)
    region_f = region.astype(F32)
    masked[nv * rays:] = jnp.zeros((masked.shape[0] - nv * rays, STEPS * LANES), F32)
    meta_in[...] = jnp.zeros_like(meta_in)
    for copy in fetches:
        copy.wait()
    firsts, places, worst = [], [], None
    for step in range(STEPS):
        cols = cols_ref[step].astype(F32)
        first = jnp.min(cols, axis=0, keepdims=True)
        off = jnp.max(jnp.abs(cols - first - sub[:rays].astype(F32)))
        worst = off if worst is None else jnp.maximum(worst, off)
        home = jnp.zeros_like(first)
        for q in range(1, regions):
            home = home + (first >= float(q * nc)).astype(F32)
        at_home = (sub8.astype(F32) == home).astype(F32)
        count = jnp.dot(at_home.astype(BF16), earlier, preferred_element_type=F32)
        rank = jnp.sum(at_home * count, axis=0, keepdims=True)
        ahead = region_f - home
        ahead = jnp.where(ahead < 0.0, ahead + float(regions), ahead)
        places.append(ahead * float(slots) + rank)
        firsts.append(first)
        live = sub[:rays] < len_ref[step:step + 1]
        for v in range(nv):
            masked[v * rays:(v + 1) * rays, step * LANES:(step + 1) * LANES] = jnp.where(live, weight_ref[step, v], 0.0)
    slot = sub[:STEPS * slots].astype(F32)
    mine = []
    for step in range(STEPS):
        ours = (slot >= float(step * slots)) & (slot < float((step + 1) * slots))
        mine.append(((places[step] == slot - float(step * slots)) & ours).astype(F32))
    mine = jnp.concatenate(mine, axis=1)

    @pl.when(worst > 0.5)
    def _():
        column = jnp.concatenate([cols_ref[s].astype(F32) - firsts[s] for s in range(STEPS)], axis=1)

        def one(d, carry):
            hit = column == d.astype(F32)
            for v in range(nv):
                weights = masked[v * rays:(v + 1) * rays]
                sorted_ref[pl.ds(v * rays + d, 1)] = jnp.sum(jnp.where(hit, weights, 0.0), axis=0, keepdims=True)
            return carry
        lax.fori_loop(0, rays, one, 0)
        masked[0:nv * rays] = sorted_ref[...]

    first = jnp.broadcast_to(jnp.concatenate(firsts, axis=1), (LANES, STEPS * LANES))
    low = pick(mine, first).astype(jnp.int32) - region * nc
    tile, shift = low >> 7, low & (LANES - 1)
    picked = pick(mine, masked[...])
    lane_s = lane[:STEPS * slots]
    for v in range(nv):
        at = v * rays
        row = picked[:, at // LANES * LANES:(at // LANES + 1) * LANES]
        at = at % LANES
        row = turn(jnp.where((lane_s >= at) & (lane_s < at + rays), row, 0.0), -at)
        for bit in range(7):
            row = jnp.where((shift >> bit) % 2 == 1, turn(row, 1 << bit), row)
        near, far = jnp.where(lane_s >= shift, row, 0.0), jnp.where(lane_s < shift, row, 0.0)
        for t in range(nc // LANES):
            there = jnp.where(tile == t, near, jnp.where(tile == t - 1, far, 0.0))
            high = there.astype(BF16)
            spread_out[v, 0:STEPS * slots, t * LANES:(t + 1) * LANES] = high
            spread_out[v, STEPS * slots:, t * LANES:(t + 1) * LANES] = (there - high.astype(F32)).astype(BF16)
    for step in range(STEPS):
        horiz = (owner_ref[step:step + 1] == region).astype(F32)
        listed = (locr_ref[step] == region).astype(F32)
        horiz = horiz + jnp.sum(locw_ref[step] * listed, axis=0, keepdims=True)
        for l in range(nl):
            meta_in[l:l + 1] = var_ref[step, pl.ds(level * nl + l, 1)]
            meta_in[nl + l:nl + l + 1] = obs_ref[step, pl.ds(level * nl + l, 1)]
        meta_in[2 * nl:2 * nl + 1] = horiz
        order = (places[step] == sub.astype(F32)).astype(F32)
        meta_ref[step] = lax.dot_general(meta_in[...], order, BY_LANES, precision=HIGHEST, preferred_element_type=F32)
    total = None
    for v in range(nv):
        copies[v].wait()
        prior = jnp.concatenate([held[v, l] for l in range(nl)], axis=0)
        high = prior.astype(BF16)
        left = jnp.concatenate([high, (prior - high.astype(F32)).astype(BF16)], axis=0)
        term = lax.dot_general(left, spread_out[v], BY_LANES, preferred_element_type=F32)
        total = term if total is None else total + term
    result = total[:nl * nm] + total[nl * nm:]
    result = result + turn(result, -STEPS * slots)
    groups = nl * nm // SUB
    packed = -(-groups // regions)
    lane8 = lane[:SUB]
    for step in range(STEPS):
        parts = [jnp.zeros((SUB, LANES), F32) for _ in range(packed)]
        for g in range(groups):
            j, k = g // regions, g % regions
            here = (lane8 >= slots * k) & (lane8 < slots * (k + 1))
            parts[j] = jnp.where(here, turn(result[g * SUB:(g + 1) * SUB], slots * (k - step)), parts[j])
        for j in range(packed):
            if step == 0:
                for d in range(msg_ref.shape[0]):
                    msg_ref[d, j * SUB:(j + 1) * SUB] = parts[j]
            else:
                later_ref[j * SUB:(j + 1) * SUB] = parts[j]


def skew(x, by, sign):
    x = turn(x, by)
    sub8 = iota((SUB, LANES), 0)
    for bit in range(3):
        x = jnp.where((sub8 >> bit) % 2 == 1, turn(x, sign << bit), x)
    return x


def pack_mixing(s, w):
    nm = s.shape[0]
    width, across = nm + 2, LANES // (nm + 2)
    lane8 = iota((SUB, LANES), 1)
    pieces = []
    for g in range(nm // SUB):
        at = width * (g % across)
        part = skew(s[g * SUB:(g + 1) * SUB], at - g * SUB, -1)
        part = jnp.where((lane8 >= at) & (lane8 <= at + nm), part, 0.0)
        part = jnp.where(lane8 == at + nm + 1, w[g * SUB:(g + 1) * SUB], part)
        if g % across:
            pieces[-1] = pieces[-1] + part
        else:
            pieces.append(part)
    return jnp.concatenate(pieces, axis=0)


def unpack_mixing(p, nm):
    width, across = nm + 2, LANES // (nm + 2)
    lane8 = iota((SUB, LANES), 1)
    band, w = [], []
    for g in range(nm // SUB):
        at, j = width * (g % across), g // across
        part = p[j * SUB:(j + 1) * SUB]
        band.append(skew(jnp.where((lane8 >= at) & (lane8 <= at + nm), part, 0.0), g * SUB - at, 1))
        w.append(part[:, at + nm + 1:at + nm + 2])
    return jnp.concatenate(band, axis=0), jnp.concatenate(w, axis=0)


def mixing_rows(first, second, nm):
    (band, w), (band_2, w_2) = first, second
    lane = iota((nm, LANES), 1)
    sub = iota((nm, LANES), 0)
    top = jnp.where((lane > sub) & (lane < nm), band, 0.0)
    low = jnp.where(lane < sub, turn(band_2, -nm), 0.0)
    top = jnp.where(lane == nm, w, top)
    low = jnp.where(lane == nm, w_2, low)
    rest = jnp.zeros((LANES - 2 * nm, LANES), F32)
    turned = jnp.concatenate([top, low, rest], axis=0).T
    return turned[nm:nm + 1] - (band + turned[:nm])


def local_kernel(step, nl, nm, regions, slots, levels, level_count, cores, *refs):
    *got, meta_ref, msg_ref, local_ref, spread_ref = refs
    region = lax.axis_index("region")
    level = lax.axis_index("level")
    member = lax.axis_index("member")
    members = nm * cores
    scale = levels / 4.0
    lane8 = iota((SUB, LANES), 1)
    packed = -(-(nl * nm // SUB) // regions)
    all_spread = []
    for l in range(nl):
        rows = []
        for half, c in enumerate((member, 1 - member)):
            for r in range(nm // SUB):
                g = l * (nm // SUB) + r
                j, k = g // regions, g % regions
                row = None
                for s in range(regions):
                    if len(got) == 1:
                        source = jnp.where(region >= s, region - s, region - s + regions)
                        part = got[0][source * cores + c, j * SUB:(j + 1) * SUB]
                    else:
                        part = got[s][(half * packed + j) * SUB:(half * packed + j + 1) * SUB]
                    part = turn(part, slots * (s - k))
                    row = part if row is None else jnp.where(lane8 >= slots * s, part, row)
                rows.append(row)
        predicted = jnp.concatenate(rows, axis=0)
        mean = jnp.sum(predicted, axis=0, keepdims=True) * (1.0 / members)
        spread = predicted - mean
        variance = jnp.sum(spread * spread, axis=0, keepdims=True) * (1.0 / (members - 1.0))
        all_spread.append((mean, spread, variance))
    mats = []
    for l, (mean, spread, variance) in enumerate(all_spread):
        obs_var = meta_ref[step, l:l + 1]
        obs_value = meta_ref[step, nl + l:nl + l + 1]
        horiz = meta_ref[step, 2 * nl:2 * nl + 1]
        total_var = variance + obs_var
        gain = (obs_value - mean) / total_var
        shrink = 1.0 / (1.0 + jnp.sqrt(obs_var / total_var))
        scaled = horiz * (1.0 / (members - 1.0))
        spread_ref[l, 0:members] = spread
        spread_ref[l, members:] = jnp.zeros((LANES - members, LANES), F32)
        own = spread[:nm]
        left = scaled * (shrink / total_var) * own
        s = lax.dot_general(left, spread_ref[l], BY_LANES, precision=HIGHEST, preferred_element_type=F32)
        mats.append(pack_mixing(s, jnp.sum(scaled * gain * own, axis=1, keepdims=True)))
    up = sum(math.exp(-(nl - 1 - l) / scale) * mats[l] for l in range(nl))
    down = sum(math.exp(-l / scale) * mats[l] for l in range(nl))
    for l in range(nl):
        local_ref[l] = sum(math.exp(-abs(l - k) / scale) * mats[k] for k in range(nl))
    for d in range(level_count):
        msg_ref[d] = jnp.where(d > level, up, down)


def combine_kernel(nl, levels, level_count, got_ref, local_ref, *refs):
    out_ref = refs[-1]
    level = lax.axis_index("level")
    scale = levels / 4.0
    fade = math.exp(-nl / scale)
    rows = got_ref.shape[1]
    zero = jnp.zeros(got_ref.shape[1:], F32)
    below = lax.fori_loop(0, level, lambda d, acc: acc * fade + got_ref[d], zero)
    above = lax.fori_loop(0, level_count - 1 - level, lambda d, acc: acc * fade + got_ref[level_count - 1 - d], zero)
    for l in range(nl):
        out_ref[l * rows:(l + 1) * rows] = (
            math.exp(-(l + 1) / scale) * below + math.exp(-(nl - l) / scale) * above + local_ref[l]
        )
    if len(refs) > 1:
        out_ref[nl * rows:] = refs[0][...]


def forecast_kernel(nl, nm, regions, slots, own_ref, other_ref, mix_ref, msg_ref, full_ref):
    lane8 = iota((SUB, LANES), 1)
    lane = iota((nm, LANES), 1)
    per = nm // SUB
    packed = -(-nl * per // regions)
    first = own_ref.shape[0] - packed * SUB
    rows = first // nl
    parts = [jnp.zeros((SUB, LANES), F32) for _ in range(2 * packed)]
    rest = jnp.zeros((LANES - 2 * nm, LANES), F32)
    for l in range(nl):
        pieces = []
        for ref in (own_ref, other_ref):
            for r in range(per):
                j, k = (l * per + r) // regions, (l * per + r) % regions
                pieces.append(turn(ref[first + j * SUB:first + (j + 1) * SUB], -slots * k))
        prior = jnp.concatenate(pieces + [rest], axis=0)
        full_ref[l] = prior
        bands = [unpack_mixing(ref[l * rows:(l + 1) * rows], nm) for ref in (own_ref, other_ref)]
        lower = mixing_rows(bands[1], bands[0], nm)
        swapped = jnp.where(lane < nm, turn(lower, -nm), jnp.where(lane < 2 * nm, turn(lower, nm), 0.0))
        mix_ref[l] = jnp.concatenate([mixing_rows(bands[0], bands[1], nm), swapped, rest], axis=0)
        result = prior + dot(mix_ref[l], full_ref[l])
        for half in range(2):
            for r in range(per):
                j, k = (l * per + r) // regions, (l * per + r) % regions
                keep = (lane8 >= slots * k) & (lane8 < slots * (k + 1))
                at = half * per + r
                j += half * packed
                parts[j] = jnp.where(keep, turn(result[at * SUB:(at + 1) * SUB], slots * k), parts[j])
    msg_ref[...] = jnp.concatenate(parts, axis=0)


def split(x):
    high = x.astype(BF16).astype(F32)
    return high, x - high


def update_kernel(nl, nm, own_ref, other_ref, mix_ref, state_ref, theirs_ref, out_hbm,
                  out_v, left_ref, out_sem):
    nv = state_ref.shape[0]
    members = 2 * nm
    blocks = [(v, l) for l in range(nl) for v in range(nv)]
    rows = own_ref.shape[0] // nl
    lane = iota((nm, LANES), 1)
    for l in range(nl):
        bands = [unpack_mixing(ref[l * rows:(l + 1) * rows], nm) for ref in (own_ref, other_ref)]
        second = mixing_rows(bands[0], bands[1], nm)
        both = second + mix_ref[l, 0:nm] + dot(second, mix_ref[l])
        high, low = split(both)
        again = turn(high, members)
        left_ref[l, :, 0:LANES] = high + jnp.where(lane >= members, again, 0.0)
        left_ref[l, :, LANES:] = jnp.where(lane < 2 * members - LANES, again, 0.0) + turn(low, 2 * members - LANES)
    pad = jnp.zeros((2 * LANES - 3 * members, state_ref.shape[3]), F32)
    stores = []
    for i, (v, l) in enumerate(blocks):
        own = state_ref[v, l]
        high, low = split(jnp.concatenate([own, theirs_ref[v, l]], axis=0))
        right = jnp.concatenate([high, low, high, pad], axis=0).astype(BF16)
        out_v[v, l] = own + jnp.dot(left_ref[l].astype(BF16), right, preferred_element_type=F32)
        copy = pltpu.make_async_copy(out_v.at[v, l], out_hbm.at[v, l], out_sem.at[i])
        copy.start()
        stores.append(copy)
    for copy in stores:
        copy.wait()


def body(state, ray_cols, ray_len, ray_weight, owner, loc_regions, loc_weight, obs_value, obs_var):
    regions = lax.axis_size("region")
    level_count = lax.axis_size("level")
    cores = lax.axis_size("member")
    nv, nl, nm, nc = state.shape
    occ, rays = ray_cols.shape[1:]
    slots = occ // regions
    levels = nl * level_count
    assert occ == LANES and regions * slots == LANES and nm % SUB == 0 and cores == 2
    assert LANES % rays == 0 and 2 * STEPS * slots == LANES
    groups = nl * nm // SUB
    block = (-(-groups // regions) * SUB, LANES)
    mixing = (-(-(nm // SUB) // (LANES // (nm + 2))) * SUB, LANES)
    whole = pl.BlockSpec(memory_space=VMEM)
    outside = pl.BlockSpec(memory_space=pltpu.HBM)
    swap = [(0, 1), (1, 0)]
    dma = pltpu.SemaphoreType.DMA

    def call(kernel, statics, outs, scratch, *args, specs=None, out_specs=None, name=None, limit=32,
             kind=jax.ShapeDtypeStruct):
        def wrapped(*refs):
            return kernel(*statics, *refs)
        return pl.pallas_call(
            wrapped,
            out_shape=[kind(s, F32) for s in outs],
            in_specs=specs or [whole] * len(args),
            out_specs=out_specs or [whole] * len(outs),
            scratch_shapes=scratch,
            compiler_params=pltpu.CompilerParams(vmem_limit_bytes=limit * 2**20),
            name=name,
        )(*args)

    other_state = lax.ppermute(state, "member", swap)
    given = [ray_cols.swapaxes(1, 2), ray_len, ray_weight.transpose(0, 2, 3, 1), owner, loc_regions.swapaxes(1, 2),
             loc_weight.swapaxes(1, 2), obs_value.swapaxes(1, 2), obs_var.swapaxes(1, 2)]
    msg, later, meta = call(
        predict_kernel, (nl, nm, nc, regions, slots, rays),
        [(regions * cores,) + block, block, (STEPS, SUB, LANES)],
        [VMEM(state.shape, F32)] + [VMEM(a.shape, a.dtype) for a in given]
        + [VMEM((-(-nv * rays // LANES) * LANES, STEPS * LANES), F32), VMEM((nv * rays, STEPS * LANES), F32),
           VMEM((nv, 2 * STEPS * slots, nc), BF16), VMEM((SUB, LANES), F32), dma((nv,)), dma((len(given),))],
        state, *given, specs=[outside] * (1 + len(given)), name="predict", limit=60, kind=VMEM,
    )

    def assimilate(step, got, *more):
        out, local = call(
            local_kernel, (step, nl, nm, regions, slots, levels, level_count, cores),
            [(level_count,) + mixing, (nl,) + mixing], [VMEM((nl, LANES, LANES), F32)],
            *got, meta, name="local",
        )
        got = lax.all_to_all(out, "level", 0, 0, tiled=True)
        rows = nl * mixing[0] + sum(a.shape[0] for a in more)
        own, = call(combine_kernel, (nl, levels, level_count), [(rows, LANES)], [], got, local, *more, name="combine")
        return own, lax.ppermute(own, "member", swap)

    own, other = assimilate(0, [lax.all_to_all(msg, ("region", "member"), 0, 0, tiled=True)], later)
    mix, msg = call(
        forecast_kernel, (nl, nm, regions, slots),
        [(nl, LANES, LANES), (2 * block[0], LANES)], [VMEM((nl, LANES, LANES), F32)],
        own, other, name="forecast",
    )
    rings = [[(i, (i + s) % regions) for i in range(regions)] for s in range(1, regions)]
    own, other = assimilate(1, [msg] + [lax.ppermute(msg, "region", ring) for ring in rings])
    out, = call(
        update_kernel, (nl, nm), [state.shape],
        [VMEM(state.shape, F32), VMEM((nl, nm, 2 * LANES), F32), dma((nv * nl,))],
        own, other, mix, state, other_state, out_specs=[outside], name="update",
    )
    return out


def solution(mesh):
    in_specs = (P(None, "level", "member", "region"), P(), P(), P(), P(), P(), P(), P(), P())
    out_specs = P(None, "level", "member", "region")
    return jax.shard_map(body, mesh=mesh, in_specs=in_specs, out_specs=out_specs, check_vma=False)
```

```python
import math

import jax
import jax.numpy as jnp
from jax import lax
from jax.experimental import pallas as pl
from jax.experimental.pallas import tpu as pltpu
from jax.sharding import PartitionSpec as P

STEPS = 2
LANES = 128
SUB = 8
HIGHEST = lax.Precision.HIGHEST
F32 = jnp.float32
BF16 = jnp.bfloat16
VMEM = pltpu.VMEM
BY_LANES = (((1,), (1,)), ((), ()))


def iota(shape, dim):
    return lax.broadcasted_iota(jnp.int32, shape, dim)


def dot(a, b):
    return jnp.dot(a, b, precision=HIGHEST, preferred_element_type=F32)


def turn(x, by):
    by = by % LANES
    return pltpu.roll(x, by, 1) if by else x


def pick(chosen, values):
    chosen = chosen.astype(BF16)
    total = None
    for _ in range(3):
        part = values.astype(BF16)
        term = lax.dot_general(chosen, part, BY_LANES, preferred_element_type=F32)
        total = term if total is None else total + term
        values = values - part.astype(F32)
    return total


def predict_kernel(nl, nm, nc, regions, slots, rays,
                   state_hbm, cols_hbm, len_hbm, weight_hbm, owner_hbm, locr_hbm, locw_hbm, obs_hbm, var_hbm,
                   msg_ref, later_ref, meta_ref, held,
                   cols_ref, len_ref, weight_ref, owner_ref, locr_ref, locw_ref, obs_ref, var_ref,
                   masked, sorted_ref, spread_out, meta_in, state_sem, arg_sem):
    nv = state_hbm.shape[0]
    region = lax.axis_index("region")
    level = lax.axis_index("level")
    pairs = [(cols_hbm, cols_ref), (len_hbm, len_ref), (weight_hbm, weight_ref), (owner_hbm, owner_ref),
             (locr_hbm, locr_ref), (locw_hbm, locw_ref), (obs_hbm, obs_ref), (var_hbm, var_ref)]
    fetches = [pltpu.make_async_copy(a, b, arg_sem.at[i]) for i, (a, b) in enumerate(pairs)]
    for copy in fetches:
        copy.start()
    copies = [pltpu.make_async_copy(state_hbm.at[v], held.at[v], state_sem.at[v]) for v in range(nv)]
    for copy in copies:
        copy.start()
    lane = iota((LANES, LANES), 1)
    sub = iota((LANES, LANES), 0)
    sub8 = iota((SUB, LANES), 0)
    earlier = (sub < lane).astype(BF16)
    region_f = region.astype(F32)
    masked[nv * rays:] = jnp.zeros((masked.shape[0] - nv * rays, STEPS * LANES), F32)
    meta_in[...] = jnp.zeros_like(meta_in)
    for copy in fetches:
        copy.wait()
    firsts, places, worst = [], [], None
    for step in range(STEPS):
        cols = cols_ref[step].astype(F32)
        first = jnp.min(cols, axis=0, keepdims=True)
        off = jnp.max(jnp.abs(cols - first - sub[:rays].astype(F32)))
        worst = off if worst is None else jnp.maximum(worst, off)
        home = jnp.zeros_like(first)
        for q in range(1, regions):
            home = home + (first >= float(q * nc)).astype(F32)
        at_home = (sub8.astype(F32) == home).astype(F32)
        count = jnp.dot(at_home.astype(BF16), earlier, preferred_element_type=F32)
        rank = jnp.sum(at_home * count, axis=0, keepdims=True)
        ahead = region_f - home
        ahead = jnp.where(ahead < 0.0, ahead + float(regions), ahead)
        places.append(ahead * float(slots) + rank)
        firsts.append(first)
        live = sub[:rays] < len_ref[step:step + 1]
        for v in range(nv):
            masked[v * rays:(v + 1) * rays, step * LANES:(step + 1) * LANES] = jnp.where(live, weight_ref[step, v], 0.0)
    slot = sub[:STEPS * slots].astype(F32)
    mine = []
    for step in range(STEPS):
        ours = (slot >= float(step * slots)) & (slot < float((step + 1) * slots))
        mine.append(((places[step] == slot - float(step * slots)) & ours).astype(F32))
    mine = jnp.concatenate(mine, axis=1)

    @pl.when(worst > 0.5)
    def _():
        column = jnp.concatenate([cols_ref[s].astype(F32) - firsts[s] for s in range(STEPS)], axis=1)

        def one(d, carry):
            hit = column == d.astype(F32)
            for v in range(nv):
                weights = masked[v * rays:(v + 1) * rays]
                sorted_ref[pl.ds(v * rays + d, 1)] = jnp.sum(jnp.where(hit, weights, 0.0), axis=0, keepdims=True)
            return carry
        lax.fori_loop(0, rays, one, 0)
        masked[0:nv * rays] = sorted_ref[...]

    first = jnp.broadcast_to(jnp.concatenate(firsts, axis=1), (LANES, STEPS * LANES))
    low = pick(mine, first).astype(jnp.int32) - region * nc
    tile, shift = low >> 7, low & (LANES - 1)
    picked = pick(mine, masked[...])
    lane_s = lane[:STEPS * slots]
    for v in range(nv):
        at = v * rays
        row = picked[:, at // LANES * LANES:(at // LANES + 1) * LANES]
        at = at % LANES
        row = turn(jnp.where((lane_s >= at) & (lane_s < at + rays), row, 0.0), -at)
        for bit in range(7):
            row = jnp.where((shift >> bit) % 2 == 1, turn(row, 1 << bit), row)
        near, far = jnp.where(lane_s >= shift, row, 0.0), jnp.where(lane_s < shift, row, 0.0)
        for t in range(nc // LANES):
            there = jnp.where(tile == t, near, jnp.where(tile == t - 1, far, 0.0))
            high = there.astype(BF16)
            spread_out[v, 0:STEPS * slots, t * LANES:(t + 1) * LANES] = high
            spread_out[v, STEPS * slots:, t * LANES:(t + 1) * LANES] = (there - high.astype(F32)).astype(BF16)
    for step in range(STEPS):
        horiz = (owner_ref[step:step + 1] == region).astype(F32)
        listed = (locr_ref[step] == region).astype(F32)
        horiz = horiz + jnp.sum(locw_ref[step] * listed, axis=0, keepdims=True)
        for l in range(nl):
            meta_in[l:l + 1] = var_ref[step, pl.ds(level * nl + l, 1)]
            meta_in[nl + l:nl + l + 1] = obs_ref[step, pl.ds(level * nl + l, 1)]
        meta_in[2 * nl:2 * nl + 1] = horiz
        order = (places[step] == sub.astype(F32)).astype(F32)
        meta_ref[step] = lax.dot_general(meta_in[...], order, BY_LANES, precision=HIGHEST, preferred_element_type=F32)
    total = None
    for v in range(nv):
        copies[v].wait()
        prior = jnp.concatenate([held[v, l] for l in range(nl)], axis=0)
        high = prior.astype(BF16)
        left = jnp.concatenate([high, (prior - high.astype(F32)).astype(BF16)], axis=0)
        term = lax.dot_general(left, spread_out[v], BY_LANES, preferred_element_type=F32)
        total = term if total is None else total + term
    result = total[:nl * nm] + total[nl * nm:]
    result = result + turn(result, -STEPS * slots)
    groups = nl * nm // SUB
    packed = -(-groups // regions)
    lane8 = lane[:SUB]
    for step in range(STEPS):
        parts = [jnp.zeros((SUB, LANES), F32) for _ in range(packed)]
        for g in range(groups):
            j, k = g // regions, g % regions
            here = (lane8 >= slots * k) & (lane8 < slots * (k + 1))
            parts[j] = jnp.where(here, turn(result[g * SUB:(g + 1) * SUB], slots * (k - step)), parts[j])
        for j in range(packed):
            if step == 0:
                for d in range(msg_ref.shape[0]):
                    msg_ref[d, j * SUB:(j + 1) * SUB] = parts[j]
            else:
                later_ref[j * SUB:(j + 1) * SUB] = parts[j]


def skew(x, by, sign):
    x = turn(x, by)
    sub8 = iota((SUB, LANES), 0)
    for bit in range(3):
        x = jnp.where((sub8 >> bit) % 2 == 1, turn(x, sign << bit), x)
    return x


def pack_mixing(s, w):
    nm = s.shape[0]
    width, across = nm + 2, LANES // (nm + 2)
    lane8 = iota((SUB, LANES), 1)
    pieces = []
    for g in range(nm // SUB):
        at = width * (g % across)
        part = skew(s[g * SUB:(g + 1) * SUB], at - g * SUB, -1)
        part = jnp.where((lane8 >= at) & (lane8 <= at + nm), part, 0.0)
        part = jnp.where(lane8 == at + nm + 1, w[g * SUB:(g + 1) * SUB], part)
        if g % across:
            pieces[-1] = pieces[-1] + part
        else:
            pieces.append(part)
    return jnp.concatenate(pieces, axis=0)


def unpack_mixing(p, nm):
    width, across = nm + 2, LANES // (nm + 2)
    lane8 = iota((SUB, LANES), 1)
    band, w = [], []
    for g in range(nm // SUB):
        at, j = width * (g % across), g // across
        part = p[j * SUB:(j + 1) * SUB]
        band.append(skew(jnp.where((lane8 >= at) & (lane8 <= at + nm), part, 0.0), g * SUB - at, 1))
        w.append(part[:, at + nm + 1:at + nm + 2])
    return jnp.concatenate(band, axis=0), jnp.concatenate(w, axis=0)


def mixing_rows(first, second, nm):
    (band, w), (band_2, w_2) = first, second
    lane = iota((nm, LANES), 1)
    sub = iota((nm, LANES), 0)
    top = jnp.where((lane > sub) & (lane < nm), band, 0.0)
    low = jnp.where(lane < sub, turn(band_2, -nm), 0.0)
    top = jnp.where(lane == nm, w, top)
    low = jnp.where(lane == nm, w_2, low)
    rest = jnp.zeros((LANES - 2 * nm, LANES), F32)
    turned = jnp.concatenate([top, low, rest], axis=0).T
    return turned[nm:nm + 1] - (band + turned[:nm])


def pack_rows(x):
    nm = x.shape[0] - SUB
    width = nm + nm // 2 + 1
    lane8 = iota((SUB, LANES), 1)
    sub8 = iota((SUB, LANES), 0)
    w = x[nm:nm + 1]
    pieces = []
    for g in range(nm // SUB):
        part = x[g * SUB:(g + 1) * SUB]
        part = jnp.where(lane8 < nm, part, jnp.where(lane8 < width, skew(part, -g * SUB, -1), 0.0))
        if g % 2:
            pieces[-1] = pieces[-1] + turn(part, width)
        else:
            pieces.append(part)
    others = (sub8 == 0) & (lane8 >= 64) & (lane8 < 64 + nm)
    owns = (sub8 == 1) & (lane8 >= 64) & (lane8 < 64 + nm)
    pieces[-1] = pieces[-1] + jnp.where(others, turn(w, 64), 0.0) + jnp.where(owns, turn(w, 64 - nm), 0.0)
    return jnp.concatenate(pieces, axis=0)


def unpack_rows(p, nm):
    width = nm + nm // 2 + 1
    lane8 = iota((SUB, LANES), 1)
    lane = iota((nm, LANES), 1)
    sub = iota((nm, LANES), 0)
    others, band = [], []
    for g in range(nm // SUB):
        part = turn(p[g // 2 * SUB:(g // 2 + 1) * SUB], -width * (g % 2))
        others.append(jnp.where(lane8 < nm, part, 0.0))
        band.append(skew(jnp.where((lane8 >= nm) & (lane8 < width), part, 0.0), g * SUB - nm, 1))
    others, band = jnp.concatenate(others, axis=0), jnp.concatenate(band, axis=0)
    band = jnp.where(lane < nm, band, 0.0) + turn(jnp.where(lane >= nm, band, 0.0), -nm)
    apart = lane - sub
    apart = jnp.where(apart < 0, apart + nm, apart)
    once = jnp.where((lane < nm) & (apart >= 1) & (apart < nm // 2), band, 0.0)
    turned = jnp.concatenate([once, jnp.zeros((LANES - nm, LANES), F32)], axis=0).T[:nm]
    last = p[-SUB:]
    w = jnp.where(lane8[:1] < nm, turn(last[1:2], -64), 0.0)
    w = w + turn(jnp.where(lane8[:1] < nm, turn(last[0:1], -64), 0.0), nm)
    return w - (jnp.where(lane < nm, band, 0.0) + turned + turn(others, nm))


def local_kernel(step, nl, nm, regions, slots, levels, level_count, cores, *refs):
    *got, meta_ref, msg_ref, local_ref, spread_ref = refs
    region = lax.axis_index("region")
    level = lax.axis_index("level")
    member = lax.axis_index("member")
    members = nm * cores
    scale = levels / 4.0
    lane8 = iota((SUB, LANES), 1)
    packed = -(-(nl * nm // SUB) // regions)
    all_spread = []
    for l in range(nl):
        rows = []
        for half, c in enumerate((member, 1 - member)):
            for r in range(nm // SUB):
                g = l * (nm // SUB) + r
                j, k = g // regions, g % regions
                row = None
                for s in range(regions):
                    if len(got) == 1:
                        source = jnp.where(region >= s, region - s, region - s + regions)
                        part = got[0][source * cores + c, j * SUB:(j + 1) * SUB]
                    else:
                        part = got[s][(half * packed + j) * SUB:(half * packed + j + 1) * SUB]
                    part = turn(part, slots * (s - k))
                    row = part if row is None else jnp.where(lane8 >= slots * s, part, row)
                rows.append(row)
        predicted = jnp.concatenate(rows, axis=0)
        mean = jnp.sum(predicted, axis=0, keepdims=True) * (1.0 / members)
        spread = predicted - mean
        variance = jnp.sum(spread * spread, axis=0, keepdims=True) * (1.0 / (members - 1.0))
        all_spread.append((mean, spread, variance))
    mats = []
    for l, (mean, spread, variance) in enumerate(all_spread):
        obs_var = meta_ref[step, l:l + 1]
        obs_value = meta_ref[step, nl + l:nl + l + 1]
        horiz = meta_ref[step, 2 * nl:2 * nl + 1]
        total_var = variance + obs_var
        gain = (obs_value - mean) / total_var
        shrink = 1.0 / (1.0 + jnp.sqrt(obs_var / total_var))
        scaled = horiz * (1.0 / (members - 1.0))
        own = spread[:nm]
        left = scaled * (shrink / total_var) * own
        if step + 1 < STEPS:
            spread_ref[l] = jnp.concatenate([spread, jnp.zeros((LANES - members, LANES), F32)], axis=0)
        else:
            spread_ref[l] = jnp.concatenate([spread[nm:], own, own, jnp.zeros((LANES - 3 * nm, LANES), F32)], axis=0)
            left = jnp.concatenate([left, jnp.broadcast_to(scaled * gain, (SUB, LANES))], axis=0)
        product = lax.dot_general(left, spread_ref[l], BY_LANES, precision=HIGHEST, preferred_element_type=F32)
        if step + 1 < STEPS:
            mats.append(pack_mixing(product, jnp.sum(scaled * gain * own, axis=1, keepdims=True)))
        else:
            mats.append(pack_rows(product))
    up = sum(math.exp(-(nl - 1 - l) / scale) * mats[l] for l in range(nl))
    down = sum(math.exp(-l / scale) * mats[l] for l in range(nl))
    for l in range(nl):
        local_ref[l] = sum(math.exp(-abs(l - k) / scale) * mats[k] for k in range(nl))
    for d in range(level_count):
        msg_ref[d] = jnp.where(d > level, up, down)


def combine(nl, levels, level_count, got_ref, local_ref):
    level = lax.axis_index("level")
    scale = levels / 4.0
    fade = math.exp(-nl / scale)
    zero = jnp.zeros(got_ref.shape[1:], F32)
    below = lax.fori_loop(0, level, lambda d, acc: acc * fade + got_ref[d], zero)
    above = lax.fori_loop(0, level_count - 1 - level, lambda d, acc: acc * fade + got_ref[level_count - 1 - d], zero)
    return [
        math.exp(-(l + 1) / scale) * below + math.exp(-(nl - l) / scale) * above + local_ref[l] for l in range(nl)
    ]


def combine_kernel(nl, levels, level_count, got_ref, local_ref, later_ref, out_ref):
    out_ref[...] = jnp.concatenate(combine(nl, levels, level_count, got_ref, local_ref) + [later_ref[...]], axis=0)


def forecast_kernel(nl, nm, regions, slots, own_ref, other_ref, mix_ref, msg_ref, full_ref):
    lane8 = iota((SUB, LANES), 1)
    lane = iota((nm, LANES), 1)
    per = nm // SUB
    packed = -(-nl * per // regions)
    first = own_ref.shape[0] - packed * SUB
    rows = first // nl
    parts = [jnp.zeros((SUB, LANES), F32) for _ in range(2 * packed)]
    rest = jnp.zeros((LANES - 2 * nm, LANES), F32)
    for l in range(nl):
        pieces = []
        for ref in (own_ref, other_ref):
            for r in range(per):
                j, k = (l * per + r) // regions, (l * per + r) % regions
                pieces.append(turn(ref[first + j * SUB:first + (j + 1) * SUB], -slots * k))
        prior = jnp.concatenate(pieces + [rest], axis=0)
        full_ref[l] = prior
        bands = [unpack_mixing(ref[l * rows:(l + 1) * rows], nm) for ref in (own_ref, other_ref)]
        lower = mixing_rows(bands[1], bands[0], nm)
        swapped = jnp.where(lane < nm, turn(lower, -nm), jnp.where(lane < 2 * nm, turn(lower, nm), 0.0))
        mix_ref[l] = jnp.concatenate([mixing_rows(bands[0], bands[1], nm), swapped, rest], axis=0)
        result = prior + dot(mix_ref[l], full_ref[l])
        for half in range(2):
            for r in range(per):
                j, k = (l * per + r) // regions, (l * per + r) % regions
                keep = (lane8 >= slots * k) & (lane8 < slots * (k + 1))
                at = half * per + r
                j += half * packed
                parts[j] = jnp.where(keep, turn(result[at * SUB:(at + 1) * SUB], slots * k), parts[j])
    msg_ref[...] = jnp.concatenate(parts, axis=0)


def split(x):
    high = x.astype(BF16).astype(F32)
    return high, x - high


def update_kernel(nl, nm, levels, level_count, got_ref, local_ref, mix_ref, state_ref, theirs_ref, out_hbm,
                  out_v, left_ref, out_sem):
    nv = state_ref.shape[0]
    members = 2 * nm
    blocks = [(v, l) for l in range(nl) for v in range(nv)]
    lane = iota((nm, LANES), 1)
    for l, packed in enumerate(combine(nl, levels, level_count, got_ref, local_ref)):
        second = unpack_rows(packed, nm)
        both = second + mix_ref[l, 0:nm] + dot(second, mix_ref[l])
        high, low = split(both)
        again = turn(high, members)
        left_ref[l, :, 0:LANES] = high + jnp.where(lane >= members, again, 0.0)
        left_ref[l, :, LANES:] = jnp.where(lane < 2 * members - LANES, again, 0.0) + turn(low, 2 * members - LANES)
    pad = jnp.zeros((2 * LANES - 3 * members, state_ref.shape[3]), F32)
    stores = []
    for i, (v, l) in enumerate(blocks):
        own = state_ref[v, l]
        high, low = split(jnp.concatenate([own, theirs_ref[v, l]], axis=0))
        right = jnp.concatenate([high, low, high, pad], axis=0).astype(BF16)
        out_v[v, l] = own + jnp.dot(left_ref[l].astype(BF16), right, preferred_element_type=F32)
        copy = pltpu.make_async_copy(out_v.at[v, l], out_hbm.at[v, l], out_sem.at[i])
        copy.start()
        stores.append(copy)
    for copy in stores:
        copy.wait()


def body(state, ray_cols, ray_len, ray_weight, owner, loc_regions, loc_weight, obs_value, obs_var):
    regions = lax.axis_size("region")
    level_count = lax.axis_size("level")
    cores = lax.axis_size("member")
    nv, nl, nm, nc = state.shape
    occ, rays = ray_cols.shape[1:]
    slots = occ // regions
    levels = nl * level_count
    assert occ == LANES and regions * slots == LANES and nm % SUB == 0 and cores == 2
    assert LANES % rays == 0 and 2 * STEPS * slots == LANES
    groups = nl * nm // SUB
    block = (-(-groups // regions) * SUB, LANES)
    whole = pl.BlockSpec(memory_space=VMEM)
    outside = pl.BlockSpec(memory_space=pltpu.HBM)
    swap = [(0, 1), (1, 0)]
    dma = pltpu.SemaphoreType.DMA

    def call(kernel, statics, outs, scratch, *args, specs=None, out_specs=None, name=None, limit=32,
             kind=jax.ShapeDtypeStruct):
        def wrapped(*refs):
            return kernel(*statics, *refs)
        return pl.pallas_call(
            wrapped,
            out_shape=[kind(s, F32) for s in outs],
            in_specs=specs or [whole] * len(args),
            out_specs=out_specs or [whole] * len(outs),
            scratch_shapes=scratch,
            compiler_params=pltpu.CompilerParams(vmem_limit_bytes=limit * 2**20),
            name=name,
        )(*args)

    other_state = lax.ppermute(state, "member", swap)
    given = [ray_cols.swapaxes(1, 2), ray_len, ray_weight.transpose(0, 2, 3, 1), owner, loc_regions.swapaxes(1, 2),
             loc_weight.swapaxes(1, 2), obs_value.swapaxes(1, 2), obs_var.swapaxes(1, 2)]
    msg, later, meta, held = call(
        predict_kernel, (nl, nm, nc, regions, slots, rays),
        [(regions * cores,) + block, block, (STEPS, SUB, LANES), state.shape],
        [VMEM(a.shape, a.dtype) for a in given]
        + [VMEM((-(-nv * rays // LANES) * LANES, STEPS * LANES), F32), VMEM((nv * rays, STEPS * LANES), F32),
           VMEM((nv, 2 * STEPS * slots, nc), BF16), VMEM((SUB, LANES), F32), dma((nv,)), dma((len(given),))],
        state, *given, specs=[outside] * (1 + len(given)), name="predict", limit=56, kind=VMEM,
    )

    def assimilate(step, got, rows):
        out, local = call(
            local_kernel, (step, nl, nm, regions, slots, levels, level_count, cores),
            [(level_count, rows, LANES), (nl, rows, LANES)], [VMEM((nl, LANES, LANES), F32)],
            *got, meta, name="local",
        )
        return lax.all_to_all(out, "level", 0, 0, tiled=True), local

    band = -(-(nm // SUB) // (LANES // (nm + 2))) * SUB
    got = assimilate(0, [lax.all_to_all(msg, ("region", "member"), 0, 0, tiled=True)], band)
    own, = call(
        combine_kernel, (nl, levels, level_count), [(nl * band + block[0], LANES)], [], *got, later, name="combine",
    )
    mix, msg = call(
        forecast_kernel, (nl, nm, regions, slots),
        [(nl, LANES, LANES), (2 * block[0], LANES)], [VMEM((nl, LANES, LANES), F32)],
        own, lax.ppermute(own, "member", swap), name="forecast",
    )
    rings = [[(i, (i + s) % regions) for i in range(regions)] for s in range(1, regions)]
    got = assimilate(1, [msg] + [lax.ppermute(msg, "region", ring) for ring in rings], -(-(nm // SUB) // 2) * SUB)
    out, = call(
        update_kernel, (nl, nm, levels, level_count), [state.shape],
        [VMEM(state.shape, F32), VMEM((nl, nm, 2 * LANES), F32), dma((nv * nl,))],
        *got, mix, held, other_state, out_specs=[outside], name="update",
    )
    return out


def solution(mesh):
    in_specs = (P(None, "level", "member", "region"), P(), P(), P(), P(), P(), P(), P(), P())
    out_specs = P(None, "level", "member", "region")
    return jax.shard_map(body, mesh=mesh, in_specs=in_specs, out_specs=out_specs, check_vma=False)
```

```python
import math

import jax
import jax.numpy as jnp
from jax import lax
from jax.experimental import pallas as pl
from jax.experimental.pallas import tpu as pltpu
from jax.sharding import PartitionSpec as P

STEPS = 2
LANES = 128
SUB = 8
HIGHEST = lax.Precision.HIGHEST
F32 = jnp.float32
BF16 = jnp.bfloat16
VMEM = pltpu.VMEM
BY_LANES = (((1,), (1,)), ((), ()))


def iota(shape, dim):
    return lax.broadcasted_iota(jnp.int32, shape, dim)


def parts(x):
    high = x.astype(BF16)
    return high, (x - high.astype(F32)).astype(BF16)


def dot(a, b, by_lanes=False):
    (a_high, a_low), (b_high, b_low) = parts(a), parts(b)
    dims = BY_LANES if by_lanes else (((1,), (0,)), ((), ()))
    left = jnp.concatenate([a_high, a_low], axis=1)
    right = jnp.concatenate([b_high, b_high], axis=1 if by_lanes else 0)
    total = lax.dot_general(left, right, dims, preferred_element_type=F32)
    return total + lax.dot_general(a_high, b_low, dims, preferred_element_type=F32)


def turn(x, by):
    by = by % LANES
    return pltpu.roll(x, by, 1) if by else x


def pick(chosen, values):
    chosen = chosen.astype(BF16)
    total = None
    for _ in range(3):
        part = values.astype(BF16)
        term = lax.dot_general(chosen, part, BY_LANES, preferred_element_type=F32)
        total = term if total is None else total + term
        values = values - part.astype(F32)
    return total


def predict_kernel(nl, nm, nc, regions, slots, rays,
                   state_hbm, cols_hbm, len_hbm, weight_hbm, owner_hbm, locr_hbm, locw_hbm, obs_hbm, var_hbm,
                   msg_ref, later_ref, meta_ref, held,
                   cols_ref, len_ref, weight_ref, owner_ref, locr_ref, locw_ref, obs_ref, var_ref,
                   masked, sorted_ref, spread_out, meta_in, state_sem, arg_sem):
    nv = state_hbm.shape[0]
    region = lax.axis_index("region")
    level = lax.axis_index("level")
    pairs = [(cols_hbm, cols_ref), (len_hbm, len_ref), (weight_hbm, weight_ref), (owner_hbm, owner_ref),
             (locr_hbm, locr_ref), (locw_hbm, locw_ref), (obs_hbm, obs_ref), (var_hbm, var_ref)]
    fetches = [pltpu.make_async_copy(a, b, arg_sem.at[i]) for i, (a, b) in enumerate(pairs)]
    for copy in fetches:
        copy.start()
    copies = [pltpu.make_async_copy(state_hbm.at[v], held.at[v], state_sem.at[v]) for v in range(nv)]
    for copy in copies:
        copy.start()
    lane = iota((LANES, LANES), 1)
    sub = iota((LANES, LANES), 0)
    sub8 = iota((SUB, LANES), 0)
    earlier = (sub < lane).astype(BF16)
    region_f = region.astype(F32)
    masked[nv * rays:] = jnp.zeros((masked.shape[0] - nv * rays, STEPS * LANES), F32)
    meta_in[...] = jnp.zeros_like(meta_in)
    for copy in fetches:
        copy.wait()
    firsts, places, worst = [], [], None
    for step in range(STEPS):
        cols = cols_ref[step].astype(F32)
        first = jnp.min(cols, axis=0, keepdims=True)
        off = jnp.max(jnp.abs(cols - first - sub[:rays].astype(F32)))
        worst = off if worst is None else jnp.maximum(worst, off)
        home = jnp.zeros_like(first)
        for q in range(1, regions):
            home = home + (first >= float(q * nc)).astype(F32)
        at_home = (sub8.astype(F32) == home).astype(F32)
        count = jnp.dot(at_home.astype(BF16), earlier, preferred_element_type=F32)
        rank = jnp.sum(at_home * count, axis=0, keepdims=True)
        ahead = region_f - home
        ahead = jnp.where(ahead < 0.0, ahead + float(regions), ahead)
        places.append(ahead * float(slots) + rank)
        firsts.append(first)
        live = sub[:rays] < len_ref[step:step + 1]
        for v in range(nv):
            masked[v * rays:(v + 1) * rays, step * LANES:(step + 1) * LANES] = jnp.where(live, weight_ref[step, v], 0.0)
    slot = sub[:STEPS * slots].astype(F32)
    mine = []
    for step in range(STEPS):
        ours = (slot >= float(step * slots)) & (slot < float((step + 1) * slots))
        mine.append(((places[step] == slot - float(step * slots)) & ours).astype(F32))
    mine = jnp.concatenate(mine, axis=1)

    @pl.when(worst > 0.5)
    def _():
        column = jnp.concatenate([cols_ref[s].astype(F32) - firsts[s] for s in range(STEPS)], axis=1)

        def one(d, carry):
            hit = column == d.astype(F32)
            for v in range(nv):
                weights = masked[v * rays:(v + 1) * rays]
                sorted_ref[pl.ds(v * rays + d, 1)] = jnp.sum(jnp.where(hit, weights, 0.0), axis=0, keepdims=True)
            return carry
        lax.fori_loop(0, rays, one, 0)
        masked[0:nv * rays] = sorted_ref[...]

    first = jnp.broadcast_to(jnp.concatenate(firsts, axis=1), (LANES, STEPS * LANES))
    low = pick(mine, first).astype(jnp.int32) - region * nc
    tile, shift = low >> 7, low & (LANES - 1)
    picked = pick(mine, masked[...])
    lane_s = lane[:STEPS * slots]
    for v in range(nv):
        at = v * rays
        row = picked[:, at // LANES * LANES:(at // LANES + 1) * LANES]
        at = at % LANES
        row = turn(jnp.where((lane_s >= at) & (lane_s < at + rays), row, 0.0), -at)
        for bit in range(7):
            row = jnp.where((shift >> bit) % 2 == 1, turn(row, 1 << bit), row)
        near, far = jnp.where(lane_s >= shift, row, 0.0), jnp.where(lane_s < shift, row, 0.0)
        for t in range(nc // LANES):
            there = jnp.where(tile == t, near, jnp.where(tile == t - 1, far, 0.0))
            high = there.astype(BF16)
            spread_out[v, 0:STEPS * slots, t * LANES:(t + 1) * LANES] = high
            spread_out[v, STEPS * slots:, t * LANES:(t + 1) * LANES] = (there - high.astype(F32)).astype(BF16)
    for step in range(STEPS):
        horiz = (owner_ref[step:step + 1] == region).astype(F32)
        listed = (locr_ref[step] == region).astype(F32)
        horiz = horiz + jnp.sum(locw_ref[step] * listed, axis=0, keepdims=True)
        for l in range(nl):
            meta_in[l:l + 1] = var_ref[step, pl.ds(level * nl + l, 1)]
            meta_in[nl + l:nl + l + 1] = obs_ref[step, pl.ds(level * nl + l, 1)]
        meta_in[2 * nl:2 * nl + 1] = horiz
        order = (places[step] == sub.astype(F32)).astype(F32)
        meta_ref[step] = lax.dot_general(meta_in[...], order, BY_LANES, precision=HIGHEST, preferred_element_type=F32)
    total = None
    for v in range(nv):
        copies[v].wait()
        prior = jnp.concatenate([held[v, l] for l in range(nl)], axis=0)
        high = prior.astype(BF16)
        left = jnp.concatenate([high, (prior - high.astype(F32)).astype(BF16)], axis=0)
        term = lax.dot_general(left, spread_out[v], BY_LANES, preferred_element_type=F32)
        total = term if total is None else total + term
    result = total[:nl * nm] + total[nl * nm:]
    result = result + turn(result, -STEPS * slots)
    groups = nl * nm // SUB
    packed = -(-groups // regions)
    lane8 = lane[:SUB]
    for step in range(STEPS):
        parts = [jnp.zeros((SUB, LANES), F32) for _ in range(packed)]
        for g in range(groups):
            j, k = g // regions, g % regions
            here = (lane8 >= slots * k) & (lane8 < slots * (k + 1))
            parts[j] = jnp.where(here, turn(result[g * SUB:(g + 1) * SUB], slots * (k - step)), parts[j])
        for j in range(packed):
            if step == 0:
                for d in range(msg_ref.shape[0]):
                    msg_ref[d, j * SUB:(j + 1) * SUB] = parts[j]
            else:
                later_ref[j * SUB:(j + 1) * SUB] = parts[j]


def skew(x, by, sign):
    x = turn(x, by)
    sub8 = iota((SUB, LANES), 0)
    for bit in range(3):
        x = jnp.where((sub8 >> bit) % 2 == 1, turn(x, sign << bit), x)
    return x


def pack_mixing(s, w):
    nm = s.shape[0]
    width, across = nm + 2, LANES // (nm + 2)
    lane8 = iota((SUB, LANES), 1)
    pieces = []
    for g in range(nm // SUB):
        at = width * (g % across)
        part = skew(s[g * SUB:(g + 1) * SUB], at - g * SUB, -1)
        part = jnp.where((lane8 >= at) & (lane8 <= at + nm), part, 0.0)
        part = jnp.where(lane8 == at + nm + 1, w[g * SUB:(g + 1) * SUB], part)
        if g % across:
            pieces[-1] = pieces[-1] + part
        else:
            pieces.append(part)
    return jnp.concatenate(pieces, axis=0)


def unpack_mixing(p, nm):
    width, across = nm + 2, LANES // (nm + 2)
    lane8 = iota((SUB, LANES), 1)
    band, w = [], []
    for g in range(nm // SUB):
        at, j = width * (g % across), g // across
        part = p[j * SUB:(j + 1) * SUB]
        band.append(skew(jnp.where((lane8 >= at) & (lane8 <= at + nm), part, 0.0), g * SUB - at, 1))
        w.append(part[:, at + nm + 1:at + nm + 2])
    return jnp.concatenate(band, axis=0), jnp.concatenate(w, axis=0)


def mixing_rows(first, second, nm):
    (band, w), (band_2, w_2) = first, second
    lane = iota((nm, LANES), 1)
    sub = iota((nm, LANES), 0)
    top = jnp.where((lane > sub) & (lane < nm), band, 0.0)
    low = jnp.where(lane < sub, turn(band_2, -nm), 0.0)
    top = jnp.where(lane == nm, w, top)
    low = jnp.where(lane == nm, w_2, low)
    rest = jnp.zeros((LANES - 2 * nm, LANES), F32)
    turned = jnp.concatenate([top, low, rest], axis=0).T
    return turned[nm:nm + 1] - (band + turned[:nm])


def pack_rows(x):
    nm = x.shape[0] - SUB
    width = nm + nm // 2 + 1
    lane8 = iota((SUB, LANES), 1)
    sub8 = iota((SUB, LANES), 0)
    w = x[nm:nm + 1]
    pieces = []
    for g in range(nm // SUB):
        part = x[g * SUB:(g + 1) * SUB]
        part = jnp.where(lane8 < nm, part, jnp.where(lane8 < width, skew(part, -g * SUB, -1), 0.0))
        if g % 2:
            pieces[-1] = pieces[-1] + turn(part, width)
        else:
            pieces.append(part)
    others = (sub8 == 0) & (lane8 >= 64) & (lane8 < 64 + nm)
    owns = (sub8 == 1) & (lane8 >= 64) & (lane8 < 64 + nm)
    pieces[-1] = pieces[-1] + jnp.where(others, turn(w, 64), 0.0) + jnp.where(owns, turn(w, 64 - nm), 0.0)
    return jnp.concatenate(pieces, axis=0)


def unpack_rows(p, nm):
    width = nm + nm // 2 + 1
    lane8 = iota((SUB, LANES), 1)
    lane = iota((nm, LANES), 1)
    sub = iota((nm, LANES), 0)
    others, band = [], []
    for g in range(nm // SUB):
        part = turn(p[g // 2 * SUB:(g // 2 + 1) * SUB], -width * (g % 2))
        others.append(jnp.where(lane8 < nm, part, 0.0))
        band.append(skew(jnp.where((lane8 >= nm) & (lane8 < width), part, 0.0), g * SUB - nm, 1))
    others, band = jnp.concatenate(others, axis=0), jnp.concatenate(band, axis=0)
    band = jnp.where(lane < nm, band, 0.0) + turn(jnp.where(lane >= nm, band, 0.0), -nm)
    apart = lane - sub
    apart = jnp.where(apart < 0, apart + nm, apart)
    once = jnp.where((lane < nm) & (apart >= 1) & (apart < nm // 2), band, 0.0)
    turned = jnp.concatenate([once, jnp.zeros((LANES - nm, LANES), F32)], axis=0).T[:nm]
    last = p[-SUB:]
    w = jnp.where(lane8[:1] < nm, turn(last[1:2], -64), 0.0)
    w = w + turn(jnp.where(lane8[:1] < nm, turn(last[0:1], -64), 0.0), nm)
    return w - (jnp.where(lane < nm, band, 0.0) + turned + turn(others, nm))


def local_kernel(step, nl, nm, regions, slots, levels, level_count, cores, *refs):
    *got, meta_ref, msg_ref, local_ref, spread_ref = refs
    region = lax.axis_index("region")
    level = lax.axis_index("level")
    member = lax.axis_index("member")
    members = nm * cores
    scale = levels / 4.0
    lane8 = iota((SUB, LANES), 1)
    packed = -(-(nl * nm // SUB) // regions)
    all_spread = []
    for l in range(nl):
        rows = []
        for half, c in enumerate((member, 1 - member)):
            for r in range(nm // SUB):
                g = l * (nm // SUB) + r
                j, k = g // regions, g % regions
                row = None
                for s in range(regions):
                    if len(got) == 1:
                        source = jnp.where(region >= s, region - s, region - s + regions)
                        part = got[0][source * cores + c, j * SUB:(j + 1) * SUB]
                    else:
                        part = got[s][(half * packed + j) * SUB:(half * packed + j + 1) * SUB]
                    part = turn(part, slots * (s - k))
                    row = part if row is None else jnp.where(lane8 >= slots * s, part, row)
                rows.append(row)
        predicted = jnp.concatenate(rows, axis=0)
        mean = jnp.sum(predicted, axis=0, keepdims=True) * (1.0 / members)
        spread = predicted - mean
        variance = jnp.sum(spread * spread, axis=0, keepdims=True) * (1.0 / (members - 1.0))
        all_spread.append((mean, spread, variance))
    mats = []
    for l, (mean, spread, variance) in enumerate(all_spread):
        obs_var = meta_ref[step, l:l + 1]
        obs_value = meta_ref[step, nl + l:nl + l + 1]
        horiz = meta_ref[step, 2 * nl:2 * nl + 1]
        total_var = variance + obs_var
        gain = (obs_value - mean) / total_var
        shrink = 1.0 / (1.0 + jnp.sqrt(obs_var / total_var))
        scaled = horiz * (1.0 / (members - 1.0))
        own = spread[:nm]
        left = scaled * (shrink / total_var) * own
        if step + 1 < STEPS:
            spread_ref[l] = jnp.concatenate([spread, jnp.zeros((LANES - members, LANES), F32)], axis=0)
        else:
            spread_ref[l] = jnp.concatenate([spread[nm:], own, own, jnp.zeros((LANES - 3 * nm, LANES), F32)], axis=0)
            left = jnp.concatenate([left, jnp.broadcast_to(scaled * gain, (SUB, LANES))], axis=0)
        product = dot(left, spread_ref[l], by_lanes=True)
        if step + 1 < STEPS:
            mats.append(pack_mixing(product, jnp.sum(scaled * gain * own, axis=1, keepdims=True)))
        else:
            mats.append(pack_rows(product))
    up = sum(math.exp(-(nl - 1 - l) / scale) * mats[l] for l in range(nl))
    down = sum(math.exp(-l / scale) * mats[l] for l in range(nl))
    for l in range(nl):
        local_ref[l] = sum(math.exp(-abs(l - k) / scale) * mats[k] for k in range(nl))
    for d in range(level_count):
        msg_ref[d] = jnp.where(d > level, up, down)


def combine(nl, levels, level_count, got_ref, local_ref):
    level = lax.axis_index("level")
    scale = levels / 4.0
    fade = math.exp(-nl / scale)
    zero = jnp.zeros(got_ref.shape[1:], F32)
    below = lax.fori_loop(0, level, lambda d, acc: acc * fade + got_ref[d], zero)
    above = lax.fori_loop(0, level_count - 1 - level, lambda d, acc: acc * fade + got_ref[level_count - 1 - d], zero)
    return [
        math.exp(-(l + 1) / scale) * below + math.exp(-(nl - l) / scale) * above + local_ref[l] for l in range(nl)
    ]


def combine_kernel(nl, levels, level_count, got_ref, local_ref, later_ref, out_ref):
    out_ref[...] = jnp.concatenate(combine(nl, levels, level_count, got_ref, local_ref) + [later_ref[...]], axis=0)


def forecast_kernel(nl, nm, regions, slots, own_ref, other_ref, mix_ref, msg_ref, full_ref):
    lane8 = iota((SUB, LANES), 1)
    lane = iota((nm, LANES), 1)
    per = nm // SUB
    packed = -(-nl * per // regions)
    first = own_ref.shape[0] - packed * SUB
    rows = first // nl
    pieces_out = [jnp.zeros((SUB, LANES), F32) for _ in range(2 * packed)]
    rest = jnp.zeros((LANES - 2 * nm, LANES), F32)
    for l in range(nl):
        pieces = []
        for ref in (own_ref, other_ref):
            for r in range(per):
                j, k = (l * per + r) // regions, (l * per + r) % regions
                pieces.append(turn(ref[first + j * SUB:first + (j + 1) * SUB], -slots * k))
        prior = jnp.concatenate(pieces + [rest], axis=0)
        full_ref[l] = prior
        bands = [unpack_mixing(ref[l * rows:(l + 1) * rows], nm) for ref in (own_ref, other_ref)]
        lower = mixing_rows(bands[1], bands[0], nm)
        swapped = jnp.where(lane < nm, turn(lower, -nm), jnp.where(lane < 2 * nm, turn(lower, nm), 0.0))
        mix_ref[l] = jnp.concatenate([mixing_rows(bands[0], bands[1], nm), swapped, rest], axis=0)
        result = prior + dot(mix_ref[l], full_ref[l])
        for half in range(2):
            for r in range(per):
                j, k = (l * per + r) // regions, (l * per + r) % regions
                keep = (lane8 >= slots * k) & (lane8 < slots * (k + 1))
                at = half * per + r
                j += half * packed
                pieces_out[j] = jnp.where(keep, turn(result[at * SUB:(at + 1) * SUB], slots * k), pieces_out[j])
    msg_ref[...] = jnp.concatenate(pieces_out, axis=0)


def split(x):
    high = x.astype(BF16).astype(F32)
    return high, x - high


def update_kernel(nl, nm, levels, level_count, got_ref, local_ref, mix_ref, state_ref, theirs_ref, out_hbm,
                  out_v, left_ref, out_sem):
    nv = state_ref.shape[0]
    members = 2 * nm
    blocks = [(v, l) for l in range(nl) for v in range(nv)]
    lane = iota((nm, LANES), 1)
    for l, packed in enumerate(combine(nl, levels, level_count, got_ref, local_ref)):
        second = unpack_rows(packed, nm)
        both = second + mix_ref[l, 0:nm] + dot(second, mix_ref[l])
        high, low = split(both)
        again = turn(high, members)
        left_ref[l, :, 0:LANES] = high + jnp.where(lane >= members, again, 0.0)
        left_ref[l, :, LANES:] = jnp.where(lane < 2 * members - LANES, again, 0.0) + turn(low, 2 * members - LANES)
    pad = jnp.zeros((2 * LANES - 3 * members, state_ref.shape[3]), F32)
    stores = []
    for i, (v, l) in enumerate(blocks):
        own = state_ref[v, l]
        high, low = split(jnp.concatenate([own, theirs_ref[v, l]], axis=0))
        right = jnp.concatenate([high, low, high, pad], axis=0).astype(BF16)
        out_v[v, l] = own + jnp.dot(left_ref[l].astype(BF16), right, preferred_element_type=F32)
        copy = pltpu.make_async_copy(out_v.at[v, l], out_hbm.at[v, l], out_sem.at[i])
        copy.start()
        stores.append(copy)
    for copy in stores:
        copy.wait()


def body(state, ray_cols, ray_len, ray_weight, owner, loc_regions, loc_weight, obs_value, obs_var):
    regions = lax.axis_size("region")
    level_count = lax.axis_size("level")
    cores = lax.axis_size("member")
    nv, nl, nm, nc = state.shape
    occ, rays = ray_cols.shape[1:]
    slots = occ // regions
    levels = nl * level_count
    assert occ == LANES and regions * slots == LANES and nm % SUB == 0 and cores == 2
    assert LANES % rays == 0 and 2 * STEPS * slots == LANES
    groups = nl * nm // SUB
    block = (-(-groups // regions) * SUB, LANES)
    whole = pl.BlockSpec(memory_space=VMEM)
    outside = pl.BlockSpec(memory_space=pltpu.HBM)
    swap = [(0, 1), (1, 0)]
    dma = pltpu.SemaphoreType.DMA

    def call(kernel, statics, outs, scratch, *args, specs=None, out_specs=None, name=None, limit=32,
             kind=jax.ShapeDtypeStruct):
        def wrapped(*refs):
            return kernel(*statics, *refs)
        return pl.pallas_call(
            wrapped,
            out_shape=[kind(s, F32) for s in outs],
            in_specs=specs or [whole] * len(args),
            out_specs=out_specs or [whole] * len(outs),
            scratch_shapes=scratch,
            compiler_params=pltpu.CompilerParams(vmem_limit_bytes=limit * 2**20),
            name=name,
        )(*args)

    other_state = lax.ppermute(state, "member", swap)
    given = [ray_cols.swapaxes(1, 2), ray_len, ray_weight.transpose(0, 2, 3, 1), owner, loc_regions.swapaxes(1, 2),
             loc_weight.swapaxes(1, 2), obs_value.swapaxes(1, 2), obs_var.swapaxes(1, 2)]
    msg, later, meta, held = call(
        predict_kernel, (nl, nm, nc, regions, slots, rays),
        [(regions * cores,) + block, block, (STEPS, SUB, LANES), state.shape],
        [VMEM(a.shape, a.dtype) for a in given]
        + [VMEM((-(-nv * rays // LANES) * LANES, STEPS * LANES), F32), VMEM((nv * rays, STEPS * LANES), F32),
           VMEM((nv, 2 * STEPS * slots, nc), BF16), VMEM((SUB, LANES), F32), dma((nv,)), dma((len(given),))],
        state, *given, specs=[outside] * (1 + len(given)), name="predict", limit=56, kind=VMEM,
    )

    def assimilate(step, got, rows):
        out, local = call(
            local_kernel, (step, nl, nm, regions, slots, levels, level_count, cores),
            [(level_count, rows, LANES), (nl, rows, LANES)], [VMEM((nl, LANES, LANES), F32)],
            *got, meta, name="local",
        )
        return lax.all_to_all(out, "level", 0, 0, tiled=True), local

    band = -(-(nm // SUB) // (LANES // (nm + 2))) * SUB
    got = assimilate(0, [lax.all_to_all(msg, ("region", "member"), 0, 0, tiled=True)], band)
    own, = call(
        combine_kernel, (nl, levels, level_count), [(nl * band + block[0], LANES)], [], *got, later, name="combine",
    )
    mix, msg = call(
        forecast_kernel, (nl, nm, regions, slots),
        [(nl, LANES, LANES), (2 * block[0], LANES)], [VMEM((nl, LANES, LANES), F32)],
        own, lax.ppermute(own, "member", swap), name="forecast",
    )
    rings = [[(i, (i + s) % regions) for i in range(regions)] for s in range(1, regions)]
    got = assimilate(1, [msg] + [lax.ppermute(msg, "region", ring) for ring in rings], -(-(nm // SUB) // 2) * SUB)
    out, = call(
        update_kernel, (nl, nm, levels, level_count), [state.shape],
        [VMEM(state.shape, F32), VMEM((nl, nm, 2 * LANES), F32), dma((nv * nl,))],
        *got, mix, held, other_state, out_specs=[outside], name="update",
    )
    return out


def solution(mesh):
    in_specs = (P(None, "level", "member", "region"), P(), P(), P(), P(), P(), P(), P(), P())
    out_specs = P(None, "level", "member", "region")
    return jax.shard_map(body, mesh=mesh, in_specs=in_specs, out_specs=out_specs, check_vma=False)
```

```python
import math

import jax
import jax.numpy as jnp
from jax import lax
from jax.experimental import pallas as pl
from jax.experimental.pallas import tpu as pltpu
from jax.sharding import PartitionSpec as P

STEPS = 2
LANES = 128
SUB = 8
HIGHEST = lax.Precision.HIGHEST
F32 = jnp.float32
BF16 = jnp.bfloat16
VMEM = pltpu.VMEM
BY_LANES = (((1,), (1,)), ((), ()))


def iota(shape, dim):
    return lax.broadcasted_iota(jnp.int32, shape, dim)


def parts(x):
    high = x.astype(BF16)
    return high, (x - high.astype(F32)).astype(BF16)


def dot(a, b, by_lanes=False):
    (a_high, a_low), (b_high, b_low) = parts(a), parts(b)
    dims = BY_LANES if by_lanes else (((1,), (0,)), ((), ()))
    left = jnp.concatenate([a_high, a_low], axis=1)
    right = jnp.concatenate([b_high, b_high], axis=1 if by_lanes else 0)
    total = lax.dot_general(left, right, dims, preferred_element_type=F32)
    return total + lax.dot_general(a_high, b_low, dims, preferred_element_type=F32)


def turn(x, by):
    by = by % LANES
    return pltpu.roll(x, by, 1) if by else x


def pick(chosen, values):
    chosen = chosen.astype(BF16)
    total = None
    for _ in range(3):
        part = values.astype(BF16)
        term = lax.dot_general(chosen, part, BY_LANES, preferred_element_type=F32)
        total = term if total is None else total + term
        values = values - part.astype(F32)
    return total


def predict_kernel(nl, nm, nc, regions, slots, rays,
                   state_hbm, cols_hbm, len_hbm, weight_hbm, owner_hbm, locr_hbm, locw_hbm, obs_hbm, var_hbm,
                   msg_ref, later_ref, meta_ref, held,
                   cols_ref, len_ref, weight_ref, owner_ref, locr_ref, locw_ref, obs_ref, var_ref,
                   masked, sorted_ref, spread_out, meta_in, state_sem, arg_sem):
    nv = state_hbm.shape[0]
    region = lax.axis_index("region")
    level = lax.axis_index("level")
    pairs = [(cols_hbm, cols_ref), (len_hbm, len_ref), (weight_hbm, weight_ref), (owner_hbm, owner_ref),
             (locr_hbm, locr_ref), (locw_hbm, locw_ref), (obs_hbm, obs_ref), (var_hbm, var_ref)]
    fetches = [pltpu.make_async_copy(a, b, arg_sem.at[i]) for i, (a, b) in enumerate(pairs)]
    for copy in fetches:
        copy.start()
    copies = [pltpu.make_async_copy(state_hbm.at[v], held.at[v], state_sem.at[v]) for v in range(nv)]
    for copy in copies:
        copy.start()
    lane = iota((LANES, LANES), 1)
    sub = iota((LANES, LANES), 0)
    sub8 = iota((SUB, LANES), 0)
    earlier = (sub < lane).astype(BF16)
    region_f = region.astype(F32)
    masked[nv * rays:] = jnp.zeros((masked.shape[0] - nv * rays, STEPS * LANES), F32)
    meta_in[...] = jnp.zeros_like(meta_in)
    for copy in fetches:
        copy.wait()
    firsts, places, worst = [], [], None
    for step in range(STEPS):
        cols = cols_ref[step].astype(F32)
        first = jnp.min(cols, axis=0, keepdims=True)
        off = jnp.max(jnp.abs(cols - first - sub[:rays].astype(F32)))
        worst = off if worst is None else jnp.maximum(worst, off)
        home = jnp.zeros_like(first)
        for q in range(1, regions):
            home = home + (first >= float(q * nc)).astype(F32)
        at_home = (sub8.astype(F32) == home).astype(F32)
        count = jnp.dot(at_home.astype(BF16), earlier, preferred_element_type=F32)
        rank = jnp.sum(at_home * count, axis=0, keepdims=True)
        ahead = region_f - home
        ahead = jnp.where(ahead < 0.0, ahead + float(regions), ahead)
        places.append(ahead * float(slots) + rank)
        firsts.append(first)
        live = sub[:rays] < len_ref[step:step + 1]
        for v in range(nv):
            masked[v * rays:(v + 1) * rays, step * LANES:(step + 1) * LANES] = jnp.where(live, weight_ref[step, v], 0.0)
    slot = sub[:STEPS * slots].astype(F32)
    mine = []
    for step in range(STEPS):
        ours = (slot >= float(step * slots)) & (slot < float((step + 1) * slots))
        mine.append(((places[step] == slot - float(step * slots)) & ours).astype(F32))
    mine = jnp.concatenate(mine, axis=1)

    @pl.when(worst > 0.5)
    def _():
        column = jnp.concatenate([cols_ref[s].astype(F32) - firsts[s] for s in range(STEPS)], axis=1)

        def one(d, carry):
            hit = column == d.astype(F32)
            for v in range(nv):
                weights = masked[v * rays:(v + 1) * rays]
                sorted_ref[pl.ds(v * rays + d, 1)] = jnp.sum(jnp.where(hit, weights, 0.0), axis=0, keepdims=True)
            return carry
        lax.fori_loop(0, rays, one, 0)
        masked[0:nv * rays] = sorted_ref[...]

    first = jnp.broadcast_to(jnp.concatenate(firsts, axis=1), (LANES, STEPS * LANES))
    low = pick(mine, first).astype(jnp.int32) - region * nc
    tile, shift = low >> 7, low & (LANES - 1)
    picked = pick(mine, masked[...])
    lane_s = lane[:STEPS * slots]
    for v in range(nv):
        at = v * rays
        row = picked[:, at // LANES * LANES:(at // LANES + 1) * LANES]
        at = at % LANES
        row = turn(jnp.where((lane_s >= at) & (lane_s < at + rays), row, 0.0), -at)
        for bit in range(7):
            row = jnp.where((shift >> bit) % 2 == 1, turn(row, 1 << bit), row)
        near, far = jnp.where(lane_s >= shift, row, 0.0), jnp.where(lane_s < shift, row, 0.0)
        for t in range(nc // LANES):
            there = jnp.where(tile == t, near, jnp.where(tile == t - 1, far, 0.0))
            high = there.astype(BF16)
            spread_out[v, 0:STEPS * slots, t * LANES:(t + 1) * LANES] = high
            spread_out[v, STEPS * slots:, t * LANES:(t + 1) * LANES] = (there - high.astype(F32)).astype(BF16)
    for step in range(STEPS):
        horiz = (owner_ref[step:step + 1] == region).astype(F32)
        listed = (locr_ref[step] == region).astype(F32)
        horiz = horiz + jnp.sum(locw_ref[step] * listed, axis=0, keepdims=True)
        for l in range(nl):
            meta_in[l:l + 1] = var_ref[step, pl.ds(level * nl + l, 1)]
            meta_in[nl + l:nl + l + 1] = obs_ref[step, pl.ds(level * nl + l, 1)]
        meta_in[2 * nl:2 * nl + 1] = horiz
        order = (places[step] == sub.astype(F32)).astype(F32)
        meta_ref[step] = lax.dot_general(meta_in[...], order, BY_LANES, precision=HIGHEST, preferred_element_type=F32)
    total = None
    for v in range(nv):
        copies[v].wait()
        prior = jnp.concatenate([held[v, l] for l in range(nl)], axis=0)
        high = prior.astype(BF16)
        left = jnp.concatenate([high, (prior - high.astype(F32)).astype(BF16)], axis=0)
        term = lax.dot_general(left, spread_out[v], BY_LANES, preferred_element_type=F32)
        total = term if total is None else total + term
    result = total[:nl * nm] + total[nl * nm:]
    result = result + turn(result, -STEPS * slots)
    groups = nl * nm // SUB
    packed = -(-groups // regions)
    lane8 = lane[:SUB]
    for step in range(STEPS):
        parts = [jnp.zeros((SUB, LANES), F32) for _ in range(packed)]
        for g in range(groups):
            j, k = g // regions, g % regions
            here = (lane8 >= slots * k) & (lane8 < slots * (k + 1))
            parts[j] = jnp.where(here, turn(result[g * SUB:(g + 1) * SUB], slots * (k - step)), parts[j])
        for j in range(packed):
            if step == 0:
                for d in range(msg_ref.shape[0]):
                    msg_ref[d, j * SUB:(j + 1) * SUB] = parts[j]
            else:
                later_ref[j * SUB:(j + 1) * SUB] = parts[j]


def skew(x, by, sign):
    x = turn(x, by)
    sub8 = iota((SUB, LANES), 0)
    for bit in range(3):
        x = jnp.where((sub8 >> bit) % 2 == 1, turn(x, sign << bit), x)
    return x


def pack_mixing(s, w):
    nm = s.shape[0]
    width, across = nm + 2, LANES // (nm + 2)
    lane8 = iota((SUB, LANES), 1)
    pieces = []
    for g in range(nm // SUB):
        at = width * (g % across)
        part = skew(s[g * SUB:(g + 1) * SUB], at - g * SUB, -1)
        part = jnp.where((lane8 >= at) & (lane8 <= at + nm), part, 0.0)
        part = jnp.where(lane8 == at + nm + 1, w[g * SUB:(g + 1) * SUB], part)
        if g % across:
            pieces[-1] = pieces[-1] + part
        else:
            pieces.append(part)
    return jnp.concatenate(pieces, axis=0)


def unpack_mixing(p, nm):
    width, across = nm + 2, LANES // (nm + 2)
    lane8 = iota((SUB, LANES), 1)
    band, w = [], []
    for g in range(nm // SUB):
        at, j = width * (g % across), g // across
        part = p[j * SUB:(j + 1) * SUB]
        band.append(skew(jnp.where((lane8 >= at) & (lane8 <= at + nm), part, 0.0), g * SUB - at, 1))
        w.append(part[:, at + nm + 1:at + nm + 2])
    return jnp.concatenate(band, axis=0), jnp.concatenate(w, axis=0)


def mixing_rows(first, second, nm):
    (band, w), (band_2, w_2) = first, second
    lane = iota((nm, LANES), 1)
    sub = iota((nm, LANES), 0)
    top = jnp.where((lane > sub) & (lane < nm), band, 0.0)
    low = jnp.where(lane < sub, turn(band_2, -nm), 0.0)
    top = jnp.where(lane == nm, w, top)
    low = jnp.where(lane == nm, w_2, low)
    rest = jnp.zeros((LANES - 2 * nm, LANES), F32)
    turned = jnp.concatenate([top, low, rest], axis=0).T
    return turned[nm:nm + 1] - (band + turned[:nm])


def pack_rows(x):
    nm = x.shape[0] - SUB
    width = nm + nm // 2 + 1
    lane8 = iota((SUB, LANES), 1)
    sub8 = iota((SUB, LANES), 0)
    w = x[nm:nm + 1]
    pieces = []
    for g in range(nm // SUB):
        part = x[g * SUB:(g + 1) * SUB]
        part = jnp.where(lane8 < nm, part, jnp.where(lane8 < width, skew(part, -g * SUB, -1), 0.0))
        if g % 2:
            pieces[-1] = pieces[-1] + turn(part, width)
        else:
            pieces.append(part)
    others = (sub8 == 0) & (lane8 >= 64) & (lane8 < 64 + nm)
    owns = (sub8 == 1) & (lane8 >= 64) & (lane8 < 64 + nm)
    pieces[-1] = pieces[-1] + jnp.where(others, turn(w, 64), 0.0) + jnp.where(owns, turn(w, 64 - nm), 0.0)
    return jnp.concatenate(pieces, axis=0)


def unpack_rows(p, nm):
    width = nm + nm // 2 + 1
    lane8 = iota((SUB, LANES), 1)
    lane = iota((nm, LANES), 1)
    sub = iota((nm, LANES), 0)
    others, band = [], []
    for g in range(nm // SUB):
        part = turn(p[g // 2 * SUB:(g // 2 + 1) * SUB], -width * (g % 2))
        others.append(jnp.where(lane8 < nm, part, 0.0))
        band.append(skew(jnp.where((lane8 >= nm) & (lane8 < width), part, 0.0), g * SUB - nm, 1))
    others, band = jnp.concatenate(others, axis=0), jnp.concatenate(band, axis=0)
    band = jnp.where(lane < nm, band, 0.0) + turn(jnp.where(lane >= nm, band, 0.0), -nm)
    apart = lane - sub
    apart = jnp.where(apart < 0, apart + nm, apart)
    once = jnp.where((lane < nm) & (apart >= 1) & (apart < nm // 2), band, 0.0)
    turned = jnp.concatenate([once, jnp.zeros((LANES - nm, LANES), F32)], axis=0).T[:nm]
    last = p[-SUB:]
    w = jnp.where(lane8[:1] < nm, turn(last[1:2], -64), 0.0)
    w = w + turn(jnp.where(lane8[:1] < nm, turn(last[0:1], -64), 0.0), nm)
    return w - (jnp.where(lane < nm, band, 0.0) + turned + turn(others, nm))


def local_kernel(step, nl, nm, regions, slots, levels, level_count, cores, *refs):
    *got, meta_ref, msg_ref, local_ref, spread_ref = refs
    region = lax.axis_index("region")
    level = lax.axis_index("level")
    member = lax.axis_index("member")
    members = nm * cores
    scale = levels / 4.0
    lane8 = iota((SUB, LANES), 1)
    packed = -(-(nl * nm // SUB) // regions)
    all_spread = []
    for l in range(nl):
        rows = []
        for half, c in enumerate((member, 1 - member)):
            for r in range(nm // SUB):
                g = l * (nm // SUB) + r
                j, k = g // regions, g % regions
                row = None
                for s in range(regions):
                    if len(got) == 1:
                        source = jnp.where(region >= s, region - s, region - s + regions)
                        part = got[0][source * cores + c, j * SUB:(j + 1) * SUB]
                    else:
                        part = got[s][(half * packed + j) * SUB:(half * packed + j + 1) * SUB]
                    part = turn(part, slots * (s - k))
                    row = part if row is None else jnp.where(lane8 >= slots * s, part, row)
                rows.append(row)
        predicted = jnp.concatenate(rows, axis=0)
        mean = jnp.sum(predicted, axis=0, keepdims=True) * (1.0 / members)
        spread = predicted - mean
        variance = jnp.sum(spread * spread, axis=0, keepdims=True) * (1.0 / (members - 1.0))
        all_spread.append((mean, spread, variance))
    mats = []
    for l, (mean, spread, variance) in enumerate(all_spread):
        obs_var = meta_ref[step, l:l + 1]
        obs_value = meta_ref[step, nl + l:nl + l + 1]
        horiz = meta_ref[step, 2 * nl:2 * nl + 1]
        total_var = variance + obs_var
        gain = (obs_value - mean) / total_var
        shrink = 1.0 / (1.0 + jnp.sqrt(obs_var / total_var))
        scaled = horiz * (1.0 / (members - 1.0))
        own = spread[:nm]
        left = scaled * (shrink / total_var) * own
        if step + 1 < STEPS:
            spread_ref[l] = jnp.concatenate([spread, jnp.zeros((LANES - members, LANES), F32)], axis=0)
        else:
            spread_ref[l] = jnp.concatenate([spread[nm:], own, own, jnp.zeros((LANES - 3 * nm, LANES), F32)], axis=0)
            left = jnp.concatenate([left, jnp.broadcast_to(scaled * gain, (SUB, LANES))], axis=0)
        product = dot(left, spread_ref[l], by_lanes=True)
        if step + 1 < STEPS:
            mats.append(pack_mixing(product, jnp.sum(scaled * gain * own, axis=1, keepdims=True)))
        else:
            mats.append(pack_rows(product))
    up = sum(math.exp(-(nl - 1 - l) / scale) * mats[l] for l in range(nl))
    down = sum(math.exp(-l / scale) * mats[l] for l in range(nl))
    for l in range(nl):
        local_ref[l] = sum(math.exp(-abs(l - k) / scale) * mats[k] for k in range(nl))
    for d in range(level_count):
        msg_ref[d] = jnp.where(d > level, up, down)


def combine(nl, levels, level_count, got_ref, local_ref):
    level = lax.axis_index("level")
    scale = levels / 4.0
    fade = math.exp(-nl / scale)
    zero = jnp.zeros(got_ref.shape[1:], F32)
    below = lax.fori_loop(0, level, lambda d, acc: acc * fade + got_ref[d], zero)
    above = lax.fori_loop(0, level_count - 1 - level, lambda d, acc: acc * fade + got_ref[level_count - 1 - d], zero)
    return [
        math.exp(-(l + 1) / scale) * below + math.exp(-(nl - l) / scale) * above + local_ref[l] for l in range(nl)
    ]


def combine_kernel(nl, levels, level_count, got_ref, local_ref, later_ref, out_ref):
    out_ref[...] = jnp.concatenate(combine(nl, levels, level_count, got_ref, local_ref) + [later_ref[...]], axis=0)


def forecast_kernel(nl, nm, regions, slots, own_ref, other_ref, mix_ref, msg_ref, full_ref):
    lane8 = iota((SUB, LANES), 1)
    lane = iota((nm, LANES), 1)
    per = nm // SUB
    packed = -(-nl * per // regions)
    first = own_ref.shape[0] - packed * SUB
    rows = first // nl
    pieces_out = [jnp.zeros((SUB, LANES), F32) for _ in range(2 * packed)]
    rest = jnp.zeros((LANES - 2 * nm, LANES), F32)
    for l in range(nl):
        pieces = []
        for ref in (own_ref, other_ref):
            for r in range(per):
                j, k = (l * per + r) // regions, (l * per + r) % regions
                pieces.append(turn(ref[first + j * SUB:first + (j + 1) * SUB], -slots * k))
        prior = jnp.concatenate(pieces + [rest], axis=0)
        full_ref[l] = prior
        bands = [unpack_mixing(ref[l * rows:(l + 1) * rows], nm) for ref in (own_ref, other_ref)]
        lower = mixing_rows(bands[1], bands[0], nm)
        swapped = jnp.where(lane < nm, turn(lower, -nm), jnp.where(lane < 2 * nm, turn(lower, nm), 0.0))
        mix_ref[l] = jnp.concatenate([mixing_rows(bands[0], bands[1], nm), swapped, rest], axis=0)
        result = prior + dot(mix_ref[l], full_ref[l])
        for half in range(2):
            for r in range(per):
                j, k = (l * per + r) // regions, (l * per + r) % regions
                keep = (lane8 >= slots * k) & (lane8 < slots * (k + 1))
                at = half * per + r
                j += half * packed
                pieces_out[j] = jnp.where(keep, turn(result[at * SUB:(at + 1) * SUB], slots * k), pieces_out[j])
    msg_ref[...] = jnp.concatenate(pieces_out, axis=0)


def split(x):
    high = x.astype(BF16).astype(F32)
    return high, x - high


def update_kernel(nl, nm, levels, level_count, got_ref, local_ref, mix_ref, state_ref, theirs_ref, out_hbm,
                  out_v, left_ref, out_sem):
    nv = state_ref.shape[0]
    members = 2 * nm
    blocks = [(v, l) for l in range(nl) for v in range(nv)]
    lane = iota((nm, LANES), 1)
    for l, packed in enumerate(combine(nl, levels, level_count, got_ref, local_ref)):
        second = unpack_rows(packed, nm)
        both = second + mix_ref[l, 0:nm] + dot(second, mix_ref[l])
        high, low = split(both)
        again = turn(high, members)
        left_ref[l, :, 0:LANES] = high + jnp.where(lane >= members, again, 0.0)
        left_ref[l, :, LANES:] = jnp.where(lane < 2 * members - LANES, again, 0.0) + turn(low, 2 * members - LANES)
    pad = jnp.zeros((2 * LANES - 3 * members, state_ref.shape[3]), F32)
    stores = []
    for i, (v, l) in enumerate(blocks):
        own = state_ref[v, l]
        high, low = split(jnp.concatenate([own, theirs_ref[v, l]], axis=0))
        right = jnp.concatenate([high, low, high, pad], axis=0).astype(BF16)
        out_v[v, l] = own + jnp.dot(left_ref[l].astype(BF16), right, preferred_element_type=F32)
        copy = pltpu.make_async_copy(out_v.at[v, l], out_hbm.at[v, l], out_sem.at[i])
        copy.start()
        stores.append(copy)
    for copy in stores:
        copy.wait()


def body(state, ray_cols, ray_len, ray_weight, owner, loc_regions, loc_weight, obs_value, obs_var):
    regions = lax.axis_size("region")
    level_count = lax.axis_size("level")
    cores = lax.axis_size("member")
    nv, nl, nm, nc = state.shape
    occ, rays = ray_cols.shape[1:]
    slots = occ // regions
    levels = nl * level_count
    assert occ == LANES and regions * slots == LANES and nm % SUB == 0 and cores == 2
    assert LANES % rays == 0 and 2 * STEPS * slots == LANES
    groups = nl * nm // SUB
    block = (-(-groups // regions) * SUB, LANES)
    whole = pl.BlockSpec(memory_space=VMEM)
    outside = pl.BlockSpec(memory_space=pltpu.HBM)
    swap = [(0, 1), (1, 0)]
    dma = pltpu.SemaphoreType.DMA

    def call(kernel, statics, outs, scratch, *args, specs=None, out_specs=None, name=None, limit=32,
             kind=jax.ShapeDtypeStruct):
        def wrapped(*refs):
            return kernel(*statics, *refs)
        return pl.pallas_call(
            wrapped,
            out_shape=[kind(s, F32) for s in outs],
            in_specs=specs or [whole] * len(args),
            out_specs=out_specs or [whole] * len(outs),
            scratch_shapes=scratch,
            compiler_params=pltpu.CompilerParams(vmem_limit_bytes=limit * 2**20),
            name=name,
        )(*args)

    given = [ray_cols.swapaxes(1, 2), ray_len, ray_weight.transpose(0, 2, 3, 1), owner, loc_regions.swapaxes(1, 2),
             loc_weight.swapaxes(1, 2), obs_value.swapaxes(1, 2), obs_var.swapaxes(1, 2)]
    msg, later, meta, held = call(
        predict_kernel, (nl, nm, nc, regions, slots, rays),
        [(regions * cores,) + block, block, (STEPS, SUB, LANES), state.shape],
        [VMEM(a.shape, a.dtype) for a in given]
        + [VMEM((-(-nv * rays // LANES) * LANES, STEPS * LANES), F32), VMEM((nv * rays, STEPS * LANES), F32),
           VMEM((nv, 2 * STEPS * slots, nc), BF16), VMEM((SUB, LANES), F32), dma((nv,)), dma((len(given),))],
        state, *given, specs=[outside] * (1 + len(given)), name="predict", limit=56, kind=VMEM,
    )

    def assimilate(step, got, rows):
        out, local = call(
            local_kernel, (step, nl, nm, regions, slots, levels, level_count, cores),
            [(level_count, rows, LANES), (nl, rows, LANES)], [VMEM((nl, LANES, LANES), F32)],
            *got, meta, name="local",
        )
        return lax.all_to_all(out, "level", 0, 0, tiled=True), local

    band = -(-(nm // SUB) // (LANES // (nm + 2))) * SUB
    got = assimilate(0, [lax.all_to_all(msg, ("region", "member"), 0, 0, tiled=True)], band)
    own, = call(
        combine_kernel, (nl, levels, level_count), [(nl * band + block[0], LANES)], [], *got, later, name="combine",
    )
    mix, msg = call(
        forecast_kernel, (nl, nm, regions, slots),
        [(nl, LANES, LANES), (2 * block[0], LANES)], [VMEM((nl, LANES, LANES), F32)],
        own, lax.ppermute(own, "member", swap), name="forecast",
    )
    rings = [[(i, (i + s) % regions) for i in range(regions)] for s in range(1, regions)]
    got = assimilate(1, [msg] + [lax.ppermute(msg, "region", ring) for ring in rings], -(-(nm // SUB) // 2) * SUB)
    other_state = lax.ppermute(held, "member", swap)
    out, = call(
        update_kernel, (nl, nm, levels, level_count), [state.shape],
        [VMEM(state.shape, F32), VMEM((nl, nm, 2 * LANES), F32), dma((nv * nl,))],
        *got, mix, held, other_state, out_specs=[outside], name="update",
    )
    return out


def solution(mesh):
    in_specs = (P(None, "level", "member", "region"), P(), P(), P(), P(), P(), P(), P(), P())
    out_specs = P(None, "level", "member", "region")
    return jax.shard_map(body, mesh=mesh, in_specs=in_specs, out_specs=out_specs, check_vma=False)
```

```python
import math

import jax
import jax.numpy as jnp
from jax import lax
from jax.experimental import pallas as pl
from jax.experimental.pallas import tpu as pltpu
from jax.sharding import PartitionSpec as P

STEPS = 2
LANES = 128
SUB = 8
HIGHEST = lax.Precision.HIGHEST
F32 = jnp.float32
BF16 = jnp.bfloat16
VMEM = pltpu.VMEM
BY_LANES = (((1,), (1,)), ((), ()))


def iota(shape, dim):
    return lax.broadcasted_iota(jnp.int32, shape, dim)


def parts(x):
    high = x.astype(BF16)
    return high, (x - high.astype(F32)).astype(BF16)


def dot(a, b, by_lanes=False):
    (a_high, a_low), (b_high, b_low) = parts(a), parts(b)
    dims = BY_LANES if by_lanes else (((1,), (0,)), ((), ()))
    left = jnp.concatenate([a_high, a_low], axis=1)
    right = jnp.concatenate([b_high, b_high], axis=1 if by_lanes else 0)
    total = lax.dot_general(left, right, dims, preferred_element_type=F32)
    return total + lax.dot_general(a_high, b_low, dims, preferred_element_type=F32)


def turn(x, by):
    by = by % LANES
    return pltpu.roll(x, by, 1) if by else x


def pick(chosen, values):
    chosen = chosen.astype(BF16)
    total = None
    for _ in range(3):
        part = values.astype(BF16)
        term = lax.dot_general(chosen, part, BY_LANES, preferred_element_type=F32)
        total = term if total is None else total + term
        values = values - part.astype(F32)
    return total


def predict_kernel(nl, nm, nc, regions, slots, rays,
                   state_hbm, cols_hbm, len_hbm, weight_hbm, owner_hbm, locr_hbm, locw_hbm, obs_hbm, var_hbm,
                   msg_ref, later_ref, meta_ref, held,
                   cols_ref, len_ref, weight_ref, owner_ref, locr_ref, locw_ref, obs_ref, var_ref,
                   masked, sorted_ref, spread_out, meta_in, state_sem, arg_sem):
    nv = state_hbm.shape[0]
    region = lax.axis_index("region")
    level = lax.axis_index("level")
    pairs = [(cols_hbm, cols_ref), (len_hbm, len_ref), (weight_hbm, weight_ref), (owner_hbm, owner_ref),
             (locr_hbm, locr_ref), (locw_hbm, locw_ref), (obs_hbm, obs_ref), (var_hbm, var_ref)]
    fetches = [pltpu.make_async_copy(a, b, arg_sem.at[i]) for i, (a, b) in enumerate(pairs)]
    for copy in fetches:
        copy.start()
    copies = [pltpu.make_async_copy(state_hbm.at[v], held.at[v], state_sem.at[v]) for v in range(nv)]
    for copy in copies:
        copy.start()
    lane = iota((LANES, LANES), 1)
    sub = iota((LANES, LANES), 0)
    sub8 = iota((SUB, LANES), 0)
    earlier = (sub < lane).astype(BF16)
    region_f = region.astype(F32)
    masked[nv * rays:] = jnp.zeros((masked.shape[0] - nv * rays, STEPS * LANES), F32)
    meta_in[...] = jnp.zeros_like(meta_in)
    for copy in fetches:
        copy.wait()
    firsts, places, worst = [], [], None
    for step in range(STEPS):
        cols = cols_ref[step].astype(F32)
        first = jnp.min(cols, axis=0, keepdims=True)
        off = jnp.max(jnp.abs(cols - first - sub[:rays].astype(F32)))
        worst = off if worst is None else jnp.maximum(worst, off)
        home = jnp.zeros_like(first)
        for q in range(1, regions):
            home = home + (first >= float(q * nc)).astype(F32)
        at_home = (sub8.astype(F32) == home).astype(F32)
        count = jnp.dot(at_home.astype(BF16), earlier, preferred_element_type=F32)
        rank = jnp.sum(at_home * count, axis=0, keepdims=True)
        ahead = region_f - home
        ahead = jnp.where(ahead < 0.0, ahead + float(regions), ahead)
        places.append(ahead * float(slots) + rank)
        firsts.append(first)
        live = sub[:rays] < len_ref[step:step + 1]
        for v in range(nv):
            masked[v * rays:(v + 1) * rays, step * LANES:(step + 1) * LANES] = jnp.where(live, weight_ref[step, v], 0.0)
    slot = sub[:STEPS * slots].astype(F32)
    mine = []
    for step in range(STEPS):
        ours = (slot >= float(step * slots)) & (slot < float((step + 1) * slots))
        mine.append(((places[step] == slot - float(step * slots)) & ours).astype(F32))
    mine = jnp.concatenate(mine, axis=1)

    @pl.when(worst > 0.5)
    def _():
        column = jnp.concatenate([cols_ref[s].astype(F32) - firsts[s] for s in range(STEPS)], axis=1)

        def one(d, carry):
            hit = column == d.astype(F32)
            for v in range(nv):
                weights = masked[v * rays:(v + 1) * rays]
                sorted_ref[pl.ds(v * rays + d, 1)] = jnp.sum(jnp.where(hit, weights, 0.0), axis=0, keepdims=True)
            return carry
        lax.fori_loop(0, rays, one, 0)
        masked[0:nv * rays] = sorted_ref[...]

    first = jnp.broadcast_to(jnp.concatenate(firsts, axis=1), (LANES, STEPS * LANES))
    low = pick(mine, first).astype(jnp.int32) - region * nc
    tile, shift = low >> 7, low & (LANES - 1)
    picked = pick(mine, masked[...])
    lane_s = lane[:STEPS * slots]
    for v in range(nv):
        at = v * rays
        row = picked[:, at // LANES * LANES:(at // LANES + 1) * LANES]
        at = at % LANES
        row = turn(jnp.where((lane_s >= at) & (lane_s < at + rays), row, 0.0), -at)
        for bit in range(7):
            row = jnp.where((shift >> bit) % 2 == 1, turn(row, 1 << bit), row)
        near, far = jnp.where(lane_s >= shift, row, 0.0), jnp.where(lane_s < shift, row, 0.0)
        for t in range(nc // LANES):
            there = jnp.where(tile == t, near, jnp.where(tile == t - 1, far, 0.0))
            high = there.astype(BF16)
            spread_out[v, 0:STEPS * slots, t * LANES:(t + 1) * LANES] = high
            spread_out[v, STEPS * slots:, t * LANES:(t + 1) * LANES] = (there - high.astype(F32)).astype(BF16)
    for step in range(STEPS):
        horiz = (owner_ref[step:step + 1] == region).astype(F32)
        listed = (locr_ref[step] == region).astype(F32)
        horiz = horiz + jnp.sum(locw_ref[step] * listed, axis=0, keepdims=True)
        for l in range(nl):
            meta_in[l:l + 1] = var_ref[step, pl.ds(level * nl + l, 1)]
            meta_in[nl + l:nl + l + 1] = obs_ref[step, pl.ds(level * nl + l, 1)]
        meta_in[2 * nl:2 * nl + 1] = horiz
        order = (places[step] == sub.astype(F32)).astype(F32)
        meta_ref[step] = lax.dot_general(meta_in[...], order, BY_LANES, precision=HIGHEST, preferred_element_type=F32)
    total = None
    for v in range(nv):
        copies[v].wait()
        prior = jnp.concatenate([held[v, l] for l in range(nl)], axis=0)
        high = prior.astype(BF16)
        left = jnp.concatenate([high, (prior - high.astype(F32)).astype(BF16)], axis=0)
        term = lax.dot_general(left, spread_out[v], BY_LANES, preferred_element_type=F32)
        total = term if total is None else total + term
    result = total[:nl * nm] + total[nl * nm:]
    result = result + turn(result, -STEPS * slots)
    groups = nl * nm // SUB
    packed = -(-groups // regions)
    lane8 = lane[:SUB]
    for step in range(STEPS):
        parts = [jnp.zeros((SUB, LANES), F32) for _ in range(packed)]
        for g in range(groups):
            j, k = g // regions, g % regions
            here = (lane8 >= slots * k) & (lane8 < slots * (k + 1))
            parts[j] = jnp.where(here, turn(result[g * SUB:(g + 1) * SUB], slots * (k - step)), parts[j])
        for j in range(packed):
            if step == 0:
                for d in range(msg_ref.shape[0]):
                    msg_ref[d, j * SUB:(j + 1) * SUB] = parts[j]
            else:
                later_ref[j * SUB:(j + 1) * SUB] = parts[j]


def skew(x, by, sign):
    x = turn(x, by)
    sub8 = iota((SUB, LANES), 0)
    for bit in range(3):
        x = jnp.where((sub8 >> bit) % 2 == 1, turn(x, sign << bit), x)
    return x


def pack_mixing(s, w):
    nm = s.shape[0]
    width, across = nm + 2, LANES // (nm + 2)
    lane8 = iota((SUB, LANES), 1)
    pieces = []
    for g in range(nm // SUB):
        at = width * (g % across)
        part = skew(s[g * SUB:(g + 1) * SUB], at - g * SUB, -1)
        part = jnp.where((lane8 >= at) & (lane8 <= at + nm), part, 0.0)
        part = jnp.where(lane8 == at + nm + 1, w[g * SUB:(g + 1) * SUB], part)
        if g % across:
            pieces[-1] = pieces[-1] + part
        else:
            pieces.append(part)
    return jnp.concatenate(pieces, axis=0)


def unpack_mixing(p, nm):
    width, across = nm + 2, LANES // (nm + 2)
    lane8 = iota((SUB, LANES), 1)
    band, w = [], []
    for g in range(nm // SUB):
        at, j = width * (g % across), g // across
        part = p[j * SUB:(j + 1) * SUB]
        band.append(skew(jnp.where((lane8 >= at) & (lane8 <= at + nm), part, 0.0), g * SUB - at, 1))
        w.append(part[:, at + nm + 1:at + nm + 2])
    return jnp.concatenate(band, axis=0), jnp.concatenate(w, axis=0)


def mixing_rows(first, second, nm):
    (band, w), (band_2, w_2) = first, second
    lane = iota((nm, LANES), 1)
    sub = iota((nm, LANES), 0)
    top = jnp.where((lane > sub) & (lane < nm), band, 0.0)
    low = jnp.where(lane < sub, turn(band_2, -nm), 0.0)
    top = jnp.where(lane == nm, w, top)
    low = jnp.where(lane == nm, w_2, low)
    rest = jnp.zeros((LANES - 2 * nm, LANES), F32)
    turned = jnp.concatenate([top, low, rest], axis=0).T
    return turned[nm:nm + 1] - (band + turned[:nm])


def pack_rows(x):
    nm = x.shape[0] - SUB
    width = nm + nm // 2 + 1
    lane8 = iota((SUB, LANES), 1)
    sub8 = iota((SUB, LANES), 0)
    w = x[nm:nm + 1]
    pieces = []
    for g in range(nm // SUB):
        part = x[g * SUB:(g + 1) * SUB]
        part = jnp.where(lane8 < nm, part, jnp.where(lane8 < width, skew(part, -g * SUB, -1), 0.0))
        if g % 2:
            pieces[-1] = pieces[-1] + turn(part, width)
        else:
            pieces.append(part)
    others = (sub8 == 0) & (lane8 >= 64) & (lane8 < 64 + nm)
    owns = (sub8 == 1) & (lane8 >= 64) & (lane8 < 64 + nm)
    pieces[-1] = pieces[-1] + jnp.where(others, turn(w, 64), 0.0) + jnp.where(owns, turn(w, 64 - nm), 0.0)
    return jnp.concatenate(pieces, axis=0)


def unpack_rows(p, nm):
    width = nm + nm // 2 + 1
    lane8 = iota((SUB, LANES), 1)
    lane = iota((nm, LANES), 1)
    sub = iota((nm, LANES), 0)
    others, band = [], []
    for g in range(nm // SUB):
        part = turn(p[g // 2 * SUB:(g // 2 + 1) * SUB], -width * (g % 2))
        others.append(jnp.where(lane8 < nm, part, 0.0))
        band.append(skew(jnp.where((lane8 >= nm) & (lane8 < width), part, 0.0), g * SUB - nm, 1))
    others, band = jnp.concatenate(others, axis=0), jnp.concatenate(band, axis=0)
    band = jnp.where(lane < nm, band, 0.0) + turn(jnp.where(lane >= nm, band, 0.0), -nm)
    apart = lane - sub
    apart = jnp.where(apart < 0, apart + nm, apart)
    once = jnp.where((lane < nm) & (apart >= 1) & (apart < nm // 2), band, 0.0)
    turned = jnp.concatenate([once, jnp.zeros((LANES - nm, LANES), F32)], axis=0).T[:nm]
    last = p[-SUB:]
    w = jnp.where(lane8[:1] < nm, turn(last[1:2], -64), 0.0)
    w = w + turn(jnp.where(lane8[:1] < nm, turn(last[0:1], -64), 0.0), nm)
    return w - (jnp.where(lane < nm, band, 0.0) + turned + turn(others, nm))


def local_kernel(step, nl, nm, regions, slots, levels, level_count, cores, *refs):
    *got, meta_ref, msg_ref, local_ref, spread_ref = refs
    region = lax.axis_index("region")
    level = lax.axis_index("level")
    member = lax.axis_index("member")
    members = nm * cores
    scale = levels / 4.0
    lane8 = iota((SUB, LANES), 1)
    packed = -(-(nl * nm // SUB) // regions)
    all_spread = []
    for l in range(nl):
        rows = []
        for half, c in enumerate((member, 1 - member)):
            for r in range(nm // SUB):
                g = l * (nm // SUB) + r
                j, k = g // regions, g % regions
                row = None
                for s in range(regions):
                    if len(got) == 1:
                        source = jnp.where(region >= s, region - s, region - s + regions)
                        part = got[0][source * cores + c, j * SUB:(j + 1) * SUB]
                    else:
                        part = got[s][(half * packed + j) * SUB:(half * packed + j + 1) * SUB]
                    part = turn(part, slots * (s - k))
                    row = part if row is None else jnp.where(lane8 >= slots * s, part, row)
                rows.append(row)
        predicted = jnp.concatenate(rows, axis=0)
        mean = jnp.sum(predicted, axis=0, keepdims=True) * (1.0 / members)
        spread = predicted - mean
        variance = jnp.sum(spread * spread, axis=0, keepdims=True) * (1.0 / (members - 1.0))
        all_spread.append((mean, spread, variance))
    mats = []
    for l, (mean, spread, variance) in enumerate(all_spread):
        obs_var = meta_ref[step, l:l + 1]
        obs_value = meta_ref[step, nl + l:nl + l + 1]
        horiz = meta_ref[step, 2 * nl:2 * nl + 1]
        total_var = variance + obs_var
        gain = (obs_value - mean) / total_var
        shrink = 1.0 / (1.0 + jnp.sqrt(obs_var / total_var))
        scaled = horiz * (1.0 / (members - 1.0))
        own = spread[:nm]
        left = scaled * (shrink / total_var) * own
        if step + 1 < STEPS:
            spread_ref[l] = jnp.concatenate([spread, jnp.zeros((LANES - members, LANES), F32)], axis=0)
        else:
            spread_ref[l] = jnp.concatenate([spread[nm:], own, own, jnp.zeros((LANES - 3 * nm, LANES), F32)], axis=0)
            left = jnp.concatenate([left, jnp.broadcast_to(scaled * gain, (SUB, LANES))], axis=0)
        product = dot(left, spread_ref[l], by_lanes=True)
        if step + 1 < STEPS:
            mats.append(pack_mixing(product, jnp.sum(scaled * gain * own, axis=1, keepdims=True)))
        else:
            mats.append(pack_rows(product))
    up = sum(math.exp(-(nl - 1 - l) / scale) * mats[l] for l in range(nl))
    down = sum(math.exp(-l / scale) * mats[l] for l in range(nl))
    for l in range(nl):
        local_ref[l] = sum(math.exp(-abs(l - k) / scale) * mats[k] for k in range(nl))
    if step + 1 < STEPS:
        for d in range(level_count):
            msg_ref[d] = jnp.where(d > level, up, down)
    else:
        msg_ref[...] = jnp.concatenate([up, down], axis=0)


def combine(nl, levels, inner, got_ref, local_ref):
    level = lax.axis_index("level")
    outer, place = lax.div(level, inner), lax.rem(level, inner)
    scale = levels / 4.0
    count, near = got_ref.shape[0], nl * inner
    fade = math.exp(-near / scale)
    zero = jnp.zeros(got_ref.shape[1:], F32)
    below = lax.fori_loop(0, outer, lambda d, acc: acc * fade + got_ref[d], zero)
    above = lax.fori_loop(0, count - 1 - outer, lambda d, acc: acc * fade + got_ref[count - 1 - d], zero)
    at = jnp.zeros((1, LANES), F32) + place.astype(F32) * float(nl)
    return [
        jnp.exp(-(at + float(l + 1)) / scale) * below + jnp.exp((at + float(l - near)) / scale) * above + local_ref[l]
        for l in range(nl)
    ]


def group_kernel(nl, levels, inner, *refs):
    *got, local_ref, msg_ref, part_ref = refs
    level = lax.axis_index("level")
    outer, place = lax.div(level, inner), lax.rem(level, inner)
    scale = levels / 4.0
    rows = local_ref.shape[1]
    up = down = None
    near = [local_ref[l] for l in range(nl)]
    for s, ref in enumerate(got):
        rise, fall = ref[0:rows], ref[rows:2 * rows]
        source = jnp.where(place >= s, place - s, place - s + inner)
        at = jnp.zeros((1, LANES), F32) + source.astype(F32) * float(nl)
        higher = jnp.exp((at - float(nl * (inner - 1))) / scale) * rise
        lower = jnp.exp(-at / scale) * fall
        up, down = (higher, lower) if up is None else (up + higher, down + lower)
        if s:
            for l in range(nl):
                from_below = math.exp(-(l + 1 + (s - 1) * nl) / scale) * rise
                from_above = math.exp(-((inner - s) * nl - l) / scale) * fall
                near[l] = near[l] + jnp.where(place >= s, from_below, from_above)
    for l in range(nl):
        part_ref[l] = near[l]
    for d in range(msg_ref.shape[0]):
        msg_ref[d] = jnp.where(d > outer, up, down)


def combine_kernel(nl, levels, got_ref, local_ref, later_ref, out_ref):
    out_ref[...] = jnp.concatenate(combine(nl, levels, 1, got_ref, local_ref) + [later_ref[...]], axis=0)


def forecast_kernel(nl, nm, regions, slots, own_ref, other_ref, mix_ref, msg_ref, full_ref):
    lane8 = iota((SUB, LANES), 1)
    lane = iota((nm, LANES), 1)
    per = nm // SUB
    packed = -(-nl * per // regions)
    first = own_ref.shape[0] - packed * SUB
    rows = first // nl
    pieces_out = [jnp.zeros((SUB, LANES), F32) for _ in range(2 * packed)]
    rest = jnp.zeros((LANES - 2 * nm, LANES), F32)
    for l in range(nl):
        pieces = []
        for ref in (own_ref, other_ref):
            for r in range(per):
                j, k = (l * per + r) // regions, (l * per + r) % regions
                pieces.append(turn(ref[first + j * SUB:first + (j + 1) * SUB], -slots * k))
        prior = jnp.concatenate(pieces + [rest], axis=0)
        full_ref[l] = prior
        bands = [unpack_mixing(ref[l * rows:(l + 1) * rows], nm) for ref in (own_ref, other_ref)]
        lower = mixing_rows(bands[1], bands[0], nm)
        swapped = jnp.where(lane < nm, turn(lower, -nm), jnp.where(lane < 2 * nm, turn(lower, nm), 0.0))
        mix_ref[l] = jnp.concatenate([mixing_rows(bands[0], bands[1], nm), swapped, rest], axis=0)
        result = prior + dot(mix_ref[l], full_ref[l])
        for half in range(2):
            for r in range(per):
                j, k = (l * per + r) // regions, (l * per + r) % regions
                keep = (lane8 >= slots * k) & (lane8 < slots * (k + 1))
                at = half * per + r
                j += half * packed
                pieces_out[j] = jnp.where(keep, turn(result[at * SUB:(at + 1) * SUB], slots * k), pieces_out[j])
    msg_ref[...] = jnp.concatenate(pieces_out, axis=0)


def split(x):
    high = x.astype(BF16).astype(F32)
    return high, x - high


def update_kernel(nl, nm, levels, inner, got_ref, local_ref, mix_ref, state_ref, theirs_ref, out_hbm,
                  out_v, left_ref, out_sem):
    nv = state_ref.shape[0]
    members = 2 * nm
    blocks = [(v, l) for l in range(nl) for v in range(nv)]
    lane = iota((nm, LANES), 1)
    for l, packed in enumerate(combine(nl, levels, inner, got_ref, local_ref)):
        second = unpack_rows(packed, nm)
        both = second + mix_ref[l, 0:nm] + dot(second, mix_ref[l])
        high, low = split(both)
        again = turn(high, members)
        left_ref[l, :, 0:LANES] = high + jnp.where(lane >= members, again, 0.0)
        left_ref[l, :, LANES:] = jnp.where(lane < 2 * members - LANES, again, 0.0) + turn(low, 2 * members - LANES)
    pad = jnp.zeros((2 * LANES - 3 * members, state_ref.shape[3]), F32)
    stores = []
    for i, (v, l) in enumerate(blocks):
        own = state_ref[v, l]
        high, low = split(jnp.concatenate([own, theirs_ref[v, l]], axis=0))
        right = jnp.concatenate([high, low, high, pad], axis=0).astype(BF16)
        out_v[v, l] = own + jnp.dot(left_ref[l].astype(BF16), right, preferred_element_type=F32)
        copy = pltpu.make_async_copy(out_v.at[v, l], out_hbm.at[v, l], out_sem.at[i])
        copy.start()
        stores.append(copy)
    for copy in stores:
        copy.wait()


INNER = 4


def body(state, ray_cols, ray_len, ray_weight, owner, loc_regions, loc_weight, obs_value, obs_var):
    regions = lax.axis_size("region")
    level_count = lax.axis_size("level")
    cores = lax.axis_size("member")
    nv, nl, nm, nc = state.shape
    occ, rays = ray_cols.shape[1:]
    slots = occ // regions
    levels = nl * level_count
    assert occ == LANES and regions * slots == LANES and nm % SUB == 0 and cores == 2
    assert LANES % rays == 0 and 2 * STEPS * slots == LANES
    groups = nl * nm // SUB
    block = (-(-groups // regions) * SUB, LANES)
    whole = pl.BlockSpec(memory_space=VMEM)
    outside = pl.BlockSpec(memory_space=pltpu.HBM)
    swap = [(0, 1), (1, 0)]
    dma = pltpu.SemaphoreType.DMA

    def call(kernel, statics, outs, scratch, *args, specs=None, out_specs=None, name=None, limit=32,
             kind=jax.ShapeDtypeStruct):
        def wrapped(*refs):
            return kernel(*statics, *refs)
        return pl.pallas_call(
            wrapped,
            out_shape=[kind(s, F32) for s in outs],
            in_specs=specs or [whole] * len(args),
            out_specs=out_specs or [whole] * len(outs),
            scratch_shapes=scratch,
            compiler_params=pltpu.CompilerParams(vmem_limit_bytes=limit * 2**20),
            name=name,
        )(*args)

    other_state = lax.ppermute(state, "member", swap)
    given = [ray_cols.swapaxes(1, 2), ray_len, ray_weight.transpose(0, 2, 3, 1), owner, loc_regions.swapaxes(1, 2),
             loc_weight.swapaxes(1, 2), obs_value.swapaxes(1, 2), obs_var.swapaxes(1, 2)]
    msg, later, meta, held = call(
        predict_kernel, (nl, nm, nc, regions, slots, rays),
        [(regions * cores,) + block, block, (STEPS, SUB, LANES), state.shape],
        [VMEM(a.shape, a.dtype) for a in given]
        + [VMEM((-(-nv * rays // LANES) * LANES, STEPS * LANES), F32), VMEM((nv * rays, STEPS * LANES), F32),
           VMEM((nv, 2 * STEPS * slots, nc), BF16), VMEM((SUB, LANES), F32), dma((nv,)), dma((len(given),))],
        state, *given, specs=[outside] * (1 + len(given)), name="predict", limit=56, kind=VMEM,
    )

    def assimilate(step, got, shape):
        return call(
            local_kernel, (step, nl, nm, regions, slots, levels, level_count, cores),
            [shape, (nl,) + shape[-2:] if step == 0 else (nl, shape[0] // 2, LANES)],
            [VMEM((nl, LANES, LANES), F32)], *got, meta, name="local",
        )

    band = -(-(nm // SUB) // (LANES // (nm + 2))) * SUB
    got = lax.all_to_all(msg, ("region", "member"), 0, 0, tiled=True)
    out, local = assimilate(0, [got], (level_count, band, LANES))
    got = [lax.all_to_all(out, "level", 0, 0, tiled=True), local]
    own, = call(
        combine_kernel, (nl, levels), [(nl * band + block[0], LANES)], [], *got, later, name="combine",
    )
    mix, msg = call(
        forecast_kernel, (nl, nm, regions, slots),
        [(nl, LANES, LANES), (2 * block[0], LANES)], [VMEM((nl, LANES, LANES), F32)],
        own, lax.ppermute(own, "member", swap), name="forecast",
    )
    rings = [[(i, (i + s) % regions) for i in range(regions)] for s in range(1, regions)]
    rows = -(-(nm // SUB) // 2) * SUB
    out, local = assimilate(1, [msg] + [lax.ppermute(msg, "region", ring) for ring in rings], (2 * rows, LANES))
    outer = level_count // INNER
    rings = [
        [(z * INNER + y, z * INNER + (y + s) % INNER) for z in range(outer) for y in range(INNER)] for s in range(1, INNER)
    ]
    columns = [[z * INNER + y for z in range(outer)] for y in range(INNER)]
    out, local = call(
        group_kernel, (nl, levels, INNER), [(outer, rows, LANES), (nl, rows, LANES)], [],
        out, *[lax.ppermute(out, "level", ring) for ring in rings], local, name="group",
    )
    got = lax.all_to_all(out, "level", 0, 0, tiled=True, axis_index_groups=columns)
    out, = call(
        update_kernel, (nl, nm, levels, INNER), [state.shape],
        [VMEM(state.shape, F32), VMEM((nl, nm, 2 * LANES), F32), dma((nv * nl,))],
        got, local, mix, held, other_state, out_specs=[outside], name="update",
    )
    return out


def solution(mesh):
    in_specs = (P(None, "level", "member", "region"), P(), P(), P(), P(), P(), P(), P(), P())
    out_specs = P(None, "level", "member", "region")
    return jax.shard_map(body, mesh=mesh, in_specs=in_specs, out_specs=out_specs, check_vma=False)
```
